32 devices in a mesh: seq: 8 (over z, y), head: 4 (over x, core).
Axes of the slice: x: 2, y: 2, z: 4, core: 2. Of those that a mesh axis runs over, the one named last changes fastest.
Arguments:
- hidden_in: bfloat16 [64, 8192], P(None, 'seq'), may hold values from -6 to 6
- w_query: bfloat16 [8192, 8192], P('seq', 'head'), may hold values from -0.0625 to 0.0625
- w_keyval: bfloat16 [8192, 2048], P('seq', 'head'), may hold values from -0.0625 to 0.0625
- w_out: bfloat16 [8192, 8192], P('head', 'seq'), may hold values from -0.0625 to 0.0625
- key_cache: bfloat16 [1024, 128, 1024], P('seq', None, 'head'), may hold values from -6 to 6
- value_cache: bfloat16 [1024, 128, 1024], P('seq', None, 'head'), may hold values from -6 to 6
- key_scale: float32 [1024, 8], P('seq', 'head'), may hold values from 0.25 to 300
- value_scale: float32 [1024, 8], P('seq', 'head'), may hold values from 0.5 to 2
- page_counts: int32 [64], replicated, may hold values from 1 to 128, 1024 in all
- slot_pages: int32 [1024], P('seq'), may hold values from 0 to 1023, each once
- trim: int32 [64], replicated, may hold values from 0 to 127
Outputs:
- attn_out: bfloat16 [64, 8192], P(None, 'seq')
The draws below stay inside these ranges and needn't reach their ends.
Inputs may be any that keep to these rules, and one draw needn't show every extreme that they name: `page_counts`: every request has at least one page; the page counts sum to 1024.
All inputs are finite; a program needn't handle non-finite values.
Results may differ from the reference program's by a relative error of at most 0.0095.
Values may be sent and summed in bfloat16 or wider, within the bound.
No kernel may reach another device: no remote copies, remote signals or barrier semaphores. Data moves between devices by JAX's collectives and lax.ppermute only.
A program may use at most 128 MiB of HBM per device.

```python
import math
import jax
import jax.numpy as jnp
import numpy as np
from jax import lax

D = 8192
QH = 64
KEY_VALUE_HEADS = 8
HD = 128
PAGE = 128
PAGES_DEV = 128
REQ = 64
TOTAL_PAGE_SLOTS = 1024
MOSTP = 128


def draw_key_scale(key, part):
    key = jax.random.fold_in(key, 7)
    start_offset = jnp.exp(jax.random.uniform(key, (TOTAL_PAGE_SLOTS, KEY_VALUE_HEADS), jnp.float32, math.log(0.25), math.log(2.0)))
    return start_offset


def touch_ends(array, stream_key, low, top_value):
    dims = array.shape
    spot = [jax.random.randint(jax.random.fold_in(stream_key, axis), (), 0, dims[axis]) for axis in range(len(dims))]
    array = array.at[tuple(spot)].set(low)
    longest = dims.index(max(dims))
    spot[longest] = (spot[longest] + 1) % dims[longest]
    return array.at[tuple(spot)].set(top_value)


def level_of(rng, extent, pieces, least, largest):
    factor_of, own = 1.0, jax.random.fold_in(rng, 6)
    for position, blocks in pieces:
        steps = jnp.exp(jax.random.uniform(jax.random.fold_in(own, position), (blocks,), jnp.float32, least / len(pieces), largest / len(pieces)))
        factor_of = factor_of * jnp.repeat(steps, extent[position] // blocks).reshape([-1 if axis == position else 1 for axis in range(len(extent))])
    return factor_of


def split_up(amount, total, bound, lean):
    loads = [(1 << 20) // math.isqrt(standing ** lean) + 1 for standing in range(2, amount + 1)]
    rest, given = total - bound - (amount - 1), [1] * (amount - 1)
    while rest > 0:
        candidates = [i for i in range(amount - 1) if given[i] < bound]
        mass, budget = sum([loads[i] for i in candidates]), rest
        for i in candidates:
            more = min(bound - given[i], max(1, budget * loads[i] // mass), rest)
            given[i] = given[i] + more
            rest = rest - more
    return np.array([bound] + given)


def ragged(own_key, count, total, limit, skew):
    if count == 2:
        one = jax.random.randint(own_key, (), max(1, total - limit), min(limit, total - 1) + 1)
        return jnp.stack([one, total - one])
    sizes = jnp.asarray(split_up(count, total, limit, skew), jnp.int32)
    couples = (count - 1) // 2
    source_of, taker = sizes[1:1 + 2 * couples:2], sizes[2:2 + 2 * couples:2]
    margin = jnp.minimum(source_of - 1, limit - taker)
    passed = jax.random.randint(jax.random.fold_in(own_key, 1), (couples,), 0, 1 << 20) % (margin + 1)
    sizes = sizes.at[1:1 + 2 * couples:2].set(source_of - passed).at[2:2 + 2 * couples:2].set(taker + passed)
    return sizes[jax.random.permutation(jax.random.fold_in(own_key, 2), count)]


def noise(key, dims, scale, limit, cuts=(), held_as=jnp.bfloat16):
    loudness = level_of(key, dims, cuts, -0.22, 0.18) if cuts else 1.0
    result = jax.random.normal(key, dims, jnp.float32) * scale * loudness
    return jnp.minimum(jnp.maximum(result, -limit), limit).astype(held_as)


def setup_inputs(seed: int = 0) -> dict:
    seeds = jax.random.split(jax.random.key(seed), 12)
    hidden_in = noise(seeds[0], (REQ, D), 1.0, 6.0, ((1, 8),))
    w_query = noise(seeds[1], (D, QH * HD), D ** -0.5, 0.0625, ((0, 8), (1, 4)))
    w_keyval = noise(seeds[2], (D, 2 * KEY_VALUE_HEADS * HD), D ** -0.5, 0.0625, ((0, 8), (1, 4)))
    w_out = noise(seeds[3], (QH * HD, D), (QH * HD) ** -0.5, 0.0625, ((0, 4), (1, 8)))
    key_cache = noise(seeds[4], (TOTAL_PAGE_SLOTS, PAGE, KEY_VALUE_HEADS * HD), 1.0, 6.0, ((0, 8), (2, 4)))
    value_cache = noise(seeds[5], (TOTAL_PAGE_SLOTS, PAGE, KEY_VALUE_HEADS * HD), 1.0, 6.0, ((0, 8), (2, 4)))
    key_scale = draw_key_scale(jax.random.fold_in(seeds[11], 71), 0)
    value_scale = jnp.clip(jnp.exp(math.log(2.0) - 1.3862944 * jax.random.uniform(seeds[7], (TOTAL_PAGE_SLOTS, KEY_VALUE_HEADS), jnp.float32) ** level_of(seeds[7], (TOTAL_PAGE_SLOTS, KEY_VALUE_HEADS), ((0, 8), (1, 4)), -0.2, 0.2)), 0.5, 2.0)
    page_counts = ragged(seeds[8], REQ, TOTAL_PAGE_SLOTS, MOSTP, 2).astype(jnp.int32)
    slot_pages = jax.random.permutation(seeds[9], TOTAL_PAGE_SLOTS).astype(jnp.int32)
    trim = touch_ends(jax.random.randint(seeds[10], (REQ,), 0, PAGE), jax.random.fold_in(seeds[10], 1), 0, PAGE - 1).astype(jnp.int32)
    return {"hidden_in": hidden_in, "w_query": w_query, "w_keyval": w_keyval, "w_out": w_out, "key_cache": key_cache, "value_cache": value_cache, "key_scale": key_scale, "value_scale": value_scale, "page_counts": page_counts, "slot_pages": slot_pages, "trim": trim}


masked_low = -1e+30

def page_table(page_counts, slot_pages, trim):
    start = jnp.cumsum(page_counts) - page_counts
    ends = start + page_counts
    owner = lax.optimization_barrier(jnp.sum((ends[None, :] <= slot_pages[:, None]).astype(jnp.int32), axis=1)).astype(jnp.int32)
    index = (slot_pages - start[owner]).astype(jnp.int32)
    length = (PAGE * page_counts - trim).astype(jnp.int32)
    return (owner, index, length[owner])

def reference(hidden_in, w_query, w_keyval, w_out, key_cache, value_cache, key_scale, value_scale, page_counts, slot_pages, trim):
    group = QH // KEY_VALUE_HEADS
    query = jnp.dot(hidden_in, w_query, preferred_element_type=jnp.float32).astype(jnp.bfloat16)
    keyval = jnp.dot(hidden_in, w_keyval, preferred_element_type=jnp.float32).astype(jnp.bfloat16)
    owner, index, page_len = page_table(page_counts, slot_pages, trim)
    inverse_square_root = 1.0 / math.sqrt(HD)
    query_heads = query.reshape(REQ, KEY_VALUE_HEADS, group, HD)

    def block(input_arrays):
        key_rows, value_rows, key_page_scale, value_page_scale, owner_identifiers, slot_index, page_length = input_arrays
        q_sel = query_heads[owner_identifiers].astype(jnp.float32)
        unscaled_pages = jnp.einsum('sgjd,stgd->sgjt', q_sel, key_rows.reshape(-1, PAGE, KEY_VALUE_HEADS, HD).astype(jnp.float32))
        score_matrix = unscaled_pages * (key_page_scale * inverse_square_root)[:, :, None, None]
        pos = slot_index[:, None] * PAGE + jnp.arange(PAGE, dtype=jnp.int32)[None, :]
        valid = (pos < page_length[:, None])[:, None, None, :]
        score_matrix = jnp.where(valid, score_matrix, masked_low)
        pmax = lax.optimization_barrier(jnp.max(score_matrix, axis=-1))
        probs = jnp.where(valid, jnp.exp(score_matrix - pmax[..., None]), 0.0).astype(jnp.bfloat16)
        psum = lax.optimization_barrier(jnp.sum(probs.astype(jnp.float32), axis=-1))
        pout = jnp.einsum('sgjt,stgd->sgjd', probs.astype(jnp.float32), value_rows.reshape(-1, PAGE, KEY_VALUE_HEADS, HD).astype(jnp.float32))
        pout = pout * value_page_scale[:, :, None, None]
        count = key_rows.shape[0]
        return (pmax.reshape(count, QH), psum.reshape(count, QH), pout.reshape(count, QH * HD))
    nblk = TOTAL_PAGE_SLOTS // PAGES_DEV

    def split(a):
        return a.reshape((nblk, PAGES_DEV) + a.shape[1:])
    pmax, psum, pout = lax.map(block, (split(key_cache), split(value_cache), split(key_scale), split(value_scale), split(owner), split(index), split(page_len)))
    pmax = pmax.reshape(TOTAL_PAGE_SLOTS, QH)
    psum = psum.reshape(TOTAL_PAGE_SLOTS, QH)
    pout = pout.reshape(TOTAL_PAGE_SLOTS, QH * HD)
    onehot = owner[None, :] == jnp.arange(REQ, dtype=jnp.int32)[:, None]
    cache_max = lax.optimization_barrier(jnp.max(jnp.where(onehot[:, :, None], pmax[None, :, :], masked_low), axis=1))
    weight = jnp.exp(pmax - cache_max[owner])
    cache_sum = jax.ops.segment_sum(psum * weight, owner, num_segments=REQ)
    cache_out = jax.ops.segment_sum((pout.reshape(TOTAL_PAGE_SLOTS, QH, HD) * weight[:, :, None]).reshape(TOTAL_PAGE_SLOTS, QH * HD), owner, num_segments=REQ)
    kv = keyval.reshape(REQ, KEY_VALUE_HEADS, 2, HD).astype(jnp.float32)
    new_key = kv[:, :, 0]
    new_value = kv[:, :, 1]
    own = jnp.einsum('rgjd,rgd->rgj', query_heads.astype(jnp.float32), new_key).reshape(REQ, QH) * inverse_square_root
    top = jnp.maximum(cache_max, own)
    old_part = jnp.exp(cache_max - top)
    new_part = jnp.exp(own - top)
    denom = cache_sum * old_part + new_part
    spread_value = jnp.broadcast_to(new_value[:, :, None, :], (REQ, KEY_VALUE_HEADS, group, HD)).reshape(REQ, QH, HD)
    numer = cache_out.reshape(REQ, QH, HD) * old_part[:, :, None] + new_part[:, :, None] * spread_value
    context = (numer / denom[:, :, None]).reshape(REQ, QH * HD).astype(jnp.bfloat16)
    return jnp.dot(context, w_out, preferred_element_type=jnp.float32).astype(jnp.bfloat16)
```

```python
import math

import jax
import jax.numpy as jnp
from jax import lax
from jax.sharding import PartitionSpec as P

HD = 128
PAGE = 128


masked_low = -1e30


def widen(factor, size):
    return jnp.repeat(factor, size, axis=1)


def split_three(x):
    hi = lax.reduce_precision(x, 8, 7)
    rest = x - hi
    mid = lax.reduce_precision(rest, 8, 7)
    return hi, mid, rest - mid


def exchange(x, axis, n):
    return lax.all_to_all(x.reshape(n, x.shape[0] // n, x.shape[1]), axis, 0, 0)


def gather_direct(x, axis, n):
    me = lax.axis_index(axis)
    blocks = [x]
    for shift in range(1, n):
        blocks.append(lax.ppermute(x, axis, [(j, (j + shift) % n) for j in range(n)]))
    stacked = jnp.stack(blocks)
    order = jnp.mod(me - jnp.arange(n, dtype=jnp.int32), n)
    return jnp.take(stacked, order, axis=0).reshape(n * x.shape[0], x.shape[1])


def body(
    hidden_in,
    w_query,
    w_keyval,
    w_out,
    key_cache,
    value_cache,
    key_scale,
    value_scale,
    page_counts,
    slot_pages,
    trim,
    seq_size,
    head_size,
):
    requests = hidden_in.shape[0]
    slots = key_cache.shape[0]
    kv_local = w_keyval.shape[1] // (2 * HD)
    heads_local = w_query.shape[1] // HD
    group = heads_local // kv_local
    wide = heads_local * HD
    mine = requests // seq_size
    inverse_square_root = 1.0 / math.sqrt(HD)

    part_query = jnp.dot(hidden_in, w_query, preferred_element_type=jnp.float32)
    part_keyval = jnp.dot(hidden_in, w_keyval, preferred_element_type=jnp.float32)
    parts = exchange(jnp.concatenate([part_query, part_keyval], axis=1), "seq", seq_size)
    sums = jnp.sum(parts, axis=0).astype(jnp.bfloat16)
    my_query, my_keyval = sums[:, :wide], sums[:, wide:]
    query = gather_direct(my_query, "seq", seq_size)

    start = jnp.cumsum(page_counts) - page_counts
    ends = start + page_counts
    owner = jnp.sum((ends[None, :] <= slot_pages[:, None]).astype(jnp.int32), axis=1)
    selector = owner[:, None] == jnp.arange(requests, dtype=jnp.int32)[None, :]
    select_int = selector.astype(jnp.int32)
    index = slot_pages - jnp.sum(select_int * start[None, :], axis=1)
    lengths = PAGE * page_counts - trim
    page_len = jnp.sum(select_int * lengths[None, :], axis=1)

    q_sel = jnp.dot(
        selector.astype(jnp.bfloat16), query, preferred_element_type=jnp.float32
    ).astype(jnp.bfloat16)
    q_sel = q_sel.reshape(slots, kv_local, group, HD)
    key_rows = key_cache.reshape(slots, PAGE, kv_local, HD)
    value_rows = value_cache.reshape(slots, PAGE, kv_local, HD)
    unscaled_pages = jnp.einsum(
        "sgjd,stgd->sgjt", q_sel, key_rows, preferred_element_type=jnp.float32
    )
    score_matrix = unscaled_pages * (key_scale * inverse_square_root)[:, :, None, None]
    position = index[:, None] * PAGE + jnp.arange(PAGE, dtype=jnp.int32)[None, :]
    valid = (position < page_len[:, None])[:, None, None, :]
    score_matrix = jnp.where(valid, score_matrix, masked_low)
    page_max = jnp.max(score_matrix, axis=-1)
    probs = jnp.where(valid, jnp.exp(score_matrix - page_max[..., None]), 0.0).astype(jnp.bfloat16)
    page_sum = jnp.sum(probs.astype(jnp.float32), axis=-1).reshape(slots, heads_local)
    page_out = jnp.einsum("sgjt,stgd->sgjd", probs, value_rows, preferred_element_type=jnp.float32)
    page_out = (page_out * value_scale[:, :, None, None]).reshape(slots, heads_local, HD)
    page_max = page_max.reshape(slots, heads_local)
    select_float = selector.astype(jnp.float32)
    dev_max = jnp.max(jnp.where(selector[:, :, None], page_max[:, None, :], masked_low), axis=0)
    slot_max = jnp.max(jnp.where(selector[:, :, None], dev_max[None, :, :], masked_low), axis=1)
    weight = jnp.exp(page_max - slot_max)
    dev_sum = jnp.dot(select_float.T, page_sum * weight, precision=lax.Precision.HIGHEST)
    weighted = (page_out * weight[:, :, None]).reshape(slots, wide)
    dev_out = jnp.dot(select_float.T, weighted, precision=lax.Precision.HIGHEST)

    pieces = jnp.concatenate([*split_three(dev_max), *split_three(dev_sum)], axis=1)
    pieces = jnp.pad(pieces, ((0, 0), (0, -pieces.shape[1] % 128)))
    packed = jnp.concatenate([dev_out, pieces], axis=1).astype(jnp.bfloat16)
    got = exchange(packed, "seq", seq_size).astype(jnp.float32)
    out_parts = got[:, :, :wide]
    stat = got[:, :, wide : wide + 6 * heads_local].reshape(seq_size, mine, 6, heads_local)
    max_parts = stat[:, :, 0] + stat[:, :, 1] + stat[:, :, 2]
    sum_parts = stat[:, :, 3] + stat[:, :, 4] + stat[:, :, 5]

    pairs = my_keyval.reshape(mine, kv_local, 2, HD)
    new_key = pairs[:, :, 0]
    new_value = pairs[:, :, 1].astype(jnp.float32)
    own = (
        jnp.einsum(
            "rgjd,rgd->rgj",
            my_query.reshape(mine, kv_local, group, HD),
            new_key,
            preferred_element_type=jnp.float32,
        ).reshape(mine, heads_local)
        * inverse_square_root
    )
    top = jnp.maximum(jnp.max(max_parts, axis=0), own)
    factor = jnp.exp(max_parts - top[None])
    new_part = jnp.exp(own - top)
    denom = jnp.sum(sum_parts * factor, axis=0) + new_part
    numer = jnp.sum(
        out_parts.reshape(seq_size, mine, heads_local, HD) * factor[..., None], axis=0
    )
    spread_value = jnp.broadcast_to(
        new_value[:, :, None, :], (mine, kv_local, group, HD)
    ).reshape(mine, heads_local, HD)
    numer = numer + new_part[..., None] * spread_value
    my_context = (numer / denom[..., None]).astype(jnp.bfloat16).reshape(mine, wide)
    context = lax.all_gather(my_context, "seq", axis=0, tiled=True)

    total = jnp.dot(context, w_out, preferred_element_type=jnp.float32)
    step = 1
    while step < head_size:
        total = total + lax.ppermute(
            total, "head", [(j, j ^ step) for j in range(head_size)]
        )
        step *= 2
    return total.astype(jnp.bfloat16)


def solution(mesh):
    seq_size, head_size = mesh.shape["seq"], mesh.shape["head"]

    def local(*args):
        return body(*args, seq_size=seq_size, head_size=head_size)

    return jax.shard_map(
        local,
        mesh=mesh,
        in_specs=(
            P(None, "seq"),
            P("seq", "head"),
            P("seq", "head"),
            P("head", "seq"),
            P("seq", None, "head"),
            P("seq", None, "head"),
            P("seq", "head"),
            P("seq", "head"),
            P(),
            P("seq"),
            P(),
        ),
        out_specs=P(None, "seq"),
        check_vma=False,
    )
```

```python
import math

import jax
import jax.numpy as jnp
from jax import lax
from jax.sharding import PartitionSpec as P

HD = 128
PAGE = 128


masked_low = -1e30


def widen(factor, size):
    return jnp.repeat(factor, size, axis=1)


def split_three(x):
    hi = lax.reduce_precision(x, 8, 7)
    rest = x - hi
    mid = lax.reduce_precision(rest, 8, 7)
    return hi, mid, rest - mid


def exchange(x, axis, n):
    return lax.all_to_all(x.reshape(n, x.shape[0] // n, x.shape[1]), axis, 0, 0)


def gather_direct(x, axis, n):
    return lax.all_to_all(jnp.broadcast_to(x[None], (n, *x.shape)), axis, 0, 0).reshape(
        n * x.shape[0], x.shape[1]
    )


def swap(x, axis, n, mask):
    return lax.ppermute(x, axis, [(j, j ^ mask) for j in range(n)])


def bit_groups(n):
    groups, shift = [], 0
    while (1 << shift) < n:
        size = min(4, n >> shift)
        groups.append((shift, size))
        shift += size.bit_length() - 1
    return groups


def scatter_sum(x, axis, n):
    me = lax.axis_index(axis)
    for shift, size in bit_groups(n):
        digit = (me >> shift) % size
        x = x.reshape(x.shape[0] // size, size, *x.shape[1:])

        def block(offset):
            return lax.dynamic_index_in_dim(x, digit ^ offset, axis=1, keepdims=False)

        parts = [swap(block(d), axis, n, d << shift) for d in range(1, size)]
        x = sum(parts, block(0))
    return x[0]


def gather_relative(x, axis, n):
    for shift, size in reversed(bit_groups(n)):
        parts = [x] + [swap(x, axis, n, d << shift) for d in range(1, size)]
        x = jnp.concatenate(parts, axis=0)
    return x


def relative_blocks(n):
    offsets = [0]
    for shift, size in reversed(bit_groups(n)):
        offsets = [d << shift | e for d in range(size) for e in offsets]
    return offsets


def body(
    hidden_in,
    w_query,
    w_keyval,
    w_out,
    key_cache,
    value_cache,
    key_scale,
    value_scale,
    page_counts,
    slot_pages,
    trim,
    seq_size,
    head_size,
):
    requests = hidden_in.shape[0]
    slots = key_cache.shape[0]
    kv_local = w_keyval.shape[1] // (2 * HD)
    heads_local = w_query.shape[1] // HD
    group = heads_local // kv_local
    wide = heads_local * HD
    mine = requests // seq_size
    inverse_square_root = 1.0 / math.sqrt(HD)

    part_query = jnp.dot(hidden_in, w_query, preferred_element_type=jnp.float32)
    part_keyval = jnp.dot(hidden_in, w_keyval, preferred_element_type=jnp.float32)
    part_all = jnp.concatenate([part_query, part_keyval], axis=1)
    sums = scatter_sum(
        part_all.reshape(seq_size, mine, part_all.shape[1]), "seq", seq_size
    ).astype(jnp.bfloat16)
    my_query, my_keyval = sums[:, :wide], sums[:, wide:]
    query = gather_relative(my_query, "seq", seq_size)
    offsets = jnp.array(relative_blocks(seq_size), dtype=jnp.int32)
    row_request = (
        (lax.axis_index("seq") ^ offsets)[:, None] * mine
        + jnp.arange(mine, dtype=jnp.int32)[None, :]
    ).reshape(requests)

    start = jnp.cumsum(page_counts) - page_counts
    ends = start + page_counts
    owner = jnp.sum((ends[None, :] <= slot_pages[:, None]).astype(jnp.int32), axis=1)
    selector = owner[:, None] == jnp.arange(requests, dtype=jnp.int32)[None, :]
    select_int = selector.astype(jnp.int32)
    index = slot_pages - jnp.sum(select_int * start[None, :], axis=1)
    lengths = PAGE * page_counts - trim
    page_len = jnp.sum(select_int * lengths[None, :], axis=1)

    q_sel = jnp.dot(
        (owner[:, None] == row_request[None, :]).astype(jnp.bfloat16),
        query,
        preferred_element_type=jnp.float32,
    ).astype(jnp.bfloat16)
    q_sel = q_sel.reshape(slots, kv_local, group, HD)
    key_rows = key_cache.reshape(slots, PAGE, kv_local, HD)
    value_rows = value_cache.reshape(slots, PAGE, kv_local, HD)
    unscaled_pages = jnp.einsum(
        "sgjd,stgd->sgjt", q_sel, key_rows, preferred_element_type=jnp.float32
    )
    score_matrix = unscaled_pages * (key_scale * inverse_square_root)[:, :, None, None]
    position = index[:, None] * PAGE + jnp.arange(PAGE, dtype=jnp.int32)[None, :]
    valid = (position < page_len[:, None])[:, None, None, :]
    score_matrix = jnp.where(valid, score_matrix, masked_low)
    page_max = jnp.max(score_matrix, axis=-1)
    probs = jnp.where(valid, jnp.exp(score_matrix - page_max[..., None]), 0.0).astype(jnp.bfloat16)
    page_sum = jnp.sum(probs.astype(jnp.float32), axis=-1).reshape(slots, heads_local)
    page_out = jnp.einsum("sgjt,stgd->sgjd", probs, value_rows, preferred_element_type=jnp.float32)
    page_out = (page_out * value_scale[:, :, None, None]).reshape(slots, heads_local, HD)
    page_max = page_max.reshape(slots, heads_local)
    select_float = selector.astype(jnp.float32)
    dev_max = jnp.max(jnp.where(selector[:, :, None], page_max[:, None, :], masked_low), axis=0)
    slot_max = jnp.max(jnp.where(selector[:, :, None], dev_max[None, :, :], masked_low), axis=1)
    weight = jnp.exp(page_max - slot_max)
    dev_sum = jnp.dot(select_float.T, page_sum * weight, precision=lax.Precision.HIGHEST)
    weighted = (page_out * weight[:, :, None]).reshape(slots, wide)
    dev_out = jnp.dot(select_float.T, weighted, precision=lax.Precision.HIGHEST)

    pieces = jnp.concatenate([*split_three(dev_max), *split_three(dev_sum)], axis=1)
    pieces = jnp.pad(pieces, ((0, 0), (0, -pieces.shape[1] % 128)))
    packed = jnp.concatenate([dev_out, pieces], axis=1).astype(jnp.bfloat16)
    got = exchange(packed, "seq", seq_size).astype(jnp.float32)
    out_parts = got[:, :, :wide]
    stat = got[:, :, wide : wide + 6 * heads_local].reshape(seq_size, mine, 6, heads_local)
    max_parts = stat[:, :, 0] + stat[:, :, 1] + stat[:, :, 2]
    sum_parts = stat[:, :, 3] + stat[:, :, 4] + stat[:, :, 5]

    pairs = my_keyval.reshape(mine, kv_local, 2, HD)
    new_key = pairs[:, :, 0]
    new_value = pairs[:, :, 1].astype(jnp.float32)
    own = (
        jnp.einsum(
            "rgjd,rgd->rgj",
            my_query.reshape(mine, kv_local, group, HD),
            new_key,
            preferred_element_type=jnp.float32,
        ).reshape(mine, heads_local)
        * inverse_square_root
    )
    top = jnp.maximum(jnp.max(max_parts, axis=0), own)
    factor = jnp.exp(max_parts - top[None])
    new_part = jnp.exp(own - top)
    denom = jnp.sum(sum_parts * factor, axis=0) + new_part
    numer = jnp.sum(
        out_parts.reshape(seq_size, mine, heads_local, HD) * factor[..., None], axis=0
    )
    spread_value = jnp.broadcast_to(
        new_value[:, :, None, :], (mine, kv_local, group, HD)
    ).reshape(mine, heads_local, HD)
    numer = numer + new_part[..., None] * spread_value
    my_context = (numer / denom[..., None]).astype(jnp.bfloat16).reshape(mine, wide)
    context = gather_direct(my_context, "seq", seq_size)

    total = jnp.dot(context, w_out, preferred_element_type=jnp.float32)
    step = 1
    while step < head_size:
        if step > 1:
            total = lax.reduce_precision(total, 8, 7)
            other = swap(total.astype(jnp.bfloat16), "head", head_size, step)
        else:
            other = swap(total, "head", head_size, step)
        total = total + other.astype(jnp.float32)
        step *= 2
    return total.astype(jnp.bfloat16)


def solution(mesh):
    seq_size, head_size = mesh.shape["seq"], mesh.shape["head"]

    def local(*args):
        return body(*args, seq_size=seq_size, head_size=head_size)

    return jax.shard_map(
        local,
        mesh=mesh,
        in_specs=(
            P(None, "seq"),
            P("seq", "head"),
            P("seq", "head"),
            P("head", "seq"),
            P("seq", None, "head"),
            P("seq", None, "head"),
            P("seq", "head"),
            P("seq", "head"),
            P(),
            P("seq"),
            P(),
        ),
        out_specs=P(None, "seq"),
        check_vma=False,
    )
```

```python
import functools
import math

import jax
import jax.numpy as jnp
from jax import lax
from jax.experimental import pallas as pl
from jax.experimental.pallas import tpu as pltpu
from jax.sharding import PartitionSpec as P

HD = 128
PAGE = 128
LANES = 128
CHUNK = 8
STAT = 16


masked_low = -1e30


def gather_direct(x, axis, n):
    return lax.all_to_all(jnp.broadcast_to(x[None], (n, *x.shape)), axis, 0, 0).reshape(
        n * x.shape[0], x.shape[1]
    )


def swap(x, axis, n, mask):
    return lax.ppermute(x, axis, [(j, j ^ mask) for j in range(n)])


def bit_groups(n):
    groups, shift = [], 0
    while (1 << shift) < n:
        size = min(4, n >> shift)
        groups.append((shift, size))
        shift += size.bit_length() - 1
    return groups


def scatter_sum(x, axis, n):
    me = lax.axis_index(axis)
    for shift, size in bit_groups(n):
        digit = (me >> shift) % size
        x = x.reshape(x.shape[0] // size, size, *x.shape[1:])

        def block(offset):
            return lax.dynamic_index_in_dim(x, digit ^ offset, axis=1, keepdims=False)

        parts = [swap(block(d), axis, n, d << shift) for d in range(1, size)]
        x = sum(parts, block(0))
    return x[0]


def gather_relative(x, axis, n):
    for shift, size in reversed(bit_groups(n)):
        parts = [x] + [swap(x, axis, n, d << shift) for d in range(1, size)]
        x = jnp.concatenate(parts, axis=0)
    return x


def relative_place(offset, n):
    place, weight = 0, n
    for shift, size in bit_groups(n):
        weight //= size
        place = place + ((offset >> shift) & (size - 1)) * weight
    return place


def attention_kernel(
    row_of,
    request_of,
    value_scale,
    query,
    key_factor,
    valid,
    owner,
    key_cache,
    value_cache,
    out,
    query_low,
    query_high,
    keys,
    values,
    scores,
    page_max,
    dev_max,
    total_out,
    total_sum,
    total_max,
    key_sem,
    value_sem,
):
    slots = key_cache.shape[0]
    heads = LANES // CHUNK
    group = heads // 2
    chunks = slots // CHUNK
    blocks, block_rows, _ = out.shape
    mine = block_rows // heads - 1

    def key_copy(c):
        part = pl.ds(c * CHUNK, CHUNK)
        return pltpu.make_async_copy(key_cache.at[part], keys.at[part], key_sem.at[c])

    def value_copy(c):
        part = pl.ds(c * CHUNK, CHUNK)
        return pltpu.make_async_copy(value_cache.at[part], values.at[part], value_sem.at[c])

    for c in range(chunks):
        key_copy(c).start()
    for c in range(chunks):
        value_copy(c).start()

    rows = query[...]
    low_head = lax.broadcasted_iota(jnp.int32, rows.shape, 0) % heads < group
    zero = jnp.zeros_like(rows)
    query_low[...] = jnp.where(low_head, rows, zero)
    query_high[...] = jnp.where(low_head, zero, rows)
    total_out[...] = jnp.zeros_like(total_out)
    total_sum[...] = jnp.zeros_like(total_sum)
    total_max[...] = jnp.full_like(total_max, masked_low)

    lane_slot = lax.broadcasted_iota(jnp.int32, (PAGE, LANES), 1) // heads
    token = lax.broadcasted_iota(jnp.int32, (PAGE, LANES), 0)

    @pl.loop(0, chunks)
    def _(c):
        places = [pl.multiple_of(row_of[c * CHUNK + s] * heads, heads) for s in range(CHUNK)]
        chosen = jnp.concatenate(
            [
                jnp.concatenate([ref[pl.ds(place, heads), :] for place in places], axis=0)
                for ref in (query_low, query_high)
            ],
            axis=1,
        )
        key_copy(c).wait()
        block = keys[pl.ds(c * CHUNK, CHUNK)].reshape(CHUNK * PAGE, 2 * HD)
        every = lax.dot_general(
            block, chosen, (((1,), (1,)), ((), ())), preferred_element_type=jnp.float32
        )
        score = every[:PAGE]
        for s in range(1, CHUNK):
            score = jnp.where(lane_slot == s, every[s * PAGE : (s + 1) * PAGE], score)
        score = jnp.where(
            token < valid[pl.ds(c, 1), :], score * key_factor[pl.ds(c, 1), :], masked_low
        )
        scores[c] = score
        page_max[pl.ds(c, 1), :] = jnp.max(score, axis=0, keepdims=True)

    biggest, who = page_max[...], owner[...]
    best = biggest
    for turn in range(CHUNK):
        other = pltpu.roll(biggest, turn * heads, 1) if turn else biggest
        other_who = pltpu.roll(who, turn * heads, 1) if turn else who
        for c in range(chunks):
            best = jnp.maximum(
                best, jnp.where(other_who[c : c + 1] == who, other[c : c + 1], masked_low)
            )
    dev_max[...] = best

    ones = jnp.ones((PAGE, LANES), jnp.bfloat16)

    @pl.loop(0, chunks)
    def _(c):
        top = dev_max[pl.ds(c, 1), :]
        prob = jnp.exp(scores[c] - top).T.astype(jnp.bfloat16)
        top_rows = jnp.broadcast_to(top, (PAGE, LANES)).T
        sums = jnp.dot(prob, ones, preferred_element_type=jnp.float32)
        empty = jnp.zeros((heads, PAGE), jnp.bfloat16)
        value_copy(c).wait()
        for s in range(0, CHUNK, 2):
            pair = jnp.concatenate(
                [
                    jnp.concatenate([prob[s * heads : (s + 1) * heads], empty], axis=1),
                    jnp.concatenate([empty, prob[(s + 1) * heads : (s + 2) * heads]], axis=1),
                ],
                axis=0,
            )
            block = values[pl.ds(c * CHUNK + s, 2)].reshape(2 * PAGE, 2 * HD)
            both = jnp.dot(pair, block, preferred_element_type=jnp.float32)
            for t in range(2):
                slot = c * CHUNK + s + t
                here = pl.ds(pl.multiple_of(request_of[slot] * heads, heads), heads)
                base = t * heads
                total_out[here, :] += jnp.concatenate(
                    [
                        both[base : base + group, :HD] * value_scale[2 * slot],
                        both[base + group : base + heads, HD:] * value_scale[2 * slot + 1],
                    ],
                    axis=0,
                )
                part = slice((s + t) * heads, (s + t + 1) * heads)
                total_sum[here, :] += sums[part]
                total_max[here, :] = top_rows[part]

    lane = lax.broadcasted_iota(jnp.int32, (heads, LANES), 1)
    for b in range(blocks):
        first = b * mine * heads
        out[b, : mine * heads, :] = total_out[first : first + mine * heads, :].astype(jnp.bfloat16)
        stat = jnp.zeros((heads, LANES), jnp.float32)
        for r in range(mine):
            part = slice(first + r * heads, first + (r + 1) * heads)
            both = jnp.where(lane % STAT < STAT // 2, total_max[part, :], total_sum[part, :])
            hi = both.astype(jnp.bfloat16).astype(jnp.float32)
            rest = both - hi
            mid = rest.astype(jnp.bfloat16).astype(jnp.float32)
            piece = jnp.where(lane < STAT, hi, jnp.where(lane < 2 * STAT, mid, rest - mid))
            stat = jnp.where(lane % (STAT // 2) == r, piece, stat)
        out[b, mine * heads :, :] = stat.astype(jnp.bfloat16)


def finish_kernel(got, query, keyval, out):
    sources, block_rows, _ = got.shape
    heads = LANES // CHUNK
    group = heads // 2
    mine = block_rows // heads - 1
    lane = lax.broadcasted_iota(jnp.int32, (heads, LANES), 1)
    low_head = lax.broadcasted_iota(jnp.int32, (heads, LANES), 0) < group
    new = keyval[...].astype(jnp.float32)

    def spread(r, which):
        low = jnp.broadcast_to(new[4 * r + which : 4 * r + which + 1], (heads, LANES))
        high = jnp.broadcast_to(new[4 * r + 2 + which : 4 * r + 3 + which], (heads, LANES))
        return jnp.where(low_head, low, high)

    own = jnp.zeros((heads, LANES), jnp.float32)
    for r in range(mine):
        rows = query[r * heads : (r + 1) * heads, :].astype(jnp.float32)
        dot = jnp.sum(rows * spread(r, 0), axis=1, keepdims=True) * (1.0 / math.sqrt(HD))
        own = jnp.where(lane == r, dot, own)
    maxima, sums = [], []
    for j in range(sources):
        stat = got[j, mine * heads :, :].astype(jnp.float32)
        whole = (stat + pltpu.roll(stat, LANES - STAT, 1)) + pltpu.roll(stat, LANES - 2 * STAT, 1)
        maxima.append(jnp.where(lane < mine, whole, 0.0))
        sums.append(jnp.where(lane < mine, pltpu.roll(whole, LANES - STAT // 2, 1), 0.0))
    top = functools.reduce(jnp.maximum, maxima, own)
    fresh = jnp.exp(own - top)
    factors = [jnp.exp(m - top) for m in maxima]
    denom = sum((s * f for s, f in zip(sums, factors)), fresh)
    fresh = fresh / denom
    factors = [f / denom for f in factors]
    for r in range(mine):
        numer = fresh[:, r : r + 1] * spread(r, 1)
        for j in range(sources):
            part = got[j, r * heads : (r + 1) * heads, :].astype(jnp.float32)
            numer = numer + factors[j][:, r : r + 1] * part
        out[r * heads : (r + 1) * heads, :] = numer.astype(jnp.bfloat16)


def body(
    hidden_in,
    w_query,
    w_keyval,
    w_out,
    key_cache,
    value_cache,
    key_scale,
    value_scale,
    page_counts,
    slot_pages,
    trim,
    seq_size,
    head_size,
):
    requests = hidden_in.shape[0]
    slots = key_cache.shape[0]
    kv_local = w_keyval.shape[1] // (2 * HD)
    heads_local = w_query.shape[1] // HD
    wide = heads_local * HD
    assert kv_local == 2 and heads_local * CHUNK == LANES
    assert slots % CHUNK == 0
    mine = requests // seq_size
    inverse_square_root = 1.0 / math.sqrt(HD)

    start = jnp.cumsum(page_counts) - page_counts
    ends = start + page_counts
    owner = jnp.sum((ends[None, :] <= slot_pages[:, None]).astype(jnp.int32), axis=1)
    selector = owner[:, None] == jnp.arange(requests, dtype=jnp.int32)[None, :]
    select_int = selector.astype(jnp.int32)
    index = slot_pages - jnp.sum(select_int * start[None, :], axis=1)
    lengths = PAGE * page_counts - trim
    page_valid = jnp.sum(select_int * lengths[None, :], axis=1) - index * PAGE
    block = owner // mine
    row_of = (
        relative_place(lax.axis_index("seq") ^ block, seq_size) * mine + owner - block * mine
    )

    def on_lanes(x):
        return jnp.broadcast_to(x, (slots, heads_local)).reshape(slots // CHUNK, LANES)

    key_factor = on_lanes(
        jnp.repeat(key_scale * inverse_square_root, heads_local // kv_local, axis=1)
    )
    valid = on_lanes(page_valid[:, None])
    owner_lanes = on_lanes(owner[:, None])

    part_query = jnp.dot(hidden_in, w_query, preferred_element_type=jnp.float32)
    part_keyval = jnp.dot(hidden_in, w_keyval, preferred_element_type=jnp.float32)
    part_all = jnp.concatenate([part_query, part_keyval], axis=1)
    sums = scatter_sum(
        part_all.reshape(seq_size, mine, part_all.shape[1]), "seq", seq_size
    ).astype(jnp.bfloat16)
    my_query = sums[:, :wide].reshape(mine * heads_local, HD)
    my_keyval = sums[:, wide:].reshape(mine * 2 * kv_local, HD)
    query = gather_relative(my_query, "seq", seq_size)

    smem = pl.BlockSpec(memory_space=pltpu.SMEM)
    vmem = pl.BlockSpec(memory_space=pltpu.VMEM)
    hbm = pl.BlockSpec(memory_space=pl.ANY)
    chunks = slots // CHUNK
    every_row = requests * heads_local
    block_rows = (mine + 1) * heads_local
    totals = pl.pallas_call(
        attention_kernel,
        out_shape=jax.ShapeDtypeStruct((seq_size, block_rows, HD), jnp.bfloat16),
        in_specs=[smem, smem, smem, vmem, vmem, vmem, vmem, hbm, hbm],
        out_specs=vmem,
        scratch_shapes=[
            pltpu.VMEM((every_row, HD), jnp.bfloat16),
            pltpu.VMEM((every_row, HD), jnp.bfloat16),
            pltpu.VMEM(key_cache.shape, jnp.bfloat16),
            pltpu.VMEM(value_cache.shape, jnp.bfloat16),
            pltpu.VMEM((chunks, PAGE, LANES), jnp.float32),
            pltpu.VMEM((chunks, LANES), jnp.float32),
            pltpu.VMEM((chunks, LANES), jnp.float32),
            pltpu.VMEM((every_row, HD), jnp.float32),
            pltpu.VMEM((every_row, HD), jnp.float32),
            pltpu.VMEM((every_row, HD), jnp.float32),
            pltpu.SemaphoreType.DMA((chunks,)),
            pltpu.SemaphoreType.DMA((chunks,)),
        ],
        compiler_params=pltpu.CompilerParams(vmem_limit_bytes=40 * 2**20),
        cost_estimate=pl.CostEstimate(
            flops=4 * slots * PAGE * wide,
            bytes_accessed=2 * (key_cache.size + value_cache.size),
            transcendentals=slots * PAGE * heads_local,
        ),
        name="paged_attention",
    )(
        row_of,
        owner,
        value_scale.reshape(slots * kv_local),
        query,
        key_factor,
        valid,
        owner_lanes,
        key_cache,
        value_cache,
    )

    got = lax.all_to_all(totals, "seq", 0, 0)
    my_context = pl.pallas_call(
        finish_kernel,
        out_shape=jax.ShapeDtypeStruct((mine * heads_local, HD), jnp.bfloat16),
        in_specs=[vmem, vmem, vmem],
        out_specs=vmem,
        name="finish",
    )(got, my_query, my_keyval).reshape(mine, wide)
    context = gather_direct(my_context, "seq", seq_size)

    total = jnp.dot(context, w_out, preferred_element_type=jnp.float32)
    step = 1
    while step < head_size:
        if step > 1:
            total = lax.reduce_precision(total, 8, 7)
            other = swap(total.astype(jnp.bfloat16), "head", head_size, step)
        else:
            other = swap(total, "head", head_size, step)
        total = total + other.astype(jnp.float32)
        step *= 2
    return total.astype(jnp.bfloat16)


def solution(mesh):
    seq_size, head_size = mesh.shape["seq"], mesh.shape["head"]

    def local(*args):
        return body(*args, seq_size=seq_size, head_size=head_size)

    return jax.shard_map(
        local,
        mesh=mesh,
        in_specs=(
            P(None, "seq"),
            P("seq", "head"),
            P("seq", "head"),
            P("head", "seq"),
            P("seq", None, "head"),
            P("seq", None, "head"),
            P("seq", "head"),
            P("seq", "head"),
            P(),
            P("seq"),
            P(),
        ),
        out_specs=P(None, "seq"),
        check_vma=False,
    )
```

```python
import functools
import math

import jax
import jax.numpy as jnp
from jax import lax
from jax.experimental import pallas as pl
from jax.experimental.pallas import tpu as pltpu
from jax.sharding import PartitionSpec as P

HD = 128
PAGE = 128
LANES = 128
CHUNK = 8
STAT = 16


masked_low = -1e30


def swap(x, axis, n, mask):
    return lax.ppermute(x, axis, [(j, j ^ mask) for j in range(n)])


def bit_groups(n):
    groups, shift = [], 0
    while (1 << shift) < n:
        size = min(4, n >> shift)
        groups.append((shift, size))
        shift += size.bit_length() - 1
    return groups


def scatter_sum(x, axis, n, beside):
    me = lax.axis_index(axis)
    for shift, size in bit_groups(n):
        digit = (me >> shift) % size
        x = x.reshape(x.shape[0] // size, size, *x.shape[1:])

        def block(offset):
            return lax.dynamic_index_in_dim(x, digit ^ offset, axis=1, keepdims=False)

        parts = [swap(block(d), axis, n, d << shift) for d in range(1, size)]
        if shift == 0:
            parts, beside = lax.optimization_barrier((parts, beside))
        x = sum(parts, block(0))
    return x[0], beside


def gather_relative(x, axis, n):
    for shift, size in reversed(bit_groups(n)):
        parts = [x] + [swap(x, axis, n, d << shift) for d in range(1, size)]
        x = jnp.concatenate(parts, axis=0)
    return x


def gather_in_order(x, axis, n):
    rows = x.shape[0]
    me = lax.axis_index(axis)
    held = [(0, x)]
    out = jnp.zeros((n * rows, x.shape[1]), x.dtype)
    for shift, size in reversed(bit_groups(n)):
        stacked = jnp.concatenate([block for _, block in held], axis=0)
        held = [
            (d << shift | offset, part[i * rows : (i + 1) * rows])
            for d in range(size)
            for part in [swap(stacked, axis, n, d << shift) if d else stacked]
            for i, (offset, _) in enumerate(held)
        ]
    for offset, block in held:
        out = lax.dynamic_update_slice_in_dim(out, block, (me ^ offset) * rows, axis=0)
    return out


def relative_place(offset, n):
    place, weight = 0, n
    for shift, size in bit_groups(n):
        weight //= size
        place = place + ((offset >> shift) & (size - 1)) * weight
    return place


def attention_kernel(
    place_of,
    query,
    tables,
    key_cache,
    value_cache,
    out,
    query_low,
    query_high,
    keys,
    values,
    probs,
    page_out,
    page_sum,
    page_max,
    dev_max,
    total_out,
    total_stat,
    key_sem,
    value_sem,
):
    slots = key_cache.shape[0]
    heads = LANES // CHUNK
    group = heads // 2
    chunks = slots // CHUNK
    blocks, block_rows, _ = out.shape
    mine = block_rows // heads - 1
    chunk_rows = CHUNK * heads

    def key_copy(c):
        part = pl.ds(c * CHUNK, CHUNK)
        return pltpu.make_async_copy(key_cache.at[part], keys.at[part], key_sem.at[c])

    def value_copy(c):
        part = pl.ds(c * CHUNK, CHUNK)
        return pltpu.make_async_copy(value_cache.at[part], values.at[part], value_sem.at[c])

    for c in range(chunks):
        key_copy(c).start()
        value_copy(c).start()

    rows = query[...]
    low_head = lax.broadcasted_iota(jnp.int32, rows.shape, 0) % heads < group
    zero = jnp.zeros_like(rows)
    query_low[...] = jnp.where(low_head, rows, zero)
    query_high[...] = jnp.where(low_head, zero, rows)
    total_out[...] = jnp.zeros_like(total_out)
    stat_lane = lax.broadcasted_iota(jnp.int32, total_stat.shape, 1) % STAT
    total_stat[...] = jnp.where(stat_lane < STAT // 2, masked_low, 0.0)

    def table(which, c):
        return tables[pl.ds(which * chunks + c, 1), :]

    lane_slot = lax.broadcasted_iota(jnp.int32, (PAGE, LANES), 1) // heads
    token = lax.broadcasted_iota(jnp.int32, (PAGE, LANES), 0).astype(jnp.float32)

    def score_chunk(c):
        places = [
            pl.multiple_of((place_of[c * CHUNK + s] >> 16) * heads, heads)
            for s in range(CHUNK)
        ]
        chosen = jnp.concatenate(
            [
                jnp.concatenate([ref[pl.ds(place, heads), :] for place in places], axis=0)
                for ref in (query_low, query_high)
            ],
            axis=1,
        )
        block = keys[pl.ds(c * CHUNK, CHUNK)].reshape(CHUNK * PAGE, 2 * HD)
        every = lax.dot_general(
            block, chosen, (((1,), (1,)), ((), ())), preferred_element_type=jnp.float32
        )
        score = every[:PAGE]
        for s in range(1, CHUNK):
            score = jnp.where(lane_slot == s, every[s * PAGE : (s + 1) * PAGE], score)
        score = jnp.where(token < table(1, c), score * table(0, c), masked_low)
        top = jnp.max(score, axis=0, keepdims=True)
        page_max[pl.ds(c, 1), :] = top
        probs[c] = jnp.exp(score - top).T.astype(jnp.bfloat16)

    ones = jnp.ones((PAGE, LANES), jnp.bfloat16)
    empty = jnp.zeros((heads, PAGE), jnp.bfloat16)

    def value_chunk(c):
        prob = probs[c]
        page_sum[pl.ds(pl.multiple_of(c * chunk_rows, chunk_rows), chunk_rows), :] = jnp.dot(
            prob, ones, preferred_element_type=jnp.float32
        )
        for s in range(0, CHUNK, 2):
            pair = jnp.concatenate(
                [
                    jnp.concatenate([prob[s * heads : (s + 1) * heads], empty], axis=1),
                    jnp.concatenate([empty, prob[(s + 1) * heads : (s + 2) * heads]], axis=1),
                ],
                axis=0,
            )
            block = values[pl.ds(c * CHUNK + s, 2)].reshape(2 * PAGE, 2 * HD)
            both = jnp.dot(pair, block, preferred_element_type=jnp.float32)
            page_out[pl.ds(pl.multiple_of((c * CHUNK + s) * heads, heads), 2 * heads), :] = (
                jnp.concatenate(
                    [
                        both[:group, :HD],
                        both[group:heads, HD:],
                        both[heads : heads + group, :HD],
                        both[heads + group :, HD:],
                    ],
                    axis=0,
                )
            )

    key_copy(0).wait()
    score_chunk(0)

    @pl.loop(1, chunks)
    def _(c):
        key_copy(c).wait()
        value_copy(c - 1).wait()
        value_chunk(c - 1)
        score_chunk(c)

    value_copy(chunks - 1).wait()
    value_chunk(chunks - 1)

    biggest, who = page_max[...], tables[3 * chunks :, :]
    best = biggest
    for turn in range(CHUNK):
        other = pltpu.roll(biggest, turn * heads, 1) if turn else biggest
        other_who = pltpu.roll(who, turn * heads, 1) if turn else who
        for c in range(chunks):
            best = jnp.maximum(
                best, jnp.where(other_who[c : c + 1] == who, other[c : c + 1], masked_low)
            )
    dev_max[...] = best

    keep_max = lax.broadcasted_iota(jnp.int32, (heads, LANES), 1) % STAT < STAT // 2

    @pl.loop(0, chunks)
    def _(c):
        top = dev_max[pl.ds(c, 1), :]
        weight = jnp.exp(page_max[pl.ds(c, 1), :] - top)

        def on_rows(x):
            return jnp.broadcast_to(x, (PAGE, LANES)).T

        out_weight, weight, top = on_rows(weight * table(2, c)), on_rows(weight), on_rows(top)
        for s in range(CHUNK):
            here = pl.ds(
                pl.multiple_of((place_of[c * CHUNK + s] & 0xFFFF) * heads, heads), heads
            )
            there = pl.ds(pl.multiple_of((c * CHUNK + s) * heads, heads), heads)
            part = slice(s * heads, (s + 1) * heads)
            total_out[here, :] += page_out[there, :] * out_weight[part]
            total_stat[here, :] = jnp.where(
                keep_max, top[part], total_stat[here, :] + page_sum[there, :] * weight[part]
            )

    lane = lax.broadcasted_iota(jnp.int32, (heads, LANES), 1)
    for b in range(blocks):
        first = b * mine * heads
        out[b, : mine * heads, :] = total_out[first : first + mine * heads, :].astype(jnp.bfloat16)
        stat = jnp.zeros((heads, LANES), jnp.float32)
        for r in range(mine):
            both = total_stat[first + r * heads : first + (r + 1) * heads, :]
            stat = jnp.where(lane % (STAT // 2) == r, both, stat)
        hi = stat.astype(jnp.bfloat16).astype(jnp.float32)
        rest = stat - hi
        mid = rest.astype(jnp.bfloat16).astype(jnp.float32)
        piece = jnp.where(lane < STAT, hi, jnp.where(lane < 2 * STAT, mid, rest - mid))
        out[b, mine * heads :, :] = piece.astype(jnp.bfloat16)


def finish_kernel(got, query, keyval, out):
    sources, block_rows, _ = got.shape
    heads = LANES // CHUNK
    group = heads // 2
    mine = block_rows // heads - 1
    lane = lax.broadcasted_iota(jnp.int32, (heads, LANES), 1)
    low_head = lax.broadcasted_iota(jnp.int32, (heads, LANES), 0) < group
    new = keyval[...].astype(jnp.float32)

    def spread(r, which):
        low = jnp.broadcast_to(new[4 * r + which : 4 * r + which + 1], (heads, LANES))
        high = jnp.broadcast_to(new[4 * r + 2 + which : 4 * r + 3 + which], (heads, LANES))
        return jnp.where(low_head, low, high)

    own = jnp.zeros((heads, LANES), jnp.float32)
    for r in range(mine):
        rows = query[r * heads : (r + 1) * heads, :].astype(jnp.float32)
        dot = jnp.sum(rows * spread(r, 0), axis=1, keepdims=True) * (1.0 / math.sqrt(HD))
        own = jnp.where(lane == r, dot, own)
    maxima, sums = [], []
    for j in range(sources):
        stat = got[j, mine * heads :, :].astype(jnp.float32)
        whole = (stat + pltpu.roll(stat, LANES - STAT, 1)) + pltpu.roll(stat, LANES - 2 * STAT, 1)
        maxima.append(jnp.where(lane < mine, whole, 0.0))
        sums.append(jnp.where(lane < mine, pltpu.roll(whole, LANES - STAT // 2, 1), 0.0))
    top = functools.reduce(jnp.maximum, maxima, own)
    fresh = jnp.exp(own - top)
    factors = [jnp.exp(m - top) for m in maxima]
    denom = sum((s * f for s, f in zip(sums, factors)), fresh)
    fresh = fresh / denom
    factors = [f / denom for f in factors]
    for r in range(mine):
        numer = fresh[:, r : r + 1] * spread(r, 1)
        for j in range(sources):
            part = got[j, r * heads : (r + 1) * heads, :].astype(jnp.float32)
            numer = numer + factors[j][:, r : r + 1] * part
        out[r * heads : (r + 1) * heads, :] = numer.astype(jnp.bfloat16)


def body(
    hidden_in,
    w_query,
    w_keyval,
    w_out,
    key_cache,
    value_cache,
    key_scale,
    value_scale,
    page_counts,
    slot_pages,
    trim,
    seq_size,
    head_size,
):
    requests = hidden_in.shape[0]
    slots = key_cache.shape[0]
    kv_local = w_keyval.shape[1] // (2 * HD)
    heads_local = w_query.shape[1] // HD
    wide = heads_local * HD
    assert kv_local == 2 and heads_local * CHUNK == LANES
    assert slots % CHUNK == 0
    mine = requests // seq_size
    inverse_square_root = 1.0 / math.sqrt(HD)

    start = jnp.cumsum(page_counts) - page_counts
    ends = start + page_counts
    owner = jnp.sum((ends[None, :] <= slot_pages[:, None]).astype(jnp.int32), axis=1)
    selector = owner[:, None] == jnp.arange(requests, dtype=jnp.int32)[None, :]
    select_int = selector.astype(jnp.int32)
    index = slot_pages - jnp.sum(select_int * start[None, :], axis=1)
    lengths = PAGE * page_counts - trim
    page_valid = jnp.sum(select_int * lengths[None, :], axis=1) - index * PAGE
    block = owner // mine
    row_of = (
        relative_place(lax.axis_index("seq") ^ block, seq_size) * mine + owner - block * mine
    )

    def on_lanes(x):
        return jnp.broadcast_to(x, (slots, heads_local)).reshape(slots // CHUNK, LANES)

    def per_head(x):
        return on_lanes(jnp.repeat(x, heads_local // kv_local, axis=1))

    tables = jnp.concatenate(
        [
            per_head(key_scale * inverse_square_root),
            on_lanes(page_valid[:, None].astype(jnp.float32)),
            per_head(value_scale),
            on_lanes(owner[:, None].astype(jnp.float32)),
        ],
        axis=0,
    )
    place_of = row_of * 65536 + owner

    part_query = jnp.dot(hidden_in, w_query, preferred_element_type=jnp.float32)
    part_keyval = jnp.dot(hidden_in, w_keyval, preferred_element_type=jnp.float32)
    part_all = jnp.concatenate([part_query, part_keyval], axis=1)
    sums, (tables, place_of) = scatter_sum(
        part_all.reshape(seq_size, mine, part_all.shape[1]), "seq", seq_size, (tables, place_of)
    )
    sums = sums.astype(jnp.bfloat16)
    my_query = sums[:, :wide].reshape(mine * heads_local, HD)
    my_keyval = sums[:, wide:].reshape(mine * 2 * kv_local, HD)
    query = gather_relative(my_query, "seq", seq_size)

    smem = pl.BlockSpec(memory_space=pltpu.SMEM)
    vmem = pl.BlockSpec(memory_space=pltpu.VMEM)
    hbm = pl.BlockSpec(memory_space=pl.ANY)
    chunks = slots // CHUNK
    every_row = requests * heads_local
    block_rows = (mine + 1) * heads_local
    totals = pl.pallas_call(
        attention_kernel,
        out_shape=jax.ShapeDtypeStruct((seq_size, block_rows, HD), jnp.bfloat16),
        in_specs=[smem, vmem, vmem, hbm, hbm],
        out_specs=vmem,
        scratch_shapes=[
            pltpu.VMEM((every_row, HD), jnp.bfloat16),
            pltpu.VMEM((every_row, HD), jnp.bfloat16),
            pltpu.VMEM(key_cache.shape, jnp.bfloat16),
            pltpu.VMEM(value_cache.shape, jnp.bfloat16),
            pltpu.VMEM((chunks, LANES, PAGE), jnp.bfloat16),
            pltpu.VMEM((slots * heads_local, HD), jnp.float32),
            pltpu.VMEM((slots * heads_local, HD), jnp.float32),
            pltpu.VMEM((chunks, LANES), jnp.float32),
            pltpu.VMEM((chunks, LANES), jnp.float32),
            pltpu.VMEM((every_row, HD), jnp.float32),
            pltpu.VMEM((every_row, HD), jnp.float32),
            pltpu.SemaphoreType.DMA((chunks,)),
            pltpu.SemaphoreType.DMA((chunks,)),
        ],
        compiler_params=pltpu.CompilerParams(vmem_limit_bytes=58 * 2**20),
        cost_estimate=pl.CostEstimate(
            flops=4 * slots * PAGE * wide,
            bytes_accessed=2 * (key_cache.size + value_cache.size),
            transcendentals=slots * PAGE * heads_local,
        ),
        name="paged_attention",
    )(place_of, query, tables, key_cache, value_cache)

    got = lax.all_to_all(totals, "seq", 0, 0)
    my_context = pl.pallas_call(
        finish_kernel,
        out_shape=jax.ShapeDtypeStruct((mine * heads_local, HD), jnp.bfloat16),
        in_specs=[vmem, vmem, vmem],
        out_specs=vmem,
        compiler_params=pltpu.CompilerParams(vmem_limit_bytes=6 * 2**20),
        name="finish",
    )(got, my_query, my_keyval).reshape(mine, wide)
    context = gather_in_order(my_context, "seq", seq_size)

    total = jnp.dot(context, w_out, preferred_element_type=jnp.float32)
    step = 1
    while step < head_size:
        if step > 1:
            total = lax.reduce_precision(total, 8, 7)
            other = swap(total.astype(jnp.bfloat16), "head", head_size, step)
        else:
            other = swap(total, "head", head_size, step)
        total = total + other.astype(jnp.float32)
        step *= 2
    return total.astype(jnp.bfloat16)


def solution(mesh):
    seq_size, head_size = mesh.shape["seq"], mesh.shape["head"]

    def local(*args):
        return body(*args, seq_size=seq_size, head_size=head_size)

    return jax.shard_map(
        local,
        mesh=mesh,
        in_specs=(
            P(None, "seq"),
            P("seq", "head"),
            P("seq", "head"),
            P("head", "seq"),
            P("seq", None, "head"),
            P("seq", None, "head"),
            P("seq", "head"),
            P("seq", "head"),
            P(),
            P("seq"),
            P(),
        ),
        out_specs=P(None, "seq"),
        check_vma=False,
    )
```

```python
import functools
import math

import jax
import jax.numpy as jnp
from jax import lax
from jax.experimental import pallas as pl
from jax.experimental.pallas import tpu as pltpu
from jax.sharding import PartitionSpec as P

HD = 128
PAGE = 128
LANES = 128
CHUNK = 8
STAT = 16


masked_low = -1e30


def swap(x, axis, n, mask):
    return lax.ppermute(x, axis, [(j, j ^ mask) for j in range(n)])


def bit_groups(n):
    groups, shift = [], 0
    while (1 << shift) < n:
        size = min(4, n >> shift)
        groups.append((shift, size))
        shift += size.bit_length() - 1
    return groups


def lower_groups(n):
    return bit_groups(n)[:-1]


def last_group(n):
    return bit_groups(n)[-1]


def pick_digit(x, axis, shift, size, offset):
    digit = (lax.axis_index(axis) >> shift) % size
    x = x.reshape(x.shape[0] // size, size, *x.shape[1:])
    return lax.dynamic_index_in_dim(x, digit ^ offset, axis=1, keepdims=False)


def scatter_sum(x, axis, n, beside):
    for shift, size in lower_groups(n):
        parts = [
            swap(pick_digit(x, axis, shift, size, d), axis, n, d << shift) for d in range(1, size)
        ]
        if shift == 0:
            parts, beside = lax.optimization_barrier((parts, beside))
        x = sum(parts, pick_digit(x, axis, shift, size, 0))
    shift, size = last_group(n)
    return sum([swap(x, axis, n, d << shift) for d in range(1, size)], x), beside


def gather_relative(x, axis, n):
    for shift, size in reversed(lower_groups(n)):
        parts = [x] + [swap(x, axis, n, d << shift) for d in range(1, size)]
        x = jnp.concatenate(parts, axis=0)
    return x


def relative_place(block, axis, n):
    last_shift, last_size = last_group(n)
    offset = lax.axis_index(axis) ^ block
    place, weight = block >> last_shift, n
    for shift, size in lower_groups(n):
        weight //= size
        place = place + ((offset >> shift) & (size - 1)) * weight
    return place


def gather_in_order(x, axis, n):
    last_shift, last_size = last_group(n)
    rows = x.shape[0] // last_size
    me = lax.axis_index(axis) & ((1 << last_shift) - 1)
    held = [(0, x)]
    out = jnp.zeros((n * rows, x.shape[1]), x.dtype)
    for shift, size in reversed(lower_groups(n)):
        stacked = jnp.concatenate([part for _, part in held], axis=0)
        height = x.shape[0]
        held = [
            (d << shift | offset, part[i * height : (i + 1) * height])
            for d in range(size)
            for part in [swap(stacked, axis, n, d << shift) if d else stacked]
            for i, (offset, _) in enumerate(held)
        ]
    for offset, part in held:
        for c in range(last_size):
            out = lax.dynamic_update_slice_in_dim(
                out,
                part[c * rows : (c + 1) * rows],
                ((c << last_shift) + (me ^ offset)) * rows,
                axis=0,
            )
    return out


def split_stat(stat, lane):
    hi = stat.astype(jnp.bfloat16).astype(jnp.float32)
    rest = stat - hi
    mid = rest.astype(jnp.bfloat16).astype(jnp.float32)
    piece = jnp.where(lane < STAT, hi, jnp.where(lane < 2 * STAT, mid, rest - mid))
    return piece.astype(jnp.bfloat16)


def join_stat(pieces):
    pieces = pieces.astype(jnp.float32)
    return (pieces + pltpu.roll(pieces, LANES - STAT, 1)) + pltpu.roll(
        pieces, LANES - 2 * STAT, 1
    )


def attention_kernel(
    place_of,
    query,
    tables,
    key_cache,
    value_cache,
    out,
    query_low,
    query_high,
    keys,
    values,
    probs,
    page_out,
    page_sum,
    page_max,
    dev_max,
    total_out,
    total_stat,
    key_sem,
    value_sem,
):
    slots = key_cache.shape[0]
    heads = LANES // CHUNK
    group = heads // 2
    chunks = slots // CHUNK
    blocks, block_rows, _ = out.shape
    mine = block_rows // heads - 1

    def key_copy(c):
        part = pl.ds(c * CHUNK, CHUNK)
        return pltpu.make_async_copy(key_cache.at[part], keys.at[part], key_sem.at[c])

    def value_copy(c):
        part = pl.ds(c * CHUNK, CHUNK)
        return pltpu.make_async_copy(value_cache.at[part], values.at[part], value_sem.at[c])

    for c in range(chunks):
        key_copy(c).start()
        value_copy(c).start()

    rows = query[...]
    low_head = lax.broadcasted_iota(jnp.int32, rows.shape, 0) % heads < group
    zero = jnp.zeros_like(rows)
    query_low[...] = jnp.where(low_head, rows, zero)
    query_high[...] = jnp.where(low_head, zero, rows)
    total_out[...] = jnp.zeros_like(total_out)
    stat_lane = lax.broadcasted_iota(jnp.int32, total_stat.shape, 1) % STAT
    total_stat[...] = jnp.where(stat_lane < STAT // 2, masked_low, 0.0)

    def table(which, c):
        return tables[pl.ds(which * chunks + c, 1), :]

    lane_slot = lax.broadcasted_iota(jnp.int32, (PAGE, LANES), 1) // heads
    token = lax.broadcasted_iota(jnp.int32, (PAGE, LANES), 0).astype(jnp.float32)

    def score_chunk(c):
        places = [
            pl.multiple_of((place_of[c * CHUNK + s] >> 16) * heads, heads)
            for s in range(CHUNK)
        ]
        chosen = jnp.concatenate(
            [
                jnp.concatenate([ref[pl.ds(place, heads), :] for place in places], axis=0)
                for ref in (query_low, query_high)
            ],
            axis=1,
        )
        block = keys[pl.ds(c * CHUNK, CHUNK)].reshape(CHUNK * PAGE, 2 * HD)
        every = lax.dot_general(
            block, chosen, (((1,), (1,)), ((), ())), preferred_element_type=jnp.float32
        )
        score = every[:PAGE]
        for s in range(1, CHUNK):
            score = jnp.where(lane_slot == s, every[s * PAGE : (s + 1) * PAGE], score)
        score = jnp.where(token < table(1, c), score * table(0, c), masked_low)
        top = jnp.max(score, axis=0, keepdims=True)
        page_max[pl.ds(c, 1), :] = top
        prob = jnp.exp(score - top).astype(jnp.bfloat16).astype(jnp.float32)
        page_sum[pl.ds(c, 1), :] = jnp.sum(prob, axis=0, keepdims=True)
        probs[c] = prob.T.astype(jnp.bfloat16)

    empty = jnp.zeros((heads, PAGE), jnp.bfloat16)

    def value_chunk(c):
        prob = probs[c]
        for s in range(0, CHUNK, 2):
            pair = jnp.concatenate(
                [
                    jnp.concatenate([prob[s * heads : (s + 1) * heads], empty], axis=1),
                    jnp.concatenate([empty, prob[(s + 1) * heads : (s + 2) * heads]], axis=1),
                ],
                axis=0,
            )
            block = values[pl.ds(c * CHUNK + s, 2)].reshape(2 * PAGE, 2 * HD)
            both = jnp.dot(pair, block, preferred_element_type=jnp.float32)
            page_out[pl.ds(pl.multiple_of((c * CHUNK + s) * heads, heads), 2 * heads), :] = (
                jnp.concatenate(
                    [
                        both[:group, :HD],
                        both[group:heads, HD:],
                        both[heads : heads + group, :HD],
                        both[heads + group :, HD:],
                    ],
                    axis=0,
                )
            )

    for c in range(2):
        key_copy(c).wait()
    for c in range(2):
        score_chunk(c)

    @pl.loop(1, chunks // 2)
    def _(step):
        for c in range(2):
            key_copy(2 * step + c).wait()
            value_copy(2 * step + c - 2).wait()
        for c in range(2):
            value_chunk(2 * step + c - 2)
            score_chunk(2 * step + c)

    for c in range(chunks - 2, chunks):
        value_copy(c).wait()
    for c in range(chunks - 2, chunks):
        value_chunk(c)

    biggest, who = page_max[...], tables[3 * chunks :, :]
    best = biggest
    for turn in range(CHUNK):
        other = pltpu.roll(biggest, turn * heads, 1) if turn else biggest
        other_who = pltpu.roll(who, turn * heads, 1) if turn else who
        for c in range(chunks):
            best = jnp.maximum(
                best, jnp.where(other_who[c : c + 1] == who, other[c : c + 1], masked_low)
            )
    dev_max[...] = best

    keep_max = lax.broadcasted_iota(jnp.int32, (heads, LANES), 1) % STAT < STAT // 2

    keep_max_row = lax.broadcasted_iota(jnp.int32, (PAGE, LANES), 0) % STAT < STAT // 2

    @pl.loop(0, chunks // 2)
    def _(step):
        for c in (2 * step, 2 * step + 1):
            top = dev_max[pl.ds(c, 1), :]
            weight = jnp.exp(page_max[pl.ds(c, 1), :] - top)
            out_weight = jnp.broadcast_to(weight * table(2, c), (PAGE, LANES)).T
            stat = jnp.where(keep_max_row, top, weight * page_sum[pl.ds(c, 1), :]).T
            for s in range(CHUNK):
                here = pl.ds(
                    pl.multiple_of((place_of[c * CHUNK + s] & 0xFFFF) * heads, heads), heads
                )
                there = pl.ds(pl.multiple_of((c * CHUNK + s) * heads, heads), heads)
                part = slice(s * heads, (s + 1) * heads)
                total_out[here, :] += page_out[there, :] * out_weight[part]
                total_stat[here, :] = jnp.where(
                    keep_max, stat[part], total_stat[here, :] + stat[part]
                )

    lane = lax.broadcasted_iota(jnp.int32, (heads, LANES), 1)
    for b in range(blocks):
        first = b * mine * heads
        out[b, : mine * heads, :] = total_out[first : first + mine * heads, :].astype(jnp.bfloat16)
        stat = jnp.zeros((heads, LANES), jnp.float32)
        for r in range(mine):
            both = total_stat[first + r * heads : first + (r + 1) * heads, :]
            stat = jnp.where(lane % (STAT // 2) == r, both, stat)
        out[b, mine * heads :, :] = split_stat(stat, lane)


def combine_kernel(*refs):
    *parts, out = refs
    blocks, block_rows, _ = out.shape
    heads = LANES // CHUNK
    mine = block_rows // heads - 1
    lane = lax.broadcasted_iota(jnp.int32, (heads, LANES), 1)
    for b in range(blocks):
        stats = [join_stat(part[b, mine * heads :, :]) for part in parts]
        maxima = [jnp.where(lane < mine, stat, 0.0) for stat in stats]
        top = functools.reduce(jnp.maximum, maxima)
        factors = [jnp.exp(m - top) for m in maxima]
        sums = sum(
            pltpu.roll(f, STAT // 2, 1) * jnp.where(lane < STAT, stat, 0.0)
            for f, stat in zip(factors, stats)
        )
        both = jnp.where(lane < STAT // 2, top, sums)
        both = jnp.where(lane < STAT, both, 0.0)
        both = (both + pltpu.roll(both, STAT, 1)) + pltpu.roll(both, 2 * STAT, 1)
        out[b, mine * heads :, :] = split_stat(both, lane)
        for r in range(mine):
            rows = slice(r * heads, (r + 1) * heads)
            numer = sum(
                f[:, r : r + 1] * part[b, rows, :].astype(jnp.float32)
                for f, part in zip(factors, parts)
            )
            out[b, rows, :] = numer.astype(jnp.bfloat16)


def finish_kernel(*refs):
    *parts, query, keyval, out = refs
    blocks, block_rows, _ = parts[0].shape
    heads = LANES // CHUNK
    group = heads // 2
    mine = block_rows // heads - 1
    lane = lax.broadcasted_iota(jnp.int32, (heads, LANES), 1)
    low_head = lax.broadcasted_iota(jnp.int32, (heads, LANES), 0) < group
    new = keyval[...].astype(jnp.float32)

    def spread(r, which):
        low = jnp.broadcast_to(new[4 * r + which : 4 * r + which + 1], (heads, LANES))
        high = jnp.broadcast_to(new[4 * r + 2 + which : 4 * r + 3 + which], (heads, LANES))
        return jnp.where(low_head, low, high)

    for b in range(blocks):
        own = jnp.zeros((heads, LANES), jnp.float32)
        for r in range(mine):
            request = b * mine + r
            rows = query[request * heads : (request + 1) * heads, :].astype(jnp.float32)
            dot = jnp.sum(rows * spread(request, 0), axis=1, keepdims=True)
            own = jnp.where(lane == r, dot * (1.0 / math.sqrt(HD)), own)
        maxima, sums = [], []
        for part in parts:
            whole = join_stat(part[b, mine * heads :, :])
            maxima.append(jnp.where(lane < mine, whole, 0.0))
            sums.append(jnp.where(lane < mine, pltpu.roll(whole, LANES - STAT // 2, 1), 0.0))
        top = functools.reduce(jnp.maximum, maxima, own)
        fresh = jnp.exp(own - top)
        factors = [jnp.exp(m - top) for m in maxima]
        denom = sum((s * f for s, f in zip(sums, factors)), fresh)
        fresh = fresh / denom
        factors = [f / denom for f in factors]
        for r in range(mine):
            numer = fresh[:, r : r + 1] * spread(b * mine + r, 1)
            for part, f in zip(parts, factors):
                rows = part[b, r * heads : (r + 1) * heads, :].astype(jnp.float32)
                numer = numer + f[:, r : r + 1] * rows
            request = b * mine + r
            out[request * heads : (request + 1) * heads, :] = numer.astype(jnp.bfloat16)


def body(
    hidden_in,
    w_query,
    w_keyval,
    w_out,
    key_cache,
    value_cache,
    key_scale,
    value_scale,
    page_counts,
    slot_pages,
    trim,
    seq_size,
    head_size,
):
    requests = hidden_in.shape[0]
    slots = key_cache.shape[0]
    kv_local = w_keyval.shape[1] // (2 * HD)
    heads_local = w_query.shape[1] // HD
    wide = heads_local * HD
    assert kv_local == 2 and heads_local * CHUNK == LANES
    assert slots % CHUNK == 0
    mine = requests // seq_size
    inverse_square_root = 1.0 / math.sqrt(HD)

    start = jnp.cumsum(page_counts) - page_counts
    ends = start + page_counts
    owner = jnp.sum((ends[None, :] <= slot_pages[:, None]).astype(jnp.int32), axis=1)
    selector = owner[:, None] == jnp.arange(requests, dtype=jnp.int32)[None, :]
    select_int = selector.astype(jnp.int32)
    index = slot_pages - jnp.sum(select_int * start[None, :], axis=1)
    lengths = PAGE * page_counts - trim
    page_valid = jnp.sum(select_int * lengths[None, :], axis=1) - index * PAGE
    block = owner // mine
    row_of = relative_place(block, "seq", seq_size) * mine + owner - block * mine

    def on_lanes(x):
        return jnp.broadcast_to(x, (slots, heads_local)).reshape(slots // CHUNK, LANES)

    def per_head(x):
        return on_lanes(jnp.repeat(x, heads_local // kv_local, axis=1))

    tables = jnp.concatenate(
        [
            per_head(key_scale * inverse_square_root),
            on_lanes(page_valid[:, None].astype(jnp.float32)),
            per_head(value_scale),
            on_lanes(owner[:, None].astype(jnp.float32)),
        ],
        axis=0,
    )
    place_of = row_of * 65536 + owner

    part_query = jnp.dot(hidden_in, w_query, preferred_element_type=jnp.float32)
    part_keyval = jnp.dot(hidden_in, w_keyval, preferred_element_type=jnp.float32)
    part_all = jnp.concatenate([part_query, part_keyval], axis=1)
    sums, (tables, place_of) = scatter_sum(
        part_all.reshape(seq_size, mine, part_all.shape[1]), "seq", seq_size, (tables, place_of)
    )
    sums = sums.astype(jnp.bfloat16)
    held = last_group(seq_size)[1] * mine
    sums = sums.reshape(held, -1)
    my_query = sums[:, :wide].reshape(held * heads_local, HD)
    my_keyval = sums[:, wide:].reshape(held * 2 * kv_local, HD)
    query = gather_relative(my_query, "seq", seq_size)

    smem = pl.BlockSpec(memory_space=pltpu.SMEM)
    vmem = pl.BlockSpec(memory_space=pltpu.VMEM)
    hbm = pl.BlockSpec(memory_space=pl.ANY)
    chunks = slots // CHUNK
    every_row = requests * heads_local
    block_rows = (mine + 1) * heads_local
    totals = pl.pallas_call(
        attention_kernel,
        out_shape=jax.ShapeDtypeStruct((seq_size, block_rows, HD), jnp.bfloat16),
        in_specs=[smem, vmem, vmem, hbm, hbm],
        out_specs=vmem,
        scratch_shapes=[
            pltpu.VMEM((every_row, HD), jnp.bfloat16),
            pltpu.VMEM((every_row, HD), jnp.bfloat16),
            pltpu.VMEM(key_cache.shape, jnp.bfloat16),
            pltpu.VMEM(value_cache.shape, jnp.bfloat16),
            pltpu.VMEM((chunks, LANES, PAGE), jnp.bfloat16),
            pltpu.VMEM((slots * heads_local, HD), jnp.float32),
            pltpu.VMEM((chunks, LANES), jnp.float32),
            pltpu.VMEM((chunks, LANES), jnp.float32),
            pltpu.VMEM((chunks, LANES), jnp.float32),
            pltpu.VMEM((every_row, HD), jnp.float32),
            pltpu.VMEM((every_row, HD), jnp.float32),
            pltpu.SemaphoreType.DMA((chunks,)),
            pltpu.SemaphoreType.DMA((chunks,)),
        ],
        compiler_params=pltpu.CompilerParams(vmem_limit_bytes=58 * 2**20),
        cost_estimate=pl.CostEstimate(
            flops=4 * slots * PAGE * wide,
            bytes_accessed=2 * (key_cache.size + value_cache.size),
            transcendentals=slots * PAGE * heads_local,
        ),
        name="paged_attention",
    )(place_of, query, tables, key_cache, value_cache)

    for shift, size in lower_groups(seq_size):
        parts = [pick_digit(totals, "seq", shift, size, 0)] + [
            swap(pick_digit(totals, "seq", shift, size, d), "seq", seq_size, d << shift)
            for d in range(1, size)
        ]
        totals = pl.pallas_call(
            combine_kernel,
            out_shape=jax.ShapeDtypeStruct(parts[0].shape, jnp.bfloat16),
            in_specs=[vmem] * size,
            out_specs=vmem,
            compiler_params=pltpu.CompilerParams(vmem_limit_bytes=6 * 2**20),
            name="combine",
        )(*parts)
    shift, size = last_group(seq_size)
    parts = [totals] + [swap(totals, "seq", seq_size, d << shift) for d in range(1, size)]
    my_context = pl.pallas_call(
        finish_kernel,
        out_shape=jax.ShapeDtypeStruct((held * heads_local, HD), jnp.bfloat16),
        in_specs=[vmem] * (size + 2),
        out_specs=vmem,
        compiler_params=pltpu.CompilerParams(vmem_limit_bytes=6 * 2**20),
        name="finish",
    )(*parts, my_query, my_keyval).reshape(held, wide)
    context = gather_in_order(my_context, "seq", seq_size)

    total = jnp.dot(context, w_out, preferred_element_type=jnp.float32)
    step = 1
    while step < head_size:
        if step > 1:
            total = lax.reduce_precision(total, 8, 7)
            other = swap(total.astype(jnp.bfloat16), "head", head_size, step)
        else:
            other = swap(total, "head", head_size, step)
        total = total + other.astype(jnp.float32)
        step *= 2
    return total.astype(jnp.bfloat16)


def solution(mesh):
    seq_size, head_size = mesh.shape["seq"], mesh.shape["head"]

    def local(*args):
        return body(*args, seq_size=seq_size, head_size=head_size)

    return jax.shard_map(
        local,
        mesh=mesh,
        in_specs=(
            P(None, "seq"),
            P("seq", "head"),
            P("seq", "head"),
            P("head", "seq"),
            P("seq", None, "head"),
            P("seq", None, "head"),
            P("seq", "head"),
            P("seq", "head"),
            P(),
            P("seq"),
            P(),
        ),
        out_specs=P(None, "seq"),
        check_vma=False,
    )
```

```python
import functools
import math

import jax
import jax.numpy as jnp
from jax import lax
from jax.experimental import pallas as pl
from jax.experimental.pallas import tpu as pltpu
from jax.sharding import PartitionSpec as P

HD = 128
PAGE = 128
LANES = 128
CHUNK = 8
STAT = 16


masked_low = -1e30


def swap(x, axis, n, mask):
    return lax.ppermute(x, axis, [(j, j ^ mask) for j in range(n)])


def bit_groups(n):
    groups, shift = [], 0
    while (1 << shift) < n:
        size = min(4, n >> shift)
        groups.append((shift, size))
        shift += size.bit_length() - 1
    return groups


def lower_groups(n):
    return bit_groups(n)[:-1]


def last_group(n):
    return bit_groups(n)[-1]


def pick_digit(x, axis, shift, size, offset):
    digit = (lax.axis_index(axis) >> shift) % size
    x = x.reshape(x.shape[0] // size, size, *x.shape[1:])
    return lax.dynamic_index_in_dim(x, digit ^ offset, axis=1, keepdims=False)


def after(parts, *earlier):
    return lax.optimization_barrier((parts, *earlier))[0]


def scatter_sums(halves, axis, n, beside):
    for shift, size in lower_groups(n):
        sent = [
            [swap(pick_digit(x, axis, shift, size, d), axis, n, d << shift) for d in range(1, size)]
            for x in halves
        ]
        if shift == 0:
            sent[0], beside = lax.optimization_barrier((sent[0], beside))
        sums = []
        for x, parts in zip(halves, sent):
            if sums:
                parts = after(parts, sums[-1])
            sums.append(sum(parts, pick_digit(x, axis, shift, size, 0)))
        halves = sums
    shift, size = last_group(n)
    sent = [[swap(x, axis, n, d << shift) for d in range(1, size)] for x in halves]
    sums = []
    for x, parts in zip(halves, sent):
        if sums:
            parts = after(parts, sums[-1])
        sums.append(sum(parts, x).astype(jnp.bfloat16))
    return sums, beside


def gather_relative(x, axis, n):
    parts = [x]
    for shift, size in reversed(lower_groups(n)):
        x = jnp.concatenate(parts, axis=0) if len(parts) > 1 else parts[0]
        parts = [x] + [swap(x, axis, n, d << shift) for d in range(1, size)]
    return parts


def relative_place(block, axis, n):
    last_shift, last_size = last_group(n)
    offset = lax.axis_index(axis) ^ block
    place, weight = block >> last_shift, n
    for shift, size in lower_groups(n):
        weight //= size
        place = place + ((offset >> shift) & (size - 1)) * weight
    return place


def gather_in_order(x, axis, n):
    last_shift, last_size = last_group(n)
    rows = x.shape[0] // last_size
    me = lax.axis_index(axis) & ((1 << last_shift) - 1)
    held = [(0, x)]
    out = jnp.zeros((n * rows, x.shape[1]), x.dtype)
    for shift, size in reversed(lower_groups(n)):
        stacked = jnp.concatenate([part for _, part in held], axis=0)
        height = x.shape[0]
        held = [
            (d << shift | offset, part[i * height : (i + 1) * height])
            for d in range(size)
            for part in [swap(stacked, axis, n, d << shift) if d else stacked]
            for i, (offset, _) in enumerate(held)
        ]
    for offset, part in held:
        for c in range(last_size):
            out = lax.dynamic_update_slice_in_dim(
                out,
                part[c * rows : (c + 1) * rows],
                ((c << last_shift) + (me ^ offset)) * rows,
                axis=0,
            )
    return out


def split_stat(stat, lane):
    hi = stat.astype(jnp.bfloat16).astype(jnp.float32)
    rest = stat - hi
    mid = rest.astype(jnp.bfloat16).astype(jnp.float32)
    piece = jnp.where(lane < STAT, hi, jnp.where(lane < 2 * STAT, mid, rest - mid))
    return piece.astype(jnp.bfloat16)


def join_stat(pieces):
    pieces = pieces.astype(jnp.float32)
    return (pieces + pltpu.roll(pieces, LANES - STAT, 1)) + pltpu.roll(
        pieces, LANES - 2 * STAT, 1
    )


def attention_kernel(ways, place_of, *refs):
    queries, refs = refs[: 2 * ways], refs[2 * ways :]
    (tables, key_cache, value_cache), refs = refs[:3], refs[3:]
    outs, refs = refs[:ways], refs[ways:]
    (
        query_low,
        query_high,
        keys,
        values,
        probs,
        page_out,
        page_sum,
        page_max,
        dev_max,
        total_out,
        total_stat,
        key_sem,
        value_sem,
    ) = refs
    slots = key_cache.shape[0]
    heads = LANES // CHUNK
    group = heads // 2
    chunks = slots // CHUNK
    blocks, block_rows, _ = outs[0].shape
    mine = block_rows // heads - 1
    step_chunks = 4

    def key_copy(c):
        part = pl.ds(c * CHUNK, CHUNK)
        return pltpu.make_async_copy(key_cache.at[part], keys.at[part], key_sem.at[c])

    def value_copy(c):
        part = pl.ds(c * CHUNK, CHUNK)
        return pltpu.make_async_copy(value_cache.at[part], values.at[part], value_sem.at[c])

    for c in range(chunks + step_chunks):
        if c >= step_chunks:
            value_copy(c - step_chunks).start()
        if c < chunks:
            key_copy(c).start()

    for ref, parts in ((query_low, queries[:ways]), (query_high, queries[ways:])):
        for d, part in enumerate(parts):
            count = part.shape[0]
            rows = part[...].astype(jnp.float32).reshape(count // group, group, HD)
            zero = jnp.zeros_like(rows)
            both = [rows, zero] if ref is query_low else [zero, rows]
            ref[2 * count * d : 2 * count * (d + 1), :] = (
                jnp.concatenate(both, axis=1).reshape(2 * count, HD).astype(jnp.bfloat16)
            )
    total_out[...] = jnp.zeros_like(total_out)
    stat_lane = lax.broadcasted_iota(jnp.int32, total_stat.shape, 1) % STAT
    total_stat[...] = jnp.where(stat_lane < STAT // 2, masked_low, 0.0)

    def table(which, c):
        return tables[pl.ds(which * chunks + c, 1), :]

    lane_slot = lax.broadcasted_iota(jnp.int32, (PAGE, LANES), 1) // heads
    token = lax.broadcasted_iota(jnp.int32, (PAGE, LANES), 0).astype(jnp.float32)

    def score_chunk(c):
        places = [
            pl.multiple_of(((place_of[c * CHUNK + s] >> 16) & 0xFF) * heads, heads)
            for s in range(CHUNK)
        ]
        chosen = jnp.concatenate(
            [
                jnp.concatenate([ref[pl.ds(place, heads), :] for place in places], axis=0)
                for ref in (query_low, query_high)
            ],
            axis=1,
        )
        block = keys[pl.ds(c * CHUNK, CHUNK)].reshape(CHUNK * PAGE, 2 * HD)
        every = lax.dot_general(
            block, chosen, (((1,), (1,)), ((), ())), preferred_element_type=jnp.float32
        )
        score = every[:PAGE]
        for s in range(1, CHUNK):
            score = jnp.where(lane_slot == s, every[s * PAGE : (s + 1) * PAGE], score)
        score = jnp.where(token < table(1, c), score * table(0, c), masked_low)
        top = jnp.max(score, axis=0, keepdims=True)
        page_max[pl.ds(c, 1), :] = top
        prob = jnp.exp(score - top).astype(jnp.bfloat16).astype(jnp.float32)
        page_sum[pl.ds(c, 1), :] = jnp.sum(prob, axis=0, keepdims=True)
        probs[c] = prob.T.astype(jnp.bfloat16)

    empty = jnp.zeros((heads, PAGE), jnp.bfloat16)

    def value_chunk(c):
        prob = probs[c]
        for s in range(0, CHUNK, 2):
            pair = jnp.concatenate(
                [
                    jnp.concatenate([prob[s * heads : (s + 1) * heads], empty], axis=1),
                    jnp.concatenate([empty, prob[(s + 1) * heads : (s + 2) * heads]], axis=1),
                ],
                axis=0,
            )
            block = values[pl.ds(c * CHUNK + s, 2)].reshape(2 * PAGE, 2 * HD)
            both = jnp.dot(pair, block, preferred_element_type=jnp.float32)
            page_out[pl.ds(pl.multiple_of((c * CHUNK + s) * heads, heads), 2 * heads), :] = (
                jnp.concatenate(
                    [
                        both[:group, :HD],
                        both[group:heads, HD:],
                        both[heads : heads + group, :HD],
                        both[heads + group :, HD:],
                    ],
                    axis=0,
                )
            )

    for c in range(step_chunks):
        key_copy(c).wait()
        score_chunk(c)

    @pl.loop(1, chunks // step_chunks)
    def _(step):
        first = step * step_chunks
        for c in range(step_chunks):
            key_copy(first + c).wait()
            value_copy(first + c - step_chunks).wait()
        for c in range(step_chunks):
            value_chunk(first + c - step_chunks)
            score_chunk(first + c)

    for c in range(chunks - step_chunks, chunks):
        value_copy(c).wait()
    for c in range(chunks - step_chunks, chunks):
        value_chunk(c)

    biggest, who = page_max[...], tables[3 * chunks :, :]
    best = biggest
    for turn in range(CHUNK):
        other = pltpu.roll(biggest, turn * heads, 1) if turn else biggest
        other_who = pltpu.roll(who, turn * heads, 1) if turn else who
        for c in range(chunks):
            best = jnp.maximum(
                best, jnp.where(other_who[c : c + 1] == who, other[c : c + 1], masked_low)
            )
    dev_max[...] = best

    keep_max = lax.broadcasted_iota(jnp.int32, (heads, LANES), 1) % STAT < STAT // 2

    keep_max_row = lax.broadcasted_iota(jnp.int32, (PAGE, LANES), 0) % STAT < STAT // 2

    @pl.loop(0, chunks // step_chunks)
    def _(step):
        for c in [step * step_chunks + c for c in range(step_chunks)]:
            top = dev_max[pl.ds(c, 1), :]
            weight = jnp.exp(page_max[pl.ds(c, 1), :] - top)
            out_weight = jnp.broadcast_to(weight * table(2, c), (PAGE, LANES)).T
            stat = jnp.where(keep_max_row, top, weight * page_sum[pl.ds(c, 1), :]).T
            for s in range(CHUNK):
                here = pl.ds(
                    pl.multiple_of((place_of[c * CHUNK + s] & 0xFFFF) * heads, heads), heads
                )
                there = pl.ds(pl.multiple_of((c * CHUNK + s) * heads, heads), heads)
                part = slice(s * heads, (s + 1) * heads)
                total_out[here, :] += page_out[there, :] * out_weight[part]
                total_stat[here, :] = jnp.where(
                    keep_max, stat[part], total_stat[here, :] + stat[part]
                )

    lane = lax.broadcasted_iota(jnp.int32, (heads, LANES), 1)
    digit = place_of[0] >> 24
    for d, out in enumerate(outs):
        for b in range(blocks):
            first = (b * ways + (digit ^ d)) * (mine * heads)
            rows = pl.ds(pl.multiple_of(first, mine * heads), mine * heads)
            out[b, : mine * heads, :] = total_out[rows, :].astype(jnp.bfloat16)
            both = total_stat[rows, :]
            stat = jnp.zeros((heads, LANES), jnp.float32)
            for r in range(mine):
                stat = jnp.where(
                    lane % (STAT // 2) == r, both[r * heads : (r + 1) * heads], stat
                )
            out[b, mine * heads :, :] = split_stat(stat, lane)


def combine_kernel(*refs):
    *parts, out = refs
    blocks, block_rows, _ = out.shape
    heads = LANES // CHUNK
    mine = block_rows // heads - 1
    lane = lax.broadcasted_iota(jnp.int32, (heads, LANES), 1)
    for b in range(blocks):
        stats = [join_stat(part[b, mine * heads :, :]) for part in parts]
        maxima = [jnp.where(lane < mine, stat, 0.0) for stat in stats]
        top = functools.reduce(jnp.maximum, maxima)
        factors = [jnp.exp(m - top) for m in maxima]
        sums = sum(
            pltpu.roll(f, STAT // 2, 1) * jnp.where(lane < STAT, stat, 0.0)
            for f, stat in zip(factors, stats)
        )
        both = jnp.where(lane < STAT // 2, top, sums)
        both = jnp.where(lane < STAT, both, 0.0)
        both = (both + pltpu.roll(both, STAT, 1)) + pltpu.roll(both, 2 * STAT, 1)
        out[b, mine * heads :, :] = split_stat(both, lane)
        for r in range(mine):
            rows = slice(r * heads, (r + 1) * heads)
            numer = sum(
                f[:, r : r + 1] * part[b, rows, :].astype(jnp.float32)
                for f, part in zip(factors, parts)
            )
            out[b, rows, :] = numer.astype(jnp.bfloat16)


def finish_kernel(*refs):
    *parts, query_low, query_high, new_low, new_high, out = refs
    blocks, block_rows, _ = parts[0].shape
    heads = LANES // CHUNK
    group = heads // 2
    mine = block_rows // heads - 1
    lane = lax.broadcasted_iota(jnp.int32, (heads, LANES), 1)
    low_head = lax.broadcasted_iota(jnp.int32, (heads, LANES), 0) < group
    news = [ref[...].astype(jnp.float32) for ref in (new_low, new_high)]
    queries = [ref[...].astype(jnp.float32) for ref in (query_low, query_high)]

    def spread(r, which):
        low, high = [
            jnp.broadcast_to(new[2 * r + which : 2 * r + which + 1], (heads, LANES)) for new in news
        ]
        return jnp.where(low_head, low, high)

    for b in range(blocks):
        own = jnp.zeros((heads, LANES), jnp.float32)
        for r in range(mine):
            request = b * mine + r
            rows = jnp.concatenate(
                [query[request * group : (request + 1) * group] for query in queries], axis=0
            )
            dot = jnp.sum(rows * spread(request, 0), axis=1, keepdims=True)
            own = jnp.where(lane == r, dot * (1.0 / math.sqrt(HD)), own)
        maxima, sums = [], []
        for part in parts:
            whole = join_stat(part[b, mine * heads :, :])
            maxima.append(jnp.where(lane < mine, whole, 0.0))
            sums.append(jnp.where(lane < mine, pltpu.roll(whole, LANES - STAT // 2, 1), 0.0))
        top = functools.reduce(jnp.maximum, maxima, own)
        fresh = jnp.exp(own - top)
        factors = [jnp.exp(m - top) for m in maxima]
        denom = sum((s * f for s, f in zip(sums, factors)), fresh)
        fresh = fresh / denom
        factors = [f / denom for f in factors]
        for r in range(mine):
            numer = fresh[:, r : r + 1] * spread(b * mine + r, 1)
            for part, f in zip(parts, factors):
                rows = part[b, r * heads : (r + 1) * heads, :].astype(jnp.float32)
                numer = numer + f[:, r : r + 1] * rows
            request = b * mine + r
            out[request * heads : (request + 1) * heads, :] = numer.astype(jnp.bfloat16)


def body(
    hidden_in,
    w_query,
    w_keyval,
    w_out,
    key_cache,
    value_cache,
    key_scale,
    value_scale,
    page_counts,
    slot_pages,
    trim,
    seq_size,
    head_size,
):
    requests = hidden_in.shape[0]
    slots = key_cache.shape[0]
    kv_local = w_keyval.shape[1] // (2 * HD)
    heads_local = w_query.shape[1] // HD
    wide = heads_local * HD
    group = heads_local // kv_local
    assert kv_local == 2 and heads_local * CHUNK == LANES
    assert slots % CHUNK == 0
    mine = requests // seq_size
    inverse_square_root = 1.0 / math.sqrt(HD)

    start = jnp.cumsum(page_counts) - page_counts
    ends = start + page_counts
    owner = jnp.sum((ends[None, :] <= slot_pages[:, None]).astype(jnp.int32), axis=1)
    selector = owner[:, None] == jnp.arange(requests, dtype=jnp.int32)[None, :]
    select_int = selector.astype(jnp.int32)
    index = slot_pages - jnp.sum(select_int * start[None, :], axis=1)
    lengths = PAGE * page_counts - trim
    page_valid = jnp.sum(select_int * lengths[None, :], axis=1) - index * PAGE
    block = owner // mine
    row_of = relative_place(block, "seq", seq_size) * mine + owner - block * mine

    def on_lanes(x):
        return jnp.broadcast_to(x, (slots, heads_local)).reshape(slots // CHUNK, LANES)

    def per_head(x):
        return on_lanes(jnp.repeat(x, heads_local // kv_local, axis=1))

    tables = jnp.concatenate(
        [
            per_head(key_scale * inverse_square_root),
            on_lanes(page_valid[:, None].astype(jnp.float32)),
            per_head(value_scale),
            on_lanes(owner[:, None].astype(jnp.float32)),
        ],
        axis=0,
    )
    ways = lower_groups(seq_size)[0][1]
    digit = lax.axis_index("seq") & (ways - 1)
    place_of = (digit << 24) + row_of * 65536 + owner

    part_query = jnp.dot(hidden_in, w_query, preferred_element_type=jnp.float32)
    part_keyval = jnp.dot(hidden_in, w_keyval, preferred_element_type=jnp.float32)
    held = last_group(seq_size)[1] * mine
    halves = [
        jnp.concatenate(
            [
                part_query[:, g * group * HD : (g + 1) * group * HD],
                part_keyval[:, g * 2 * HD : (g + 1) * 2 * HD],
            ],
            axis=1,
        ).reshape(seq_size, mine, -1)
        for g in range(kv_local)
    ]
    sums, (tables, place_of) = scatter_sums(halves, "seq", seq_size, (tables, place_of))
    sums = [half.reshape(held, -1) for half in sums]
    my_query = [half[:, : group * HD].reshape(held * group, HD) for half in sums]
    my_keyval = [half[:, group * HD :].reshape(held * 2, HD) for half in sums]
    query = [part for half in my_query for part in gather_relative(half, "seq", seq_size)]

    smem = pl.BlockSpec(memory_space=pltpu.SMEM)
    vmem = pl.BlockSpec(memory_space=pltpu.VMEM)
    hbm = pl.BlockSpec(memory_space=pl.ANY)
    chunks = slots // CHUNK
    every_row = requests * heads_local
    block_rows = (mine + 1) * heads_local
    totals = pl.pallas_call(
        functools.partial(attention_kernel, ways),
        out_shape=[jax.ShapeDtypeStruct((seq_size // ways, block_rows, HD), jnp.bfloat16)] * ways,
        in_specs=[smem] + [vmem] * (2 * ways + 1) + [hbm, hbm],
        out_specs=[vmem] * ways,
        scratch_shapes=[
            pltpu.VMEM((every_row, HD), jnp.bfloat16),
            pltpu.VMEM((every_row, HD), jnp.bfloat16),
            pltpu.VMEM(key_cache.shape, jnp.bfloat16),
            pltpu.VMEM(value_cache.shape, jnp.bfloat16),
            pltpu.VMEM((chunks, LANES, PAGE), jnp.bfloat16),
            pltpu.VMEM((slots * heads_local, HD), jnp.float32),
            pltpu.VMEM((chunks, LANES), jnp.float32),
            pltpu.VMEM((chunks, LANES), jnp.float32),
            pltpu.VMEM((chunks, LANES), jnp.float32),
            pltpu.VMEM((every_row, HD), jnp.float32),
            pltpu.VMEM((every_row, HD), jnp.float32),
            pltpu.SemaphoreType.DMA((chunks,)),
            pltpu.SemaphoreType.DMA((chunks,)),
        ],
        compiler_params=pltpu.CompilerParams(vmem_limit_bytes=48 * 2**20),
        cost_estimate=pl.CostEstimate(
            flops=4 * slots * PAGE * wide,
            bytes_accessed=2 * (key_cache.size + value_cache.size),
            transcendentals=slots * PAGE * heads_local,
        ),
        name="paged_attention",
    )(place_of, *query, tables, key_cache, value_cache)

    for shift, size in lower_groups(seq_size):
        if shift:
            totals = [pick_digit(totals, "seq", shift, size, d) for d in range(size)]
        parts = [
            swap(part, "seq", seq_size, d << shift) if d else part for d, part in enumerate(totals)
        ]
        totals = pl.pallas_call(
            combine_kernel,
            out_shape=jax.ShapeDtypeStruct(parts[0].shape, jnp.bfloat16),
            in_specs=[vmem] * size,
            out_specs=vmem,
            compiler_params=pltpu.CompilerParams(vmem_limit_bytes=6 * 2**20),
            name="combine",
        )(*parts)
    shift, size = last_group(seq_size)
    parts = [totals] + [swap(totals, "seq", seq_size, d << shift) for d in range(1, size)]
    my_context = pl.pallas_call(
        finish_kernel,
        out_shape=jax.ShapeDtypeStruct((held * heads_local, HD), jnp.bfloat16),
        in_specs=[vmem] * (size + 4),
        out_specs=vmem,
        compiler_params=pltpu.CompilerParams(vmem_limit_bytes=6 * 2**20),
        name="finish",
    )(*parts, *my_query, *my_keyval).reshape(held, wide)
    context = gather_in_order(my_context, "seq", seq_size)

    total = jnp.dot(context, w_out, preferred_element_type=jnp.float32)
    step = 1
    while step < head_size:
        if step > 1:
            total = lax.reduce_precision(total, 8, 7)
            other = swap(total.astype(jnp.bfloat16), "head", head_size, step)
        else:
            other = swap(total, "head", head_size, step)
        total = total + other.astype(jnp.float32)
        step *= 2
    return total.astype(jnp.bfloat16)


def solution(mesh):
    seq_size, head_size = mesh.shape["seq"], mesh.shape["head"]

    def local(*args):
        return body(*args, seq_size=seq_size, head_size=head_size)

    return jax.shard_map(
        local,
        mesh=mesh,
        in_specs=(
            P(None, "seq"),
            P("seq", "head"),
            P("seq", "head"),
            P("head", "seq"),
            P("seq", None, "head"),
            P("seq", None, "head"),
            P("seq", "head"),
            P("seq", "head"),
            P(),
            P("seq"),
            P(),
        ),
        out_specs=P(None, "seq"),
        check_vma=False,
    )
```

```python
import functools
import math

import jax
import jax.numpy as jnp
from jax import lax
from jax.experimental import pallas as pl
from jax.experimental.pallas import tpu as pltpu
from jax.sharding import PartitionSpec as P

HD = 128
PAGE = 128
LANES = 128
CHUNK = 8
STAT = 16


masked_low = -1e30


def swap(x, axis, n, mask):
    return lax.ppermute(x, axis, [(j, j ^ mask) for j in range(n)])


def bit_groups(n):
    groups, shift = [], 0
    while (1 << shift) < n:
        size = min(4, n >> shift)
        groups.append((shift, size))
        shift += size.bit_length() - 1
    return groups


def lower_groups(n):
    return bit_groups(n)[:-1]


def last_group(n):
    return bit_groups(n)[-1]


def pick_digit(x, axis, shift, size, offset):
    digit = (lax.axis_index(axis) >> shift) % size
    x = x.reshape(x.shape[0] // size, size, *x.shape[1:])
    return lax.dynamic_index_in_dim(x, digit ^ offset, axis=1, keepdims=False)


def scatter_sum(parts, axis, n, beside):
    for shift, size in lower_groups(n):
        if shift:
            parts = [pick_digit(x, axis, shift, size, d) for d in range(size)]
        sent = [swap(parts[d], axis, n, d << shift) for d in range(1, size)]
        if shift == 0:
            sent, beside = lax.optimization_barrier((sent, beside))
        x = sum(sent, parts[0])
    shift, size = last_group(n)
    return sum([swap(x, axis, n, d << shift) for d in range(1, size)], x), beside


def gather_relative(x, axis, n):
    parts = [x]
    for shift, size in reversed(lower_groups(n)):
        x = jnp.concatenate(parts, axis=0) if len(parts) > 1 else parts[0]
        parts = [x] + [swap(x, axis, n, d << shift) for d in range(1, size)]
    return parts


def relative_place(block, axis, n):
    last_shift, last_size = last_group(n)
    offset = lax.axis_index(axis) ^ block
    place, weight = block >> last_shift, n
    for shift, size in lower_groups(n):
        weight //= size
        place = place + ((offset >> shift) & (size - 1)) * weight
    return place


def gathered_blocks(me, n):
    last_shift, last_size = last_group(n)
    offsets = [0]
    for shift, size in reversed(lower_groups(n)):
        offsets = [d << shift | e for d in range(size) for e in offsets]
    low = me & ((1 << last_shift) - 1)
    return [(c << last_shift) + (low ^ e) for e in offsets for c in range(last_size)]


def project_kernel(ways, me, hidden, w_query, w_keyval, *refs):
    outs, (query, keyval, result, sem) = refs[:ways], refs[ways:]
    tile = min(512, w_keyval.shape[1])
    jobs = [
        (ref, held, col, base + col)
        for ref, held, base in ((w_query, query, 0), (w_keyval, keyval, w_query.shape[1]))
        for col in range(0, ref.shape[1], tile)
    ]
    copies = [
        pltpu.make_async_copy(
            ref.at[:, pl.ds(col, tile)], held.at[:, pl.ds(col, tile)], sem.at[i]
        )
        for i, (ref, held, col, _) in enumerate(jobs)
    ]
    for copy in copies:
        copy.start()
    rows = hidden[...]
    for copy, (_, held, col, place) in zip(copies, jobs):
        copy.wait()
        result[:, place : place + tile] = jnp.dot(
            rows, held[:, col : col + tile], preferred_element_type=jnp.float32
        )
    digit = me[0] & (ways - 1)
    for d, out in enumerate(outs):
        blocks, mine, _ = out.shape
        for b in range(blocks):
            if mine % 8 == 0:
                first = (b * ways + (digit ^ d)) * mine
                out[b] = result[pl.ds(pl.multiple_of(first, mine), mine), :]
                continue
            chosen = result[b * ways * mine : (b * ways + 1) * mine, :]
            for j in range(1, ways):
                first = (b * ways + j) * mine
                chosen = jnp.where((digit ^ d) == j, result[first : first + mine, :], chosen)
            out[b] = chosen


def output_kernel(ways, seq_size, me, *refs):
    parts, (w_out, out) = refs[:ways], refs[ways:]
    rows = jnp.concatenate([part[...] for part in parts], axis=0)
    total = jnp.dot(rows, w_out[...], preferred_element_type=jnp.float32)
    blocks = gathered_blocks(me[0], seq_size)
    mine = rows.shape[0] // len(blocks)
    if mine % 8 == 0:
        for i, block in enumerate(blocks):
            here = pl.ds(pl.multiple_of(block * mine, mine), mine)
            out[here, :] = total[i * mine : (i + 1) * mine]
        return
    for place in range(len(blocks)):
        chosen = total[:mine]
        for i, block in enumerate(blocks):
            chosen = jnp.where(block == place, total[i * mine : (i + 1) * mine], chosen)
        out[place * mine : (place + 1) * mine, :] = chosen


def split_stat(stat, lane):
    hi = stat.astype(jnp.bfloat16).astype(jnp.float32)
    rest = stat - hi
    mid = rest.astype(jnp.bfloat16).astype(jnp.float32)
    piece = jnp.where(lane < STAT, hi, jnp.where(lane < 2 * STAT, mid, rest - mid))
    return piece.astype(jnp.bfloat16)


def join_stat(pieces):
    pieces = pieces.astype(jnp.float32)
    return (pieces + pltpu.roll(pieces, LANES - STAT, 1)) + pltpu.roll(
        pieces, LANES - 2 * STAT, 1
    )


def attention_kernel(ways, place_of, *refs):
    queries, refs = refs[:ways], refs[ways:]
    (tables, key_cache, value_cache), refs = refs[:3], refs[3:]
    outs, refs = refs[:ways], refs[ways:]
    (
        query_low,
        query_high,
        keys,
        values,
        probs,
        page_out,
        page_sum,
        page_max,
        dev_max,
        total_out,
        total_stat,
        key_sem,
        value_sem,
    ) = refs
    slots = key_cache.shape[0]
    heads = LANES // CHUNK
    group = heads // 2
    chunks = slots // CHUNK
    blocks, block_rows, _ = outs[0].shape
    mine = block_rows // heads - 1
    step_chunks = 4

    def key_copy(c):
        part = pl.ds(c * CHUNK, CHUNK)
        return pltpu.make_async_copy(key_cache.at[part], keys.at[part], key_sem.at[c])

    def value_copy(c):
        part = pl.ds(c * CHUNK, CHUNK)
        return pltpu.make_async_copy(value_cache.at[part], values.at[part], value_sem.at[c])

    for c in range(chunks + step_chunks):
        if c >= step_chunks:
            value_copy(c - step_chunks).start()
        if c < chunks:
            key_copy(c).start()

    for d, part in enumerate(queries):
        rows = part[...]
        low_head = lax.broadcasted_iota(jnp.int32, rows.shape, 0) % heads < group
        zero = jnp.zeros_like(rows)
        here = slice(rows.shape[0] * d, rows.shape[0] * (d + 1))
        query_low[here, :] = jnp.where(low_head, rows, zero)
        query_high[here, :] = jnp.where(low_head, zero, rows)
    total_out[...] = jnp.zeros_like(total_out)
    stat_lane = lax.broadcasted_iota(jnp.int32, total_stat.shape, 2) % STAT
    total_stat[...] = jnp.where(stat_lane < STAT // 2, masked_low, 0.0)

    def table(which, c):
        return tables[pl.ds(which * chunks + c, 1), :]

    lane_slot = lax.broadcasted_iota(jnp.int32, (PAGE, LANES), 1) // heads
    token = lax.broadcasted_iota(jnp.int32, (PAGE, LANES), 0).astype(jnp.float32)

    def score_chunk(c):
        places = [
            pl.multiple_of(((place_of[c * CHUNK + s] >> 16) & 0xFF) * heads, heads)
            for s in range(CHUNK)
        ]
        chosen = jnp.concatenate(
            [
                jnp.concatenate([ref[pl.ds(place, heads), :] for place in places], axis=0)
                for ref in (query_low, query_high)
            ],
            axis=1,
        )
        block = keys[pl.ds(c * CHUNK, CHUNK)].reshape(CHUNK * PAGE, 2 * HD)
        every = lax.dot_general(
            block, chosen, (((1,), (1,)), ((), ())), preferred_element_type=jnp.float32
        )
        score = every[:PAGE]
        for s in range(1, CHUNK):
            score = jnp.where(lane_slot == s, every[s * PAGE : (s + 1) * PAGE], score)
        score = jnp.where(token < table(1, c), score * table(0, c), masked_low)
        top = jnp.max(score, axis=0, keepdims=True)
        page_max[pl.ds(c, 1), :] = top
        prob = jnp.exp(score - top).astype(jnp.bfloat16).astype(jnp.float32)
        page_sum[pl.ds(c, 1), :] = jnp.sum(prob, axis=0, keepdims=True)
        probs[c] = prob.T.astype(jnp.bfloat16)

    empty = jnp.zeros((heads, PAGE), jnp.bfloat16)

    def value_chunk(c):
        prob = probs[c]
        for s in range(0, CHUNK, 2):
            pair = jnp.concatenate(
                [
                    jnp.concatenate([prob[s * heads : (s + 1) * heads], empty], axis=1),
                    jnp.concatenate([empty, prob[(s + 1) * heads : (s + 2) * heads]], axis=1),
                ],
                axis=0,
            )
            block = values[pl.ds(c * CHUNK + s, 2)].reshape(2 * PAGE, 2 * HD)
            both = jnp.dot(pair, block, preferred_element_type=jnp.float32)
            page_out[pl.ds(pl.multiple_of((c * CHUNK + s) * heads, heads), 2 * heads), :] = (
                jnp.concatenate(
                    [
                        both[:group, :HD],
                        both[group:heads, HD:],
                        both[heads : heads + group, :HD],
                        both[heads + group :, HD:],
                    ],
                    axis=0,
                )
            )

    for c in range(step_chunks):
        key_copy(c).wait()
        score_chunk(c)

    @pl.loop(1, chunks // step_chunks)
    def _(step):
        first = step * step_chunks
        for c in range(step_chunks):
            key_copy(first + c).wait()
            value_copy(first + c - step_chunks).wait()
        for c in range(step_chunks):
            value_chunk(first + c - step_chunks)
            score_chunk(first + c)

    for c in range(chunks - step_chunks, chunks):
        value_copy(c).wait()
    for c in range(chunks - step_chunks, chunks):
        value_chunk(c)

    biggest, who = page_max[...], tables[3 * chunks :, :]
    best = biggest
    for turn in range(CHUNK):
        other = pltpu.roll(biggest, turn * heads, 1) if turn else biggest
        other_who = pltpu.roll(who, turn * heads, 1) if turn else who
        for c in range(chunks):
            best = jnp.maximum(
                best, jnp.where(other_who[c : c + 1] == who, other[c : c + 1], masked_low)
            )
    dev_max[...] = best

    keep_max = lax.broadcasted_iota(jnp.int32, (heads, LANES), 1) % STAT < STAT // 2

    keep_max_row = lax.broadcasted_iota(jnp.int32, (PAGE, LANES), 0) % STAT < STAT // 2

    @pl.loop(0, chunks // step_chunks)
    def _(step):
        for c in [step * step_chunks + c for c in range(step_chunks)]:
            top = dev_max[pl.ds(c, 1), :]
            weight = jnp.exp(page_max[pl.ds(c, 1), :] - top)
            out_weight = jnp.broadcast_to(weight * table(2, c), (PAGE, LANES)).T
            stat = jnp.where(keep_max_row, top, weight * page_sum[pl.ds(c, 1), :]).T
            for s in range(CHUNK):
                here = pl.ds(
                    pl.multiple_of((place_of[c * CHUNK + s] & 0xFFFF) * heads, heads), heads
                )
                there = pl.ds(pl.multiple_of((c * CHUNK + s) * heads, heads), heads)
                part = slice(s * heads, (s + 1) * heads)
                turn = s % 2
                total_out[turn, here, :] += page_out[there, :] * out_weight[part]
                total_stat[turn, here, :] = jnp.where(
                    keep_max, stat[part], total_stat[turn, here, :] + stat[part]
                )

    lane = lax.broadcasted_iota(jnp.int32, (heads, LANES), 1)
    digit = place_of[0] >> 24
    for d, out in enumerate(outs):
        for b in range(blocks):
            first = (b * ways + (digit ^ d)) * (mine * heads)
            rows = pl.ds(pl.multiple_of(first, mine * heads), mine * heads)
            out[b, : mine * heads, :] = (total_out[0, rows, :] + total_out[1, rows, :]).astype(
                jnp.bfloat16
            )
            even, odd = total_stat[0, rows, :], total_stat[1, rows, :]
            is_max = lax.broadcasted_iota(jnp.int32, even.shape, 1) % STAT < STAT // 2
            both = jnp.where(is_max, jnp.maximum(even, odd), even + odd)
            stat = jnp.zeros((heads, LANES), jnp.float32)
            for r in range(mine):
                stat = jnp.where(
                    lane % (STAT // 2) == r, both[r * heads : (r + 1) * heads], stat
                )
            out[b, mine * heads :, :] = split_stat(stat, lane)


def combine_kernel(*refs):
    *parts, out = refs
    blocks, block_rows, _ = out.shape
    heads = LANES // CHUNK
    mine = block_rows // heads - 1
    lane = lax.broadcasted_iota(jnp.int32, (heads, LANES), 1)
    for b in range(blocks):
        stats = [join_stat(part[b, mine * heads :, :]) for part in parts]
        maxima = [jnp.where(lane < mine, stat, 0.0) for stat in stats]
        top = functools.reduce(jnp.maximum, maxima)
        factors = [jnp.exp(m - top) for m in maxima]
        sums = sum(
            pltpu.roll(f, STAT // 2, 1) * jnp.where(lane < STAT, stat, 0.0)
            for f, stat in zip(factors, stats)
        )
        both = jnp.where(lane < STAT // 2, top, sums)
        both = jnp.where(lane < STAT, both, 0.0)
        both = (both + pltpu.roll(both, STAT, 1)) + pltpu.roll(both, 2 * STAT, 1)
        out[b, mine * heads :, :] = split_stat(both, lane)
        for r in range(mine):
            rows = slice(r * heads, (r + 1) * heads)
            numer = sum(
                f[:, r : r + 1] * part[b, rows, :].astype(jnp.float32)
                for f, part in zip(factors, parts)
            )
            out[b, rows, :] = numer.astype(jnp.bfloat16)


def finish_kernel(*refs):
    *parts, query, keyval, out, numers = refs
    blocks, block_rows, _ = parts[0].shape
    heads = LANES // CHUNK
    group = heads // 2
    mine = block_rows // heads - 1
    lane = lax.broadcasted_iota(jnp.int32, (heads, LANES), 1)
    low_head = lax.broadcasted_iota(jnp.int32, (heads, LANES), 0) < group
    new = keyval[...].astype(jnp.float32)

    def spread(r, which):
        low = jnp.broadcast_to(new[4 * r + which : 4 * r + which + 1], (heads, LANES))
        high = jnp.broadcast_to(new[4 * r + 2 + which : 4 * r + 3 + which], (heads, LANES))
        return jnp.where(low_head, low, high)

    for b in range(blocks):
        own = jnp.zeros((heads, LANES), jnp.float32)
        for r in range(mine):
            request = b * mine + r
            rows = query[request * heads : (request + 1) * heads, :].astype(jnp.float32)
            dot = jnp.sum(rows * spread(request, 0), axis=1, keepdims=True)
            own = jnp.where(lane == r, dot * (1.0 / math.sqrt(HD)), own)
        maxima, sums = [], []
        for part in parts:
            whole = join_stat(part[b, mine * heads :, :])
            maxima.append(jnp.where(lane < mine, whole, 0.0))
            sums.append(jnp.where(lane < mine, pltpu.roll(whole, LANES - STAT // 2, 1), 0.0))
        top = functools.reduce(jnp.maximum, maxima, own)
        fresh = jnp.exp(own - top)
        factors = [jnp.exp(m - top) for m in maxima]
        denom = sum((s * f for s, f in zip(sums, factors)), fresh)
        fresh = fresh / denom
        factors = [f / denom for f in factors]
        for r in range(mine):
            numer = fresh[:, r : r + 1] * spread(b * mine + r, 1)
            for part, f in zip(parts, factors):
                rows = part[b, r * heads : (r + 1) * heads, :].astype(jnp.float32)
                numer = numer + f[:, r : r + 1] * rows
            request = b * mine + r
            numers[request * heads : (request + 1) * heads, :] = numer
    for h in range(heads):
        out[:, h * HD : (h + 1) * HD] = numers[
            pl.ds(h, blocks * mine, stride=heads), :
        ].astype(jnp.bfloat16)


def body(
    hidden_in,
    w_query,
    w_keyval,
    w_out,
    key_cache,
    value_cache,
    key_scale,
    value_scale,
    page_counts,
    slot_pages,
    trim,
    seq_size,
    head_size,
):
    requests = hidden_in.shape[0]
    slots = key_cache.shape[0]
    kv_local = w_keyval.shape[1] // (2 * HD)
    heads_local = w_query.shape[1] // HD
    wide = heads_local * HD
    group = heads_local // kv_local
    assert kv_local == 2 and heads_local * CHUNK == LANES
    assert slots % CHUNK == 0
    mine = requests // seq_size
    inverse_square_root = 1.0 / math.sqrt(HD)

    start = jnp.cumsum(page_counts) - page_counts
    ends = start + page_counts
    owner = jnp.sum((ends[None, :] <= slot_pages[:, None]).astype(jnp.int32), axis=1)
    selector = owner[:, None] == jnp.arange(requests, dtype=jnp.int32)[None, :]
    select_int = selector.astype(jnp.int32)
    index = slot_pages - jnp.sum(select_int * start[None, :], axis=1)
    lengths = PAGE * page_counts - trim
    page_valid = jnp.sum(select_int * lengths[None, :], axis=1) - index * PAGE
    block = owner // mine
    row_of = relative_place(block, "seq", seq_size) * mine + owner - block * mine

    def on_lanes(x):
        return jnp.broadcast_to(x, (slots, heads_local)).reshape(slots // CHUNK, LANES)

    def per_head(x):
        return on_lanes(jnp.repeat(x, heads_local // kv_local, axis=1))

    tables = jnp.concatenate(
        [
            per_head(key_scale * inverse_square_root),
            on_lanes(page_valid[:, None].astype(jnp.float32)),
            per_head(value_scale),
            on_lanes(owner[:, None].astype(jnp.float32)),
        ],
        axis=0,
    )
    ways = lower_groups(seq_size)[0][1]
    digit = lax.axis_index("seq") & (ways - 1)
    place_of = (digit << 24) + row_of * 65536 + owner

    held = last_group(seq_size)[1] * mine
    columns = w_query.shape[1] + w_keyval.shape[1]
    smem = pl.BlockSpec(memory_space=pltpu.SMEM)
    vmem = pl.BlockSpec(memory_space=pltpu.VMEM)
    hbm = pl.BlockSpec(memory_space=pltpu.HBM)
    me = lax.axis_index("seq").reshape(1)
    part_shape = jax.ShapeDtypeStruct((seq_size // ways, mine, columns), jnp.float32)
    parts = pl.pallas_call(
        functools.partial(project_kernel, ways),
        out_shape=[part_shape] * ways,
        in_specs=[smem, vmem, hbm, hbm],
        out_specs=[vmem] * ways,
        scratch_shapes=[
            pltpu.VMEM(w_query.shape, jnp.bfloat16),
            pltpu.VMEM(w_keyval.shape, jnp.bfloat16),
            pltpu.VMEM((requests, columns), jnp.float32),
            pltpu.SemaphoreType.DMA((columns // min(512, w_keyval.shape[1]),)),
        ],
        compiler_params=pltpu.CompilerParams(vmem_limit_bytes=53 * 2**20),
        name="project",
    )(me, hidden_in, w_query, w_keyval)
    sums, (tables, place_of) = scatter_sum(parts, "seq", seq_size, (tables, place_of))
    sums = sums.astype(jnp.bfloat16).reshape(held, columns)
    my_query = sums[:, :wide].reshape(held * heads_local, HD)
    my_keyval = sums[:, wide:].reshape(held * 2 * kv_local, HD)
    query = gather_relative(my_query, "seq", seq_size)
    query, my_keyval = lax.optimization_barrier((query, my_keyval))

    chunks = slots // CHUNK
    every_row = requests * heads_local
    block_rows = (mine + 1) * heads_local
    totals = pl.pallas_call(
        functools.partial(attention_kernel, ways),
        out_shape=[jax.ShapeDtypeStruct((seq_size // ways, block_rows, HD), jnp.bfloat16)] * ways,
        in_specs=[smem] + [vmem] * (ways + 1) + [hbm, hbm],
        out_specs=[vmem] * ways,
        scratch_shapes=[
            pltpu.VMEM((every_row, HD), jnp.bfloat16),
            pltpu.VMEM((every_row, HD), jnp.bfloat16),
            pltpu.VMEM(key_cache.shape, jnp.bfloat16),
            pltpu.VMEM(value_cache.shape, jnp.bfloat16),
            pltpu.VMEM((chunks, LANES, PAGE), jnp.bfloat16),
            pltpu.VMEM((slots * heads_local, HD), jnp.float32),
            pltpu.VMEM((chunks, LANES), jnp.float32),
            pltpu.VMEM((chunks, LANES), jnp.float32),
            pltpu.VMEM((chunks, LANES), jnp.float32),
            pltpu.VMEM((2, every_row, HD), jnp.float32),
            pltpu.VMEM((2, every_row, HD), jnp.float32),
            pltpu.SemaphoreType.DMA((chunks,)),
            pltpu.SemaphoreType.DMA((chunks,)),
        ],
        compiler_params=pltpu.CompilerParams(vmem_limit_bytes=48 * 2**20),
        cost_estimate=pl.CostEstimate(
            flops=4 * slots * PAGE * wide,
            bytes_accessed=2 * (key_cache.size + value_cache.size),
            transcendentals=slots * PAGE * heads_local,
        ),
        name="paged_attention",
    )(place_of, *query, tables, key_cache, value_cache)

    for shift, size in lower_groups(seq_size):
        if shift:
            totals = [pick_digit(totals, "seq", shift, size, d) for d in range(size)]
        parts = [
            swap(part, "seq", seq_size, d << shift) if d else part for d, part in enumerate(totals)
        ]
        totals = pl.pallas_call(
            combine_kernel,
            out_shape=jax.ShapeDtypeStruct(parts[0].shape, jnp.bfloat16),
            in_specs=[vmem] * size,
            out_specs=vmem,
            compiler_params=pltpu.CompilerParams(vmem_limit_bytes=6 * 2**20),
            name="combine",
        )(*parts)
    shift, size = last_group(seq_size)
    parts = [totals] + [swap(totals, "seq", seq_size, d << shift) for d in range(1, size)]
    my_context = pl.pallas_call(
        finish_kernel,
        out_shape=jax.ShapeDtypeStruct((held, wide), jnp.bfloat16),
        in_specs=[vmem] * (size + 2),
        out_specs=vmem,
        scratch_shapes=[pltpu.VMEM((held * heads_local, HD), jnp.float32)],
        compiler_params=pltpu.CompilerParams(vmem_limit_bytes=6 * 2**20),
        name="finish",
    )(*parts, my_query, my_keyval)

    total = pl.pallas_call(
        functools.partial(output_kernel, ways, seq_size),
        out_shape=jax.ShapeDtypeStruct((requests, w_out.shape[1]), jnp.float32),
        in_specs=[smem] + [vmem] * (ways + 1),
        out_specs=vmem,
        compiler_params=pltpu.CompilerParams(vmem_limit_bytes=16 * 2**20),
        name="project_out",
    )(me, *gather_relative(my_context, "seq", seq_size), w_out)
    step = 1
    while step < head_size:
        if step > 1:
            total = lax.reduce_precision(total, 8, 7)
            other = swap(total.astype(jnp.bfloat16), "head", head_size, step)
        else:
            other = swap(total, "head", head_size, step)
        total = total + other.astype(jnp.float32)
        step *= 2
    return total.astype(jnp.bfloat16)


def solution(mesh):
    seq_size, head_size = mesh.shape["seq"], mesh.shape["head"]

    def local(*args):
        return body(*args, seq_size=seq_size, head_size=head_size)

    return jax.shard_map(
        local,
        mesh=mesh,
        in_specs=(
            P(None, "seq"),
            P("seq", "head"),
            P("seq", "head"),
            P("head", "seq"),
            P("seq", None, "head"),
            P("seq", None, "head"),
            P("seq", "head"),
            P("seq", "head"),
            P(),
            P("seq"),
            P(),
        ),
        out_specs=P(None, "seq"),
        check_vma=False,
    )
```

```python
import functools
import math

import jax
import jax.numpy as jnp
from jax import lax
from jax.experimental import pallas as pl
from jax.experimental.pallas import tpu as pltpu
from jax.sharding import PartitionSpec as P

HD = 128
PAGE = 128
LANES = 128
CHUNK = 8
STAT = 16


masked_low = -1e30


def swap(x, axis, n, mask):
    return lax.ppermute(x, axis, [(j, j ^ mask) for j in range(n)])


def bit_groups(n):
    groups, shift = [], 0
    while (1 << shift) < n:
        size = min(4, n >> shift)
        groups.append((shift, size))
        shift += size.bit_length() - 1
    return groups


def lower_groups(n):
    return bit_groups(n)[:-1]


def last_group(n):
    return bit_groups(n)[-1]


def pick_digit(x, axis, shift, size, offset):
    digit = (lax.axis_index(axis) >> shift) % size
    x = x.reshape(x.shape[0] // size, size, *x.shape[1:])
    return lax.dynamic_index_in_dim(x, digit ^ offset, axis=1, keepdims=False)


def scatter_terms(parts, axis, n, beside):
    for shift, size in lower_groups(n):
        if shift:
            parts = [pick_digit(x, axis, shift, size, d) for d in range(size)]
        sent = [swap(parts[d], axis, n, d << shift) for d in range(1, size)]
        if shift == 0:
            sent, beside = lax.optimization_barrier((sent, beside))
        x = sum(sent, parts[0])
    shift, size = last_group(n)
    return [x] + [swap(x, axis, n, d << shift) for d in range(1, size)], beside


def gather_relative(x, axis, n):
    parts = [x]
    for shift, size in reversed(lower_groups(n)):
        x = jnp.concatenate(parts, axis=0) if len(parts) > 1 else parts[0]
        parts = [x] + [swap(x, axis, n, d << shift) for d in range(1, size)]
    return parts


def relative_place(block, axis, n):
    last_shift, last_size = last_group(n)
    offset = lax.axis_index(axis) ^ block
    place, weight = block >> last_shift, n
    for shift, size in lower_groups(n):
        weight //= size
        place = place + ((offset >> shift) & (size - 1)) * weight
    return place


def gathered_blocks(me, n):
    last_shift, last_size = last_group(n)
    offsets = [0]
    for shift, size in reversed(lower_groups(n)):
        offsets = [d << shift | e for d in range(size) for e in offsets]
    low = me & ((1 << last_shift) - 1)
    return [(c << last_shift) + (low ^ e) for e in offsets for c in range(last_size)]


def project_kernel(ways, me, hidden, w_query, w_keyval, *refs):
    outs, (query, keyval, result, sem) = refs[:ways], refs[ways:]
    depth = w_query.shape[0]
    tile = min(256, depth)
    wide = w_query.shape[1]
    copies = [
        [
            pltpu.make_async_copy(
                ref.at[pl.ds(row, tile)], held.at[pl.ds(row, tile)], sem.at[which, row // tile]
            )
            for which, (ref, held) in enumerate(((w_query, query), (w_keyval, keyval)))
        ]
        for row in range(0, depth, tile)
    ]
    for pair in copies:
        for copy in pair:
            copy.start()
    for row, pair in zip(range(0, depth, tile), copies):
        here = slice(row, row + tile)
        rows = hidden[:, here]
        for copy, held, place in zip(pair, (query, keyval), (slice(0, wide), slice(wide, None))):
            copy.wait()
            part = jnp.dot(rows, held[here, :], preferred_element_type=jnp.float32)
            result[:, place] = result[:, place] + part if row else part
    digit = me[0] & (ways - 1)
    for d, out in enumerate(outs):
        blocks, mine, _ = out.shape
        for b in range(blocks):
            if mine % 8 == 0:
                first = (b * ways + (digit ^ d)) * mine
                out[b] = result[pl.ds(pl.multiple_of(first, mine), mine), :]
                continue
            chosen = result[b * ways * mine : (b * ways + 1) * mine, :]
            for j in range(1, ways):
                first = (b * ways + j) * mine
                chosen = jnp.where((digit ^ d) == j, result[first : first + mine, :], chosen)
            out[b] = chosen


def output_kernel(ways, seq_size, me, *refs):
    parts, (w_out, out) = refs[:ways], refs[ways:]
    rows = jnp.concatenate([part[...] for part in parts], axis=0)
    total = jnp.dot(rows, w_out[...], preferred_element_type=jnp.float32)
    blocks = gathered_blocks(me[0], seq_size)
    mine = rows.shape[0] // len(blocks)
    if mine % 8 == 0:
        for i, block in enumerate(blocks):
            here = pl.ds(pl.multiple_of(block * mine, mine), mine)
            out[here, :] = total[i * mine : (i + 1) * mine]
        return
    for place in range(len(blocks)):
        chosen = total[:mine]
        for i, block in enumerate(blocks):
            chosen = jnp.where(block == place, total[i * mine : (i + 1) * mine], chosen)
        out[place * mine : (place + 1) * mine, :] = chosen


def join_kernel(*refs):
    *parts, query, keyval, query_rows, keyval_rows = refs
    blocks, mine, columns = parts[0].shape
    held = blocks * mine
    whole = functools.reduce(jnp.add, [part[...] for part in parts]).reshape(held, columns)
    heads = query.shape[0] // held
    others = keyval.shape[0] // held
    for h in range(heads):
        query_rows[pl.ds(h, held, stride=heads), :] = whole[:, h * HD : (h + 1) * HD]
    for h in range(others):
        place = (heads + h) * HD
        keyval_rows[pl.ds(h, held, stride=others), :] = whole[:, place : place + HD]
    query[...] = query_rows[...].astype(jnp.bfloat16)
    keyval[...] = keyval_rows[...].astype(jnp.bfloat16)


def split_stat(stat, lane):
    hi = stat.astype(jnp.bfloat16).astype(jnp.float32)
    rest = stat - hi
    mid = rest.astype(jnp.bfloat16).astype(jnp.float32)
    piece = jnp.where(lane < STAT, hi, jnp.where(lane < 2 * STAT, mid, rest - mid))
    return piece.astype(jnp.bfloat16)


def join_stat(pieces):
    pieces = pieces.astype(jnp.float32)
    return (pieces + pltpu.roll(pieces, LANES - STAT, 1)) + pltpu.roll(
        pieces, LANES - 2 * STAT, 1
    )


def attention_kernel(ways, place_of, *refs):
    queries, refs = refs[:ways], refs[ways:]
    (tables, keys, values), refs = refs[:3], refs[3:]
    outs, refs = refs[:ways], refs[ways:]
    (
        query_low,
        query_high,
        probs,
        page_out,
        page_sum,
        page_max,
        dev_max,
        total_out,
        total_stat,
    ) = refs
    slots = keys.shape[0]
    heads = LANES // CHUNK
    group = heads // 2
    chunks = slots // CHUNK
    blocks, block_rows, _ = outs[0].shape
    mine = block_rows // heads - 1
    step_chunks = 4

    for d, part in enumerate(queries):
        rows = part[...]
        low_head = lax.broadcasted_iota(jnp.int32, rows.shape, 0) % heads < group
        zero = jnp.zeros_like(rows)
        here = slice(rows.shape[0] * d, rows.shape[0] * (d + 1))
        query_low[here, :] = jnp.where(low_head, rows, zero)
        query_high[here, :] = jnp.where(low_head, zero, rows)
    total_out[...] = jnp.zeros_like(total_out)
    stat_lane = lax.broadcasted_iota(jnp.int32, total_stat.shape, 2) % STAT
    total_stat[...] = jnp.where(stat_lane < STAT // 2, masked_low, 0.0)

    def table(which, c):
        return tables[pl.ds(which * chunks + c, 1), :]

    lane_slot = lax.broadcasted_iota(jnp.int32, (PAGE, LANES), 1) // heads
    token = lax.broadcasted_iota(jnp.int32, (PAGE, LANES), 0).astype(jnp.float32)

    def score_chunk(c):
        places = [
            pl.multiple_of(((place_of[c * CHUNK + s] >> 16) & 0xFF) * heads, heads)
            for s in range(CHUNK)
        ]
        chosen = jnp.concatenate(
            [
                jnp.concatenate([ref[pl.ds(place, heads), :] for place in places], axis=0)
                for ref in (query_low, query_high)
            ],
            axis=1,
        )
        block = keys[pl.ds(c * CHUNK, CHUNK)].reshape(CHUNK * PAGE, 2 * HD)
        every = lax.dot_general(
            block, chosen, (((1,), (1,)), ((), ())), preferred_element_type=jnp.float32
        )
        score = every[:PAGE]
        for s in range(1, CHUNK):
            score = jnp.where(lane_slot == s, every[s * PAGE : (s + 1) * PAGE], score)
        score = jnp.where(token < table(1, c), score * table(0, c), masked_low)
        top = jnp.max(score, axis=0, keepdims=True)
        page_max[pl.ds(c, 1), :] = top
        prob = jnp.exp(score - top).astype(jnp.bfloat16).astype(jnp.float32)
        page_sum[pl.ds(c, 1), :] = jnp.sum(prob, axis=0, keepdims=True)
        probs[c] = prob.T.astype(jnp.bfloat16)

    empty = jnp.zeros((heads, PAGE), jnp.bfloat16)

    def value_chunk(c):
        prob = probs[c]
        for s in range(0, CHUNK, 2):
            pair = jnp.concatenate(
                [
                    jnp.concatenate([prob[s * heads : (s + 1) * heads], empty], axis=1),
                    jnp.concatenate([empty, prob[(s + 1) * heads : (s + 2) * heads]], axis=1),
                ],
                axis=0,
            )
            block = values[pl.ds(c * CHUNK + s, 2)].reshape(2 * PAGE, 2 * HD)
            both = jnp.dot(pair, block, preferred_element_type=jnp.float32)
            page_out[pl.ds(pl.multiple_of((c * CHUNK + s) * heads, heads), 2 * heads), :] = (
                jnp.concatenate(
                    [
                        both[:group, :HD],
                        both[group:heads, HD:],
                        both[heads : heads + group, :HD],
                        both[heads + group :, HD:],
                    ],
                    axis=0,
                )
            )

    for c in range(step_chunks):
        score_chunk(c)

    @pl.loop(1, chunks // step_chunks)
    def _(step):
        first = step * step_chunks
        for c in range(step_chunks):
            value_chunk(first + c - step_chunks)
            score_chunk(first + c)

    for c in range(chunks - step_chunks, chunks):
        value_chunk(c)

    biggest, who = page_max[...], tables[3 * chunks :, :]
    best = biggest
    for turn in range(CHUNK):
        other = pltpu.roll(biggest, turn * heads, 1) if turn else biggest
        other_who = pltpu.roll(who, turn * heads, 1) if turn else who
        for c in range(chunks):
            best = jnp.maximum(
                best, jnp.where(other_who[c : c + 1] == who, other[c : c + 1], masked_low)
            )
    dev_max[...] = best

    keep_max = lax.broadcasted_iota(jnp.int32, (heads, LANES), 1) % STAT < STAT // 2

    keep_max_row = lax.broadcasted_iota(jnp.int32, (PAGE, LANES), 0) % STAT < STAT // 2

    @pl.loop(0, chunks // step_chunks)
    def _(step):
        for c in [step * step_chunks + c for c in range(step_chunks)]:
            top = dev_max[pl.ds(c, 1), :]
            weight = jnp.exp(page_max[pl.ds(c, 1), :] - top)
            out_weight = jnp.broadcast_to(weight * table(2, c), (PAGE, LANES)).T
            stat = jnp.where(keep_max_row, top, weight * page_sum[pl.ds(c, 1), :]).T
            for s in range(CHUNK):
                here = pl.ds(
                    pl.multiple_of((place_of[c * CHUNK + s] & 0xFFFF) * heads, heads), heads
                )
                there = pl.ds(pl.multiple_of((c * CHUNK + s) * heads, heads), heads)
                part = slice(s * heads, (s + 1) * heads)
                turn = s % 2
                total_out[turn, here, :] += page_out[there, :] * out_weight[part]
                total_stat[turn, here, :] = jnp.where(
                    keep_max, stat[part], total_stat[turn, here, :] + stat[part]
                )

    lane = lax.broadcasted_iota(jnp.int32, (heads, LANES), 1)
    digit = place_of[0] >> 24
    for d, out in enumerate(outs):
        for b in range(blocks):
            first = (b * ways + (digit ^ d)) * (mine * heads)
            rows = pl.ds(pl.multiple_of(first, mine * heads), mine * heads)
            out[b, : mine * heads, :] = (total_out[0, rows, :] + total_out[1, rows, :]).astype(
                jnp.bfloat16
            )
            even, odd = total_stat[0, rows, :], total_stat[1, rows, :]
            is_max = lax.broadcasted_iota(jnp.int32, even.shape, 1) % STAT < STAT // 2
            both = jnp.where(is_max, jnp.maximum(even, odd), even + odd)
            stat = jnp.zeros((heads, LANES), jnp.float32)
            for r in range(mine):
                stat = jnp.where(
                    lane % (STAT // 2) == r, both[r * heads : (r + 1) * heads], stat
                )
            out[b, mine * heads :, :] = split_stat(stat, lane)


def combine_kernel(*refs):
    *parts, out = refs
    blocks, block_rows, _ = out.shape
    heads = LANES // CHUNK
    mine = block_rows // heads - 1
    lane = lax.broadcasted_iota(jnp.int32, (heads, LANES), 1)
    for b in range(blocks):
        stats = [join_stat(part[b, mine * heads :, :]) for part in parts]
        maxima = [jnp.where(lane < mine, stat, 0.0) for stat in stats]
        top = functools.reduce(jnp.maximum, maxima)
        factors = [jnp.exp(m - top) for m in maxima]
        sums = sum(
            pltpu.roll(f, STAT // 2, 1) * jnp.where(lane < STAT, stat, 0.0)
            for f, stat in zip(factors, stats)
        )
        both = jnp.where(lane < STAT // 2, top, sums)
        both = jnp.where(lane < STAT, both, 0.0)
        both = (both + pltpu.roll(both, STAT, 1)) + pltpu.roll(both, 2 * STAT, 1)
        out[b, mine * heads :, :] = split_stat(both, lane)
        for r in range(mine):
            rows = slice(r * heads, (r + 1) * heads)
            numer = sum(
                f[:, r : r + 1] * part[b, rows, :].astype(jnp.float32)
                for f, part in zip(factors, parts)
            )
            out[b, rows, :] = numer.astype(jnp.bfloat16)


def finish_kernel(*refs):
    *parts, query, keyval, out, numers = refs
    blocks, block_rows, _ = parts[0].shape
    heads = LANES // CHUNK
    group = heads // 2
    mine = block_rows // heads - 1
    lane = lax.broadcasted_iota(jnp.int32, (heads, LANES), 1)
    low_head = lax.broadcasted_iota(jnp.int32, (heads, LANES), 0) < group
    new = keyval[...].astype(jnp.float32)

    def spread(r, which):
        low = jnp.broadcast_to(new[4 * r + which : 4 * r + which + 1], (heads, LANES))
        high = jnp.broadcast_to(new[4 * r + 2 + which : 4 * r + 3 + which], (heads, LANES))
        return jnp.where(low_head, low, high)

    for b in range(blocks):
        own = jnp.zeros((heads, LANES), jnp.float32)
        for r in range(mine):
            request = b * mine + r
            rows = query[request * heads : (request + 1) * heads, :].astype(jnp.float32)
            dot = jnp.sum(rows * spread(request, 0), axis=1, keepdims=True)
            own = jnp.where(lane == r, dot * (1.0 / math.sqrt(HD)), own)
        maxima, sums = [], []
        for part in parts:
            whole = join_stat(part[b, mine * heads :, :])
            maxima.append(jnp.where(lane < mine, whole, 0.0))
            sums.append(jnp.where(lane < mine, pltpu.roll(whole, LANES - STAT // 2, 1), 0.0))
        top = functools.reduce(jnp.maximum, maxima, own)
        fresh = jnp.exp(own - top)
        factors = [jnp.exp(m - top) for m in maxima]
        denom = sum((s * f for s, f in zip(sums, factors)), fresh)
        fresh = fresh / denom
        factors = [f / denom for f in factors]
        for r in range(mine):
            numer = fresh[:, r : r + 1] * spread(b * mine + r, 1)
            for part, f in zip(parts, factors):
                rows = part[b, r * heads : (r + 1) * heads, :].astype(jnp.float32)
                numer = numer + f[:, r : r + 1] * rows
            request = b * mine + r
            numers[request * heads : (request + 1) * heads, :] = numer
    for h in range(heads):
        out[:, h * HD : (h + 1) * HD] = numers[
            pl.ds(h, blocks * mine, stride=heads), :
        ].astype(jnp.bfloat16)


def body(
    hidden_in,
    w_query,
    w_keyval,
    w_out,
    key_cache,
    value_cache,
    key_scale,
    value_scale,
    page_counts,
    slot_pages,
    trim,
    seq_size,
    head_size,
):
    requests = hidden_in.shape[0]
    slots = key_cache.shape[0]
    kv_local = w_keyval.shape[1] // (2 * HD)
    heads_local = w_query.shape[1] // HD
    wide = heads_local * HD
    group = heads_local // kv_local
    assert kv_local == 2 and heads_local * CHUNK == LANES
    assert slots % CHUNK == 0
    mine = requests // seq_size
    inverse_square_root = 1.0 / math.sqrt(HD)

    start = jnp.cumsum(page_counts) - page_counts
    ends = start + page_counts
    owner = jnp.sum((ends[None, :] <= slot_pages[:, None]).astype(jnp.int32), axis=1)
    selector = owner[:, None] == jnp.arange(requests, dtype=jnp.int32)[None, :]
    select_int = selector.astype(jnp.int32)
    index = slot_pages - jnp.sum(select_int * start[None, :], axis=1)
    lengths = PAGE * page_counts - trim
    page_valid = jnp.sum(select_int * lengths[None, :], axis=1) - index * PAGE
    block = owner // mine
    row_of = relative_place(block, "seq", seq_size) * mine + owner - block * mine

    def on_lanes(x):
        return jnp.broadcast_to(x, (slots, heads_local)).reshape(slots // CHUNK, LANES)

    def per_head(x):
        return on_lanes(jnp.repeat(x, heads_local // kv_local, axis=1))

    tables = jnp.concatenate(
        [
            per_head(key_scale * inverse_square_root),
            on_lanes(page_valid[:, None].astype(jnp.float32)),
            per_head(value_scale),
            on_lanes(owner[:, None].astype(jnp.float32)),
        ],
        axis=0,
    )
    ways = lower_groups(seq_size)[0][1]
    digit = lax.axis_index("seq") & (ways - 1)
    place_of = (digit << 24) + row_of * 65536 + owner

    held = last_group(seq_size)[1] * mine
    columns = w_query.shape[1] + w_keyval.shape[1]
    smem = pl.BlockSpec(memory_space=pltpu.SMEM)
    vmem = pl.BlockSpec(memory_space=pltpu.VMEM)
    hbm = pl.BlockSpec(memory_space=pltpu.HBM)
    me = lax.axis_index("seq").reshape(1)
    part_shape = jax.ShapeDtypeStruct((seq_size // ways, mine, columns), jnp.float32)
    parts = pl.pallas_call(
        functools.partial(project_kernel, ways),
        out_shape=[part_shape] * ways,
        in_specs=[smem, vmem, hbm, hbm],
        out_specs=[vmem] * ways,
        scratch_shapes=[
            pltpu.VMEM(w_query.shape, jnp.bfloat16),
            pltpu.VMEM(w_keyval.shape, jnp.bfloat16),
            pltpu.VMEM((requests, columns), jnp.float32),
            pltpu.SemaphoreType.DMA((2, pl.cdiv(w_query.shape[0], 256))),
        ],
        compiler_params=pltpu.CompilerParams(vmem_limit_bytes=53 * 2**20),
        name="project",
    )(me, hidden_in, w_query, w_keyval)
    terms, (tables, place_of) = scatter_terms(parts, "seq", seq_size, (tables, place_of))
    row_shapes = [(held * heads_local, HD), (held * 2 * kv_local, HD)]
    my_query, my_keyval = pl.pallas_call(
        join_kernel,
        out_shape=[jax.ShapeDtypeStruct(shape, jnp.bfloat16) for shape in row_shapes],
        in_specs=[vmem] * len(terms),
        out_specs=[vmem] * 2,
        scratch_shapes=[pltpu.VMEM(shape, jnp.float32) for shape in row_shapes],
        compiler_params=pltpu.CompilerParams(vmem_limit_bytes=6 * 2**20),
        cost_estimate=pl.CostEstimate(
            flops=10**10,
            bytes_accessed=10**7,
            transcendentals=0,
        ),
        name="join",
    )(*terms)
    query = gather_relative(my_query, "seq", seq_size)

    chunks = slots // CHUNK
    every_row = requests * heads_local
    block_rows = (mine + 1) * heads_local
    totals = pl.pallas_call(
        functools.partial(attention_kernel, ways),
        out_shape=[jax.ShapeDtypeStruct((seq_size // ways, block_rows, HD), jnp.bfloat16)] * ways,
        in_specs=[smem] + [vmem] * (ways + 3),
        out_specs=[vmem] * ways,
        scratch_shapes=[
            pltpu.VMEM((every_row, HD), jnp.bfloat16),
            pltpu.VMEM((every_row, HD), jnp.bfloat16),
            pltpu.VMEM((chunks, LANES, PAGE), jnp.bfloat16),
            pltpu.VMEM((slots * heads_local, HD), jnp.float32),
            pltpu.VMEM((chunks, LANES), jnp.float32),
            pltpu.VMEM((chunks, LANES), jnp.float32),
            pltpu.VMEM((chunks, LANES), jnp.float32),
            pltpu.VMEM((2, every_row, HD), jnp.float32),
            pltpu.VMEM((2, every_row, HD), jnp.float32),
        ],
        compiler_params=pltpu.CompilerParams(vmem_limit_bytes=24 * 2**20),
        cost_estimate=pl.CostEstimate(
            flops=4 * slots * PAGE * wide,
            bytes_accessed=2 * (key_cache.size + value_cache.size),
            transcendentals=slots * PAGE * heads_local,
        ),
        name="paged_attention",
    )(place_of, *query, tables, key_cache, value_cache)

    for shift, size in lower_groups(seq_size):
        if shift:
            totals = [pick_digit(totals, "seq", shift, size, d) for d in range(size)]
        parts = [
            swap(part, "seq", seq_size, d << shift) if d else part for d, part in enumerate(totals)
        ]
        totals = pl.pallas_call(
            combine_kernel,
            out_shape=jax.ShapeDtypeStruct(parts[0].shape, jnp.bfloat16),
            in_specs=[vmem] * size,
            out_specs=vmem,
            compiler_params=pltpu.CompilerParams(vmem_limit_bytes=6 * 2**20),
            name="combine",
        )(*parts)
    shift, size = last_group(seq_size)
    parts = [totals] + [swap(totals, "seq", seq_size, d << shift) for d in range(1, size)]
    my_context = pl.pallas_call(
        finish_kernel,
        out_shape=jax.ShapeDtypeStruct((held, wide), jnp.bfloat16),
        in_specs=[vmem] * (size + 2),
        out_specs=vmem,
        scratch_shapes=[pltpu.VMEM((held * heads_local, HD), jnp.float32)],
        compiler_params=pltpu.CompilerParams(vmem_limit_bytes=6 * 2**20),
        name="finish",
    )(*parts, my_query, my_keyval)

    total = pl.pallas_call(
        functools.partial(output_kernel, ways, seq_size),
        out_shape=jax.ShapeDtypeStruct((requests, w_out.shape[1]), jnp.float32),
        in_specs=[smem] + [vmem] * (ways + 1),
        out_specs=vmem,
        compiler_params=pltpu.CompilerParams(vmem_limit_bytes=16 * 2**20),
        name="project_out",
    )(me, *gather_relative(my_context, "seq", seq_size), w_out)
    step = 1
    while step < head_size:
        if step > 1:
            total = lax.reduce_precision(total, 8, 7)
            other = swap(total.astype(jnp.bfloat16), "head", head_size, step)
        else:
            other = swap(total, "head", head_size, step)
        total = total + other.astype(jnp.float32)
        step *= 2
    return total.astype(jnp.bfloat16)


def solution(mesh):
    seq_size, head_size = mesh.shape["seq"], mesh.shape["head"]

    def local(*args):
        return body(*args, seq_size=seq_size, head_size=head_size)

    return jax.shard_map(
        local,
        mesh=mesh,
        in_specs=(
            P(None, "seq"),
            P("seq", "head"),
            P("seq", "head"),
            P("head", "seq"),
            P("seq", None, "head"),
            P("seq", None, "head"),
            P("seq", "head"),
            P("seq", "head"),
            P(),
            P("seq"),
            P(),
        ),
        out_specs=P(None, "seq"),
        check_vma=False,
    )
```

```python
import functools
import math

import jax
import jax.numpy as jnp
from jax import lax
from jax.experimental import pallas as pl
from jax.experimental.pallas import tpu as pltpu
from jax.sharding import PartitionSpec as P

HD = 128
PAGE = 128
LANES = 128
CHUNK = 8
STAT = 16


masked_low = -1e30


def swap(x, axis, n, mask):
    return lax.ppermute(x, axis, [(j, j ^ mask) for j in range(n)])


def bit_groups(n):
    groups, shift = [], 0
    while (1 << shift) < n:
        size = min(4, n >> shift)
        groups.append((shift, size))
        shift += size.bit_length() - 1
    return groups


def lower_groups(n):
    return bit_groups(n)[:-1]


def last_group(n):
    return bit_groups(n)[-1]


def pick_digit(x, axis, shift, size, offset):
    digit = (lax.axis_index(axis) >> shift) % size
    x = x.reshape(x.shape[0] // size, size, *x.shape[1:])
    return lax.dynamic_index_in_dim(x, digit ^ offset, axis=1, keepdims=False)


def scatter_terms(parts, axis, n, beside):
    for shift, size in lower_groups(n):
        if shift:
            parts = [pick_digit(x, axis, shift, size, d) for d in range(size)]
        sent = [swap(parts[d], axis, n, d << shift) for d in range(1, size)]
        if shift == 0:
            sent, beside = lax.optimization_barrier((sent, beside))
        x = sum(sent, parts[0])
    shift, size = last_group(n)
    return [x] + [swap(x, axis, n, d << shift) for d in range(1, size)], beside


def gather_relative(x, axis, n):
    parts = [x]
    for shift, size in reversed(lower_groups(n)):
        x = jnp.concatenate(parts, axis=0) if len(parts) > 1 else parts[0]
        parts = [x] + [swap(x, axis, n, d << shift) for d in range(1, size)]
    return parts


def relative_place(block, me, n):
    last_shift, _ = last_group(n)
    offset = me ^ block
    place, weight = block >> last_shift, n
    for shift, size in lower_groups(n):
        weight //= size
        place = place + ((offset >> shift) & (size - 1)) * weight
    return place


def gathered_blocks(me, n):
    last_shift, last_size = last_group(n)
    offsets = [0]
    for shift, size in reversed(lower_groups(n)):
        offsets = [d << shift | e for d in range(size) for e in offsets]
    low = me & ((1 << last_shift) - 1)
    return [(c << last_shift) + (low ^ e) for e in offsets for c in range(last_size)]


def table_kernel(seq_size, ways, me, counts, trim, pages, key_scale, value_scale, tables, place_of):
    requests = counts.shape[0]
    chunks = tables.shape[0] // 4
    heads = LANES // CHUNK
    mine = requests // seq_size
    page = pages[...]
    owner, first, length = [jnp.zeros_like(page)] * 3
    start = 0
    for r in range(requests):
        end = start + counts[r]
        inside = (page >= start) & (page < end)
        owner = owner + jnp.where(page >= end, 1, 0)
        first = jnp.where(inside, start, first)
        length = jnp.where(inside, PAGE * counts[r] - trim[r], length)
        start = end
    valid = length - (page - first) * PAGE
    block = owner >> (mine.bit_length() - 1)
    row = relative_place(block, me[0], seq_size) * mine + (owner & (mine - 1))
    place_of[...] = ((me[0] & (ways - 1)) << 24) + (row << 16) + owner

    chunk_slot = lax.broadcasted_iota(jnp.int32, (chunks, LANES), 1) // CHUNK
    in_chunk = chunk_slot == lax.broadcasted_iota(jnp.int32, (chunks, LANES), 0)
    slot = lax.broadcasted_iota(jnp.int32, (LANES, LANES), 0) % CHUNK
    lane = lax.broadcasted_iota(jnp.int32, (LANES, LANES), 1)
    same_slot = slot == lane // heads
    low_head = lane % heads < heads // 2

    def spread(row, to):
        rest = jnp.where(in_chunk, jnp.broadcast_to(row, (chunks, LANES)), 0.0)
        total = jnp.zeros((chunks, LANES), jnp.float32)
        for _ in range(3):
            piece = rest.astype(jnp.bfloat16)
            rest = rest - piece.astype(jnp.float32)
            total = total + jnp.dot(
                piece,
                jnp.where(to, 1.0, 0.0).astype(jnp.bfloat16),
                preferred_element_type=jnp.float32,
            )
        return total

    def by_head(scale):
        return spread(scale[0:1, :], same_slot & low_head) + spread(
            scale[1:2, :], same_slot & jnp.logical_not(low_head)
        )

    tables[:chunks, :] = by_head(key_scale) * (1.0 / math.sqrt(HD))
    tables[chunks : 2 * chunks, :] = spread(valid.astype(jnp.float32), same_slot)
    tables[2 * chunks : 3 * chunks, :] = by_head(value_scale)
    tables[3 * chunks :, :] = spread(owner.astype(jnp.float32), same_slot)


def project_kernel(ways, me, hidden, w_query, w_keyval, *refs):
    outs, (keyval_out, query, keyval, result, sem) = refs[:ways], refs[ways:]
    depth = w_query.shape[0]
    tile = min(256, depth)
    copies = [
        [
            pltpu.make_async_copy(
                ref.at[pl.ds(row, tile)], held.at[pl.ds(row, tile)], sem.at[which, row // tile]
            )
            for which, (ref, held) in enumerate(((w_query, query), (w_keyval, keyval)))
        ]
        for row in range(0, depth, tile)
    ]
    for pair in copies:
        for copy in pair:
            copy.start()
    for row, pair in zip(range(0, depth, tile), copies):
        here = slice(row, row + tile)
        rows = hidden[:, here]
        for copy, held, to in zip(pair, (query, keyval), (result, keyval_out)):
            copy.wait()
            part = jnp.dot(rows, held[here, :], preferred_element_type=jnp.float32)
            to[...] = to[...] + part if row else part
    digit = me[0] & (ways - 1)
    for d, out in enumerate(outs):
        blocks, mine, _ = out.shape
        for b in range(blocks):
            if mine % 8 == 0:
                first = (b * ways + (digit ^ d)) * mine
                out[b] = result[pl.ds(pl.multiple_of(first, mine), mine), :]
                continue
            chosen = result[b * ways * mine : (b * ways + 1) * mine, :]
            for j in range(1, ways):
                first = (b * ways + j) * mine
                chosen = jnp.where((digit ^ d) == j, result[first : first + mine, :], chosen)
            out[b] = chosen


def output_kernel(ways, seq_size, me, *refs):
    parts, (w_out, rounded, out) = refs[:ways], refs[ways:]
    rows = jnp.concatenate([part[...] for part in parts], axis=0)
    total = jnp.dot(rows, w_out[...], preferred_element_type=jnp.float32)
    blocks = gathered_blocks(me[0], seq_size)
    mine = rows.shape[0] // len(blocks)
    if mine % 8 == 0:
        for i, block in enumerate(blocks):
            here = pl.ds(pl.multiple_of(block * mine, mine), mine)
            out[here, :] = total[i * mine : (i + 1) * mine]
        rounded[...] = out[...].astype(jnp.bfloat16)
        return
    for place in range(len(blocks)):
        chosen = total[:mine]
        for i, block in enumerate(blocks):
            chosen = jnp.where(block == place, total[i * mine : (i + 1) * mine], chosen)
        out[place * mine : (place + 1) * mine, :] = chosen
    rounded[...] = out[...].astype(jnp.bfloat16)


def join_kernel(*refs):
    *parts, out, rows = refs
    blocks, mine, columns = parts[0].shape
    held = blocks * mine
    whole = functools.reduce(jnp.add, [part[...] for part in parts]).reshape(held, columns)
    heads = columns // HD
    for h in range(heads):
        rows[pl.ds(h, held, stride=heads), :] = whole[:, h * HD : (h + 1) * HD]
    out[...] = rows[...].astype(jnp.bfloat16)


def new_rows(mine):
    return -(-4 * mine // 16) * 16


def split_stat(stat, lane):
    hi = stat.astype(jnp.bfloat16).astype(jnp.float32)
    rest = stat - hi
    mid = rest.astype(jnp.bfloat16).astype(jnp.float32)
    piece = jnp.where(lane < STAT, hi, jnp.where(lane < 2 * STAT, mid, rest - mid))
    return piece.astype(jnp.bfloat16)


def join_stat(pieces):
    pieces = pieces.astype(jnp.float32)
    return (pieces + pltpu.roll(pieces, LANES - STAT, 1)) + pltpu.roll(
        pieces, LANES - 2 * STAT, 1
    )


def attention_kernel(ways, mine, place_of, *refs):
    queries, refs = refs[:ways], refs[ways:]
    (keyval, tables, keys, values), refs = refs[:4], refs[4:]
    outs, refs = refs[:ways], refs[ways:]
    (
        query_low,
        query_high,
        probs,
        page_out,
        page_sum,
        page_max,
        dev_max,
        total_out,
        total_stat,
        keyval_rows,
    ) = refs
    slots = keys.shape[0]
    heads = LANES // CHUNK
    group = heads // 2
    chunks = slots // CHUNK
    blocks = outs[0].shape[0]
    step_chunks = 4

    for d, part in enumerate(queries):
        rows = part[...]
        low_head = lax.broadcasted_iota(jnp.int32, rows.shape, 0) % heads < group
        zero = jnp.zeros_like(rows)
        here = slice(rows.shape[0] * d, rows.shape[0] * (d + 1))
        query_low[here, :] = jnp.where(low_head, rows, zero)
        query_high[here, :] = jnp.where(low_head, zero, rows)
    total_out[...] = jnp.zeros_like(total_out)
    stat_lane = lax.broadcasted_iota(jnp.int32, total_stat.shape, 2) % STAT
    total_stat[...] = jnp.where(stat_lane < STAT // 2, masked_low, 0.0)

    def table(which, c):
        return tables[pl.ds(which * chunks + c, 1), :]

    lane_slot = lax.broadcasted_iota(jnp.int32, (PAGE, LANES), 1) // heads
    token = lax.broadcasted_iota(jnp.int32, (PAGE, LANES), 0).astype(jnp.float32)

    def score_chunk(c):
        places = [
            pl.multiple_of(((place_of[c * CHUNK + s] >> 16) & 0xFF) * heads, heads)
            for s in range(CHUNK)
        ]
        chosen = jnp.concatenate(
            [
                jnp.concatenate([ref[pl.ds(place, heads), :] for place in places], axis=0)
                for ref in (query_low, query_high)
            ],
            axis=1,
        )
        block = keys[pl.ds(c * CHUNK, CHUNK)].reshape(CHUNK * PAGE, 2 * HD)
        every = lax.dot_general(
            block, chosen, (((1,), (1,)), ((), ())), preferred_element_type=jnp.float32
        )
        score = every[:PAGE]
        for s in range(1, CHUNK):
            score = jnp.where(lane_slot == s, every[s * PAGE : (s + 1) * PAGE], score)
        score = jnp.where(token < table(1, c), score * table(0, c), masked_low)
        top = jnp.max(score, axis=0, keepdims=True)
        page_max[pl.ds(c, 1), :] = top
        prob = jnp.exp(score - top).astype(jnp.bfloat16).astype(jnp.float32)
        page_sum[pl.ds(c, 1), :] = jnp.sum(prob, axis=0, keepdims=True)
        probs[c] = prob.T.astype(jnp.bfloat16)

    empty = jnp.zeros((heads, PAGE), jnp.bfloat16)

    def value_chunk(c):
        prob = probs[c]
        for s in range(0, CHUNK, 2):
            pair = jnp.concatenate(
                [
                    jnp.concatenate([prob[s * heads : (s + 1) * heads], empty], axis=1),
                    jnp.concatenate([empty, prob[(s + 1) * heads : (s + 2) * heads]], axis=1),
                ],
                axis=0,
            )
            block = values[pl.ds(c * CHUNK + s, 2)].reshape(2 * PAGE, 2 * HD)
            both = jnp.dot(pair, block, preferred_element_type=jnp.float32)
            page_out[pl.ds(pl.multiple_of((c * CHUNK + s) * heads, heads), 2 * heads), :] = (
                jnp.concatenate(
                    [
                        both[:group, :HD],
                        both[group:heads, HD:],
                        both[heads : heads + group, :HD],
                        both[heads + group :, HD:],
                    ],
                    axis=0,
                )
            )

    for c in range(step_chunks):
        score_chunk(c)

    @pl.loop(1, chunks // step_chunks)
    def _(step):
        first = step * step_chunks
        for c in range(step_chunks):
            value_chunk(first + c - step_chunks)
            score_chunk(first + c)

    for c in range(chunks - step_chunks, chunks):
        value_chunk(c)

    biggest, who = page_max[...], tables[3 * chunks :, :]
    best = biggest
    for turn in range(CHUNK):
        other = pltpu.roll(biggest, turn * heads, 1) if turn else biggest
        other_who = pltpu.roll(who, turn * heads, 1) if turn else who
        for c in range(chunks):
            best = jnp.maximum(
                best, jnp.where(other_who[c : c + 1] == who, other[c : c + 1], masked_low)
            )
    dev_max[...] = best

    keep_max = lax.broadcasted_iota(jnp.int32, (heads, LANES), 1) % STAT < STAT // 2

    keep_max_row = lax.broadcasted_iota(jnp.int32, (PAGE, LANES), 0) % STAT < STAT // 2

    @pl.loop(0, chunks // step_chunks)
    def _(step):
        for c in [step * step_chunks + c for c in range(step_chunks)]:
            top = dev_max[pl.ds(c, 1), :]
            weight = jnp.exp(page_max[pl.ds(c, 1), :] - top)
            out_weight = jnp.broadcast_to(weight * table(2, c), (PAGE, LANES)).T
            stat = jnp.where(keep_max_row, top, weight * page_sum[pl.ds(c, 1), :]).T
            for s in range(CHUNK):
                here = pl.ds(
                    pl.multiple_of((place_of[c * CHUNK + s] & 0xFFFF) * heads, heads), heads
                )
                there = pl.ds(pl.multiple_of((c * CHUNK + s) * heads, heads), heads)
                part = slice(s * heads, (s + 1) * heads)
                turn = s % 2
                total_out[turn, here, :] += page_out[there, :] * out_weight[part]
                total_stat[turn, here, :] = jnp.where(
                    keep_max, stat[part], total_stat[turn, here, :] + stat[part]
                )

    lane = lax.broadcasted_iota(jnp.int32, (heads, LANES), 1)
    digit = place_of[0] >> 24
    for j in range(4):
        keyval_rows[pl.ds(j, keyval.shape[0], stride=4), :] = keyval[:, j * HD : (j + 1) * HD]
    for d, out in enumerate(outs):
        for b in range(blocks):
            block = b * ways + (digit ^ d)
            rows = pl.ds(pl.multiple_of(block * (mine * heads), mine * heads), mine * heads)
            out[b, : mine * heads, :] = (total_out[0, rows, :] + total_out[1, rows, :]).astype(
                jnp.bfloat16
            )
            even, odd = total_stat[0, rows, :], total_stat[1, rows, :]
            is_max = lax.broadcasted_iota(jnp.int32, even.shape, 1) % STAT < STAT // 2
            both = jnp.where(is_max, jnp.maximum(even, odd), even + odd)
            stat = jnp.zeros((heads, LANES), jnp.float32)
            for r in range(mine):
                stat = jnp.where(
                    lane % (STAT // 2) == r, both[r * heads : (r + 1) * heads], stat
                )
            out[b, mine * heads : (mine + 1) * heads, :] = split_stat(stat, lane)
            new = keyval_rows[pl.ds(pl.multiple_of(block * (4 * mine), 4 * mine), 4 * mine), :]
            if new.shape[0] < new_rows(mine):
                empty_rows = jnp.zeros((new_rows(mine) - new.shape[0], LANES), jnp.float32)
                new = jnp.concatenate([new, empty_rows], axis=0)
            out[b, (mine + 1) * heads :, :] = new.astype(jnp.bfloat16)


def combine_kernel(mine, *refs):
    *parts, out = refs
    blocks = out.shape[0]
    heads = LANES // CHUNK
    lane = lax.broadcasted_iota(jnp.int32, (heads, LANES), 1)
    for b in range(blocks):
        stats = [join_stat(part[b, mine * heads : (mine + 1) * heads, :]) for part in parts]
        maxima = [jnp.where(lane < mine, stat, 0.0) for stat in stats]
        top = functools.reduce(jnp.maximum, maxima)
        factors = [jnp.exp(m - top) for m in maxima]
        sums = sum(
            pltpu.roll(f, STAT // 2, 1) * jnp.where(lane < STAT, stat, 0.0)
            for f, stat in zip(factors, stats)
        )
        both = jnp.where(lane < STAT // 2, top, sums)
        both = jnp.where(lane < STAT, both, 0.0)
        both = (both + pltpu.roll(both, STAT, 1)) + pltpu.roll(both, 2 * STAT, 1)
        out[b, mine * heads : (mine + 1) * heads, :] = split_stat(both, lane)
        new = sum(part[b, (mine + 1) * heads :, :].astype(jnp.float32) for part in parts)
        out[b, (mine + 1) * heads :, :] = new.astype(jnp.bfloat16)
        for r in range(mine):
            rows = slice(r * heads, (r + 1) * heads)
            numer = sum(
                f[:, r : r + 1] * part[b, rows, :].astype(jnp.float32)
                for f, part in zip(factors, parts)
            )
            out[b, rows, :] = numer.astype(jnp.bfloat16)


def finish_kernel(mine, *refs):
    *parts, query, out, numers = refs
    blocks = parts[0].shape[0]
    heads = LANES // CHUNK
    group = heads // 2
    lane = lax.broadcasted_iota(jnp.int32, (heads, LANES), 1)
    low_head = lax.broadcasted_iota(jnp.int32, (heads, LANES), 0) < group
    def spread(new, r, which):
        low = jnp.broadcast_to(new[4 * r + which : 4 * r + which + 1], (heads, LANES))
        high = jnp.broadcast_to(new[4 * r + 2 + which : 4 * r + 3 + which], (heads, LANES))
        return jnp.where(low_head, low, high)

    for b in range(blocks):
        new = sum(part[b, (mine + 1) * heads :, :].astype(jnp.float32) for part in parts)
        new = new.astype(jnp.bfloat16).astype(jnp.float32)
        own = jnp.zeros((heads, LANES), jnp.float32)
        for r in range(mine):
            request = b * mine + r
            rows = query[request * heads : (request + 1) * heads, :].astype(jnp.float32)
            dot = jnp.sum(rows * spread(new, r, 0), axis=1, keepdims=True)
            own = jnp.where(lane == r, dot * (1.0 / math.sqrt(HD)), own)
        maxima, sums = [], []
        for part in parts:
            whole = join_stat(part[b, mine * heads : (mine + 1) * heads, :])
            maxima.append(jnp.where(lane < mine, whole, 0.0))
            sums.append(jnp.where(lane < mine, pltpu.roll(whole, LANES - STAT // 2, 1), 0.0))
        top = functools.reduce(jnp.maximum, maxima, own)
        fresh = jnp.exp(own - top)
        factors = [jnp.exp(m - top) for m in maxima]
        denom = sum((s * f for s, f in zip(sums, factors)), fresh)
        fresh = fresh / denom
        factors = [f / denom for f in factors]
        for r in range(mine):
            numer = fresh[:, r : r + 1] * spread(new, r, 1)
            for part, f in zip(parts, factors):
                rows = part[b, r * heads : (r + 1) * heads, :].astype(jnp.float32)
                numer = numer + f[:, r : r + 1] * rows
            request = b * mine + r
            numers[request * heads : (request + 1) * heads, :] = numer
    for h in range(heads):
        out[:, h * HD : (h + 1) * HD] = numers[
            pl.ds(h, blocks * mine, stride=heads), :
        ].astype(jnp.bfloat16)


def body(
    hidden_in,
    w_query,
    w_keyval,
    w_out,
    key_cache,
    value_cache,
    key_scale,
    value_scale,
    page_counts,
    slot_pages,
    trim,
    seq_size,
    head_size,
):
    requests = hidden_in.shape[0]
    slots = key_cache.shape[0]
    kv_local = w_keyval.shape[1] // (2 * HD)
    heads_local = w_query.shape[1] // HD
    wide = heads_local * HD
    group = heads_local // kv_local
    assert kv_local == 2 and heads_local * CHUNK == LANES
    assert slots % CHUNK == 0
    mine = requests // seq_size
    inverse_square_root = 1.0 / math.sqrt(HD)

    assert slots == LANES and mine & (mine - 1) == 0
    ways = lower_groups(seq_size)[0][1]
    chunks = slots // CHUNK
    smem = pl.BlockSpec(memory_space=pltpu.SMEM)
    vmem = pl.BlockSpec(memory_space=pltpu.VMEM)
    hbm = pl.BlockSpec(memory_space=pl.ANY)
    small = pltpu.CompilerParams(vmem_limit_bytes=6 * 2**20)
    me = lax.axis_index("seq").reshape(1)

    tables, place_of = pl.pallas_call(
        functools.partial(table_kernel, seq_size, ways),
        out_shape=[
            jax.ShapeDtypeStruct((4 * chunks, LANES), jnp.float32),
            jax.ShapeDtypeStruct((1, slots), jnp.int32),
        ],
        in_specs=[smem, smem, smem, vmem, vmem, vmem],
        out_specs=[vmem, vmem],
        compiler_params=small,
        name="page_table",
    )(me, page_counts, trim, slot_pages.reshape(1, slots), key_scale.T, value_scale.T)
    place_of = place_of.reshape(slots)

    held = last_group(seq_size)[1] * mine
    part_shape = jax.ShapeDtypeStruct((seq_size // ways, mine, wide), jnp.float32)
    keyval_shape = jax.ShapeDtypeStruct((requests, w_keyval.shape[1]), jnp.float32)
    *parts, keyval = pl.pallas_call(
        functools.partial(project_kernel, ways),
        out_shape=[part_shape] * ways + [keyval_shape],
        in_specs=[smem, vmem, hbm, hbm],
        out_specs=[vmem] * (ways + 1),
        scratch_shapes=[
            pltpu.VMEM(w_query.shape, jnp.bfloat16),
            pltpu.VMEM(w_keyval.shape, jnp.bfloat16),
            pltpu.VMEM((requests, wide), jnp.float32),
            pltpu.SemaphoreType.DMA((2, pl.cdiv(w_query.shape[0], 256))),
        ],
        compiler_params=pltpu.CompilerParams(vmem_limit_bytes=53 * 2**20),
        name="project",
    )(me, hidden_in, w_query, w_keyval)
    terms, (tables, place_of) = scatter_terms(parts, "seq", seq_size, (tables, place_of))
    my_query = pl.pallas_call(
        join_kernel,
        out_shape=jax.ShapeDtypeStruct((held * heads_local, HD), jnp.bfloat16),
        in_specs=[vmem] * len(terms),
        out_specs=vmem,
        scratch_shapes=[pltpu.VMEM((held * heads_local, HD), jnp.float32)],
        compiler_params=small,
        cost_estimate=pl.CostEstimate(flops=10**10, bytes_accessed=10**7, transcendentals=0),
        name="join",
    )(*terms)
    query = gather_relative(my_query, "seq", seq_size)

    every_row = requests * heads_local
    block_rows = (mine + 1) * heads_local + new_rows(mine)
    totals = pl.pallas_call(
        functools.partial(attention_kernel, ways, mine),
        out_shape=[jax.ShapeDtypeStruct((seq_size // ways, block_rows, HD), jnp.bfloat16)] * ways,
        in_specs=[smem] + [vmem] * (ways + 4),
        out_specs=[vmem] * ways,
        scratch_shapes=[
            pltpu.VMEM((every_row, HD), jnp.bfloat16),
            pltpu.VMEM((every_row, HD), jnp.bfloat16),
            pltpu.VMEM((chunks, LANES, PAGE), jnp.bfloat16),
            pltpu.VMEM((slots * heads_local, HD), jnp.float32),
            pltpu.VMEM((chunks, LANES), jnp.float32),
            pltpu.VMEM((chunks, LANES), jnp.float32),
            pltpu.VMEM((chunks, LANES), jnp.float32),
            pltpu.VMEM((2, every_row, HD), jnp.float32),
            pltpu.VMEM((2, every_row, HD), jnp.float32),
            pltpu.VMEM((requests * 2 * kv_local, HD), jnp.float32),
        ],
        compiler_params=pltpu.CompilerParams(vmem_limit_bytes=24 * 2**20),
        cost_estimate=pl.CostEstimate(
            flops=4 * slots * PAGE * wide,
            bytes_accessed=2 * (key_cache.size + value_cache.size),
            transcendentals=slots * PAGE * heads_local,
        ),
        name="paged_attention",
    )(place_of, *query, keyval, tables, key_cache, value_cache)

    for shift, size in lower_groups(seq_size):
        if shift:
            totals = [pick_digit(totals, "seq", shift, size, d) for d in range(size)]
        parts = [
            swap(part, "seq", seq_size, d << shift) if d else part for d, part in enumerate(totals)
        ]
        totals = pl.pallas_call(
            functools.partial(combine_kernel, mine),
            out_shape=jax.ShapeDtypeStruct(parts[0].shape, jnp.bfloat16),
            in_specs=[vmem] * size,
            out_specs=vmem,
            compiler_params=pltpu.CompilerParams(vmem_limit_bytes=6 * 2**20),
            name="combine",
        )(*parts)
    shift, size = last_group(seq_size)
    parts = [totals] + [swap(totals, "seq", seq_size, d << shift) for d in range(1, size)]
    my_context = pl.pallas_call(
        functools.partial(finish_kernel, mine),
        out_shape=jax.ShapeDtypeStruct((held, wide), jnp.bfloat16),
        in_specs=[vmem] * (size + 1),
        out_specs=vmem,
        scratch_shapes=[pltpu.VMEM((held * heads_local, HD), jnp.float32)],
        compiler_params=pltpu.CompilerParams(vmem_limit_bytes=6 * 2**20),
        name="finish",
    )(*parts, my_query)

    total = pl.pallas_call(
        functools.partial(output_kernel, ways, seq_size),
        out_shape=jax.ShapeDtypeStruct((requests, w_out.shape[1]), jnp.bfloat16),
        in_specs=[smem] + [vmem] * (ways + 1),
        out_specs=vmem,
        scratch_shapes=[pltpu.VMEM((requests, w_out.shape[1]), jnp.float32)],
        compiler_params=pltpu.CompilerParams(vmem_limit_bytes=16 * 2**20),
        name="project_out",
    )(me, *gather_relative(my_context, "seq", seq_size), w_out)
    mask = head_size // 2
    while mask:
        if mask > 1:
            if total.dtype != jnp.bfloat16:
                total = lax.reduce_precision(total, 8, 7).astype(jnp.bfloat16)
            other = swap(total, "head", head_size, mask)
            total = total.astype(jnp.float32) + other.astype(jnp.float32)
        else:
            total = total + swap(total, "head", head_size, mask)
        mask //= 2
    return total.astype(jnp.bfloat16)


def solution(mesh):
    seq_size, head_size = mesh.shape["seq"], mesh.shape["head"]

    def local(*args):
        return body(*args, seq_size=seq_size, head_size=head_size)

    return jax.shard_map(
        local,
        mesh=mesh,
        in_specs=(
            P(None, "seq"),
            P("seq", "head"),
            P("seq", "head"),
            P("head", "seq"),
            P("seq", None, "head"),
            P("seq", None, "head"),
            P("seq", "head"),
            P("seq", "head"),
            P(),
            P("seq"),
            P(),
        ),
        out_specs=P(None, "seq"),
        check_vma=False,
    )
```

```python
import functools
import math

import jax
import jax.numpy as jnp
from jax import lax
from jax.experimental import pallas as pl
from jax.experimental.pallas import tpu as pltpu
from jax.sharding import PartitionSpec as P

HD = 128
PAGE = 128
LANES = 128
CHUNK = 8
STAT = 16


masked_low = -1e30


def swap(x, axis, n, mask):
    return lax.ppermute(x, axis, [(j, j ^ mask) for j in range(n)])


def way_order(size):
    return [0, size - 1, *range(1, size - 1)]


def swap_all(parts, axis, n, shift):
    return [
        swap(parts[d], axis, n, d << shift) if d else parts[0] for d in way_order(len(parts))
    ]


def in_order(parts):
    return [parts[i] for i in sorted(range(len(parts)), key=way_order(len(parts)).__getitem__)]


def bit_groups(n):
    groups, shift = [], 0
    while (1 << shift) < n:
        size = min(4, n >> shift)
        groups.append((shift, size))
        shift += size.bit_length() - 1
    return groups


def lower_groups(n):
    return bit_groups(n)[:-1]


def last_group(n):
    return bit_groups(n)[-1]


def pick_digit(x, axis, shift, size, offset):
    digit = (lax.axis_index(axis) >> shift) % size
    x = x.reshape(x.shape[0] // size, size, *x.shape[1:])
    return lax.dynamic_index_in_dim(x, digit ^ offset, axis=1, keepdims=False)


def scatter_terms(parts, axis, n, beside):
    for shift, size in lower_groups(n):
        if shift:
            parts = [pick_digit(x, axis, shift, size, d) for d in range(size)]
        got = swap_all(parts, axis, n, shift)
        if shift == 0:
            got, beside = lax.optimization_barrier((got, beside))
        x = sum(got[1:], got[0])
    shift, size = last_group(n)
    return [x] + [swap(x, axis, n, d << shift) for d in range(1, size)], beside


def gather_relative(x, axis, n):
    parts = [x]
    for shift, size in reversed(lower_groups(n)):
        x = jnp.concatenate(in_order(parts), axis=0) if len(parts) > 1 else parts[0]
        parts = swap_all([x] * size, axis, n, shift)
    return parts


def relative_place(block, me, n):
    last_shift, _ = last_group(n)
    offset = me ^ block
    place, weight = block >> last_shift, n
    for shift, size in lower_groups(n):
        weight //= size
        place = place + ((offset >> shift) & (size - 1)) * weight
    return place


def gathered_blocks(me, n):
    last_shift, last_size = last_group(n)
    offsets = [0]
    for shift, size in reversed(lower_groups(n)):
        offsets = [d << shift | e for d in range(size) for e in offsets]
    low = me & ((1 << last_shift) - 1)
    return [(c << last_shift) + (low ^ e) for e in offsets for c in range(last_size)]


def table_kernel(seq_size, ways, me, counts, trim, pages, key_scale, value_scale, tables, place_of):
    requests = counts.shape[0]
    chunks = tables.shape[0] // 4
    heads = LANES // CHUNK
    mine = requests // seq_size
    page = pages[...]
    owner, first, length = [jnp.zeros_like(page)] * 3
    start = 0
    for r in range(requests):
        end = start + counts[r]
        inside = (page >= start) & (page < end)
        owner = owner + jnp.where(page >= end, 1, 0)
        first = jnp.where(inside, start, first)
        length = jnp.where(inside, PAGE * counts[r] - trim[r], length)
        start = end
    valid = length - (page - first) * PAGE
    block = owner >> (mine.bit_length() - 1)
    row = relative_place(block, me[0], seq_size) * mine + (owner & (mine - 1))
    place_of[...] = ((me[0] & (ways - 1)) << 24) + (row << 16) + owner

    chunk_slot = lax.broadcasted_iota(jnp.int32, (chunks, LANES), 1) // CHUNK
    in_chunk = chunk_slot == lax.broadcasted_iota(jnp.int32, (chunks, LANES), 0)
    slot = lax.broadcasted_iota(jnp.int32, (LANES, LANES), 0) % CHUNK
    lane = lax.broadcasted_iota(jnp.int32, (LANES, LANES), 1)
    same_slot = slot == lane // heads
    low_head = lane % heads < heads // 2

    def spread(row, to):
        rest = jnp.where(in_chunk, jnp.broadcast_to(row, (chunks, LANES)), 0.0)
        total = jnp.zeros((chunks, LANES), jnp.float32)
        for _ in range(3):
            piece = rest.astype(jnp.bfloat16)
            rest = rest - piece.astype(jnp.float32)
            total = total + jnp.dot(
                piece,
                jnp.where(to, 1.0, 0.0).astype(jnp.bfloat16),
                preferred_element_type=jnp.float32,
            )
        return total

    def by_head(scale):
        return spread(scale[0:1, :], same_slot & low_head) + spread(
            scale[1:2, :], same_slot & jnp.logical_not(low_head)
        )

    tables[:chunks, :] = by_head(key_scale) * (1.0 / math.sqrt(HD))
    tables[chunks : 2 * chunks, :] = spread(valid.astype(jnp.float32), same_slot)
    tables[2 * chunks : 3 * chunks, :] = by_head(value_scale)
    tables[3 * chunks :, :] = spread(owner.astype(jnp.float32), same_slot)


def project_kernel(ways, me, hidden, w_query, w_keyval, *refs):
    outs, (keyval_out, query, keyval, result, sem) = refs[:ways], refs[ways:]
    depth = w_query.shape[0]
    tile = min(256, depth)
    copies = [
        [
            pltpu.make_async_copy(
                ref.at[pl.ds(row, tile)], held.at[pl.ds(row, tile)], sem.at[which, row // tile]
            )
            for which, (ref, held) in enumerate(((w_query, query), (w_keyval, keyval)))
        ]
        for row in range(0, depth, tile)
    ]
    for pair in copies:
        for copy in pair:
            copy.start()
    for row, pair in zip(range(0, depth, tile), copies):
        here = slice(row, row + tile)
        rows = hidden[:, here]
        for copy, held, to in zip(pair, (query, keyval), (result, keyval_out)):
            copy.wait()
            part = jnp.dot(rows, held[here, :], preferred_element_type=jnp.float32)
            to[...] = to[...] + part if row else part
    digit = me[0] & (ways - 1)
    for d, out in enumerate(outs):
        blocks, mine, _ = out.shape
        for b in range(blocks):
            if mine % 8 == 0:
                first = (b * ways + (digit ^ d)) * mine
                out[b] = result[pl.ds(pl.multiple_of(first, mine), mine), :]
                continue
            chosen = result[b * ways * mine : (b * ways + 1) * mine, :]
            for j in range(1, ways):
                first = (b * ways + j) * mine
                chosen = jnp.where((digit ^ d) == j, result[first : first + mine, :], chosen)
            out[b] = chosen


def output_kernel(ways, seq_size, me, *refs):
    parts, (w_out, rounded, out) = refs[:ways], refs[ways:]
    rows = jnp.concatenate([part[...] for part in in_order(parts)], axis=0)
    total = jnp.dot(rows, w_out[...], preferred_element_type=jnp.float32)
    blocks = gathered_blocks(me[0], seq_size)
    mine = rows.shape[0] // len(blocks)
    if mine % 8 == 0:
        for i, block in enumerate(blocks):
            here = pl.ds(pl.multiple_of(block * mine, mine), mine)
            out[here, :] = total[i * mine : (i + 1) * mine]
        rounded[...] = out[...].astype(jnp.bfloat16)
        return
    for place in range(len(blocks)):
        chosen = total[:mine]
        for i, block in enumerate(blocks):
            chosen = jnp.where(block == place, total[i * mine : (i + 1) * mine], chosen)
        out[place * mine : (place + 1) * mine, :] = chosen
    rounded[...] = out[...].astype(jnp.bfloat16)


def join_kernel(*refs):
    *parts, out, rows = refs
    blocks, mine, columns = parts[0].shape
    held = blocks * mine
    whole = functools.reduce(jnp.add, [part[...] for part in parts]).reshape(held, columns)
    heads = columns // HD
    for h in range(heads):
        rows[pl.ds(h, held, stride=heads), :] = whole[:, h * HD : (h + 1) * HD]
    out[...] = rows[...].astype(jnp.bfloat16)


def new_rows(mine):
    return -(-4 * mine // 16) * 16


def split_stat(stat, lane):
    hi = stat.astype(jnp.bfloat16).astype(jnp.float32)
    rest = stat - hi
    mid = rest.astype(jnp.bfloat16).astype(jnp.float32)
    piece = jnp.where(lane < STAT, hi, jnp.where(lane < 2 * STAT, mid, rest - mid))
    return piece.astype(jnp.bfloat16)


def join_stat(pieces):
    pieces = pieces.astype(jnp.float32)
    return (pieces + pltpu.roll(pieces, LANES - STAT, 1)) + pltpu.roll(
        pieces, LANES - 2 * STAT, 1
    )


def attention_kernel(ways, mine, place_of, *refs):
    queries, refs = refs[:ways], refs[ways:]
    (keyval, tables, keys, values), refs = refs[:4], refs[4:]
    outs, refs = refs[:ways], refs[ways:]
    (
        query_low,
        query_high,
        probs,
        page_out,
        page_sum,
        page_max,
        dev_max,
        total_out,
        total_stat,
        keyval_rows,
    ) = refs
    slots = keys.shape[0]
    heads = LANES // CHUNK
    group = heads // 2
    chunks = slots // CHUNK
    blocks = outs[0].shape[0]
    step_chunks = 4

    for d, part in enumerate(in_order(queries)):
        rows = part[...]
        low_head = lax.broadcasted_iota(jnp.int32, rows.shape, 0) % heads < group
        zero = jnp.zeros_like(rows)
        here = slice(rows.shape[0] * d, rows.shape[0] * (d + 1))
        query_low[here, :] = jnp.where(low_head, rows, zero)
        query_high[here, :] = jnp.where(low_head, zero, rows)
    total_out[...] = jnp.zeros_like(total_out)
    stat_lane = lax.broadcasted_iota(jnp.int32, total_stat.shape, 2) % STAT
    total_stat[...] = jnp.where(stat_lane < STAT // 2, masked_low, 0.0)

    def table(which, c):
        return tables[pl.ds(which * chunks + c, 1), :]

    lane_slot = lax.broadcasted_iota(jnp.int32, (PAGE, LANES), 1) // heads
    token = lax.broadcasted_iota(jnp.int32, (PAGE, LANES), 0).astype(jnp.float32)

    def score_chunk(c):
        places = [
            pl.multiple_of(((place_of[c * CHUNK + s] >> 16) & 0xFF) * heads, heads)
            for s in range(CHUNK)
        ]
        chosen = jnp.concatenate(
            [
                jnp.concatenate([ref[pl.ds(place, heads), :] for place in places], axis=0)
                for ref in (query_low, query_high)
            ],
            axis=1,
        )
        block = keys[pl.ds(c * CHUNK, CHUNK)].reshape(CHUNK * PAGE, 2 * HD)
        every = lax.dot_general(
            block, chosen, (((1,), (1,)), ((), ())), preferred_element_type=jnp.float32
        )
        score = every[:PAGE]
        for s in range(1, CHUNK):
            score = jnp.where(lane_slot == s, every[s * PAGE : (s + 1) * PAGE], score)
        score = jnp.where(token < table(1, c), score * table(0, c), masked_low)
        top = jnp.max(score, axis=0, keepdims=True)
        page_max[pl.ds(c, 1), :] = top
        prob = jnp.exp(score - top).astype(jnp.bfloat16).astype(jnp.float32)
        page_sum[pl.ds(c, 1), :] = jnp.sum(prob, axis=0, keepdims=True)
        probs[c] = prob.T.astype(jnp.bfloat16)

    empty = jnp.zeros((heads, PAGE), jnp.bfloat16)

    def value_chunk(c):
        prob = probs[c]
        for s in range(0, CHUNK, 2):
            pair = jnp.concatenate(
                [
                    jnp.concatenate([prob[s * heads : (s + 1) * heads], empty], axis=1),
                    jnp.concatenate([empty, prob[(s + 1) * heads : (s + 2) * heads]], axis=1),
                ],
                axis=0,
            )
            block = values[pl.ds(c * CHUNK + s, 2)].reshape(2 * PAGE, 2 * HD)
            both = jnp.dot(pair, block, preferred_element_type=jnp.float32)
            page_out[pl.ds(pl.multiple_of((c * CHUNK + s) * heads, heads), 2 * heads), :] = (
                jnp.concatenate(
                    [
                        both[:group, :HD],
                        both[group:heads, HD:],
                        both[heads : heads + group, :HD],
                        both[heads + group :, HD:],
                    ],
                    axis=0,
                )
            )

    for c in range(step_chunks):
        score_chunk(c)

    @pl.loop(1, chunks // step_chunks)
    def _(step):
        first = step * step_chunks
        for c in range(step_chunks):
            value_chunk(first + c - step_chunks)
            score_chunk(first + c)

    for c in range(chunks - step_chunks, chunks):
        value_chunk(c)

    biggest, who = page_max[...], tables[3 * chunks :, :]
    best = biggest
    for turn in range(CHUNK):
        other = pltpu.roll(biggest, turn * heads, 1) if turn else biggest
        other_who = pltpu.roll(who, turn * heads, 1) if turn else who
        for c in range(chunks):
            best = jnp.maximum(
                best, jnp.where(other_who[c : c + 1] == who, other[c : c + 1], masked_low)
            )
    dev_max[...] = best

    keep_max = lax.broadcasted_iota(jnp.int32, (heads, LANES), 1) % STAT < STAT // 2

    keep_max_row = lax.broadcasted_iota(jnp.int32, (PAGE, LANES), 0) % STAT < STAT // 2

    @pl.loop(0, chunks // step_chunks)
    def _(step):
        for c in [step * step_chunks + c for c in range(step_chunks)]:
            top = dev_max[pl.ds(c, 1), :]
            weight = jnp.exp(page_max[pl.ds(c, 1), :] - top)
            out_weight = jnp.broadcast_to(weight * table(2, c), (PAGE, LANES)).T
            stat = jnp.where(keep_max_row, top, weight * page_sum[pl.ds(c, 1), :]).T
            for s in range(CHUNK):
                here = pl.ds(
                    pl.multiple_of((place_of[c * CHUNK + s] & 0xFFFF) * heads, heads), heads
                )
                there = pl.ds(pl.multiple_of((c * CHUNK + s) * heads, heads), heads)
                part = slice(s * heads, (s + 1) * heads)
                turn = s % 2
                total_out[turn, here, :] += page_out[there, :] * out_weight[part]
                total_stat[turn, here, :] = jnp.where(
                    keep_max, stat[part], total_stat[turn, here, :] + stat[part]
                )

    lane = lax.broadcasted_iota(jnp.int32, (heads, LANES), 1)
    digit = place_of[0] >> 24
    for j in range(4):
        keyval_rows[pl.ds(j, keyval.shape[0], stride=4), :] = keyval[:, j * HD : (j + 1) * HD]
    for d, out in enumerate(outs):
        for b in range(blocks):
            block = b * ways + (digit ^ d)
            rows = pl.ds(pl.multiple_of(block * (mine * heads), mine * heads), mine * heads)
            out[b, : mine * heads, :] = (total_out[0, rows, :] + total_out[1, rows, :]).astype(
                jnp.bfloat16
            )
            even, odd = total_stat[0, rows, :], total_stat[1, rows, :]
            is_max = lax.broadcasted_iota(jnp.int32, even.shape, 1) % STAT < STAT // 2
            both = jnp.where(is_max, jnp.maximum(even, odd), even + odd)
            stat = jnp.zeros((heads, LANES), jnp.float32)
            for r in range(mine):
                stat = jnp.where(
                    lane % (STAT // 2) == r, both[r * heads : (r + 1) * heads], stat
                )
            out[b, mine * heads : (mine + 1) * heads, :] = split_stat(stat, lane)
            new = keyval_rows[pl.ds(pl.multiple_of(block * (4 * mine), 4 * mine), 4 * mine), :]
            if new.shape[0] < new_rows(mine):
                empty_rows = jnp.zeros((new_rows(mine) - new.shape[0], LANES), jnp.float32)
                new = jnp.concatenate([new, empty_rows], axis=0)
            out[b, (mine + 1) * heads :, :] = new.astype(jnp.bfloat16)


def combine_kernel(mine, *refs):
    *parts, out = refs
    blocks = out.shape[0]
    heads = LANES // CHUNK
    lane = lax.broadcasted_iota(jnp.int32, (heads, LANES), 1)
    for b in range(blocks):
        stats = [join_stat(part[b, mine * heads : (mine + 1) * heads, :]) for part in parts]
        maxima = [jnp.where(lane < mine, stat, 0.0) for stat in stats]
        top = functools.reduce(jnp.maximum, maxima)
        factors = [jnp.exp(m - top) for m in maxima]
        sums = sum(
            pltpu.roll(f, STAT // 2, 1) * jnp.where(lane < STAT, stat, 0.0)
            for f, stat in zip(factors, stats)
        )
        both = jnp.where(lane < STAT // 2, top, sums)
        both = jnp.where(lane < STAT, both, 0.0)
        both = (both + pltpu.roll(both, STAT, 1)) + pltpu.roll(both, 2 * STAT, 1)
        out[b, mine * heads : (mine + 1) * heads, :] = split_stat(both, lane)
        new = sum(part[b, (mine + 1) * heads :, :].astype(jnp.float32) for part in parts)
        out[b, (mine + 1) * heads :, :] = new.astype(jnp.bfloat16)
        for r in range(mine):
            rows = slice(r * heads, (r + 1) * heads)
            numer = sum(
                f[:, r : r + 1] * part[b, rows, :].astype(jnp.float32)
                for f, part in zip(factors, parts)
            )
            out[b, rows, :] = numer.astype(jnp.bfloat16)


def finish_kernel(mine, *refs):
    *parts, query, out, numers = refs
    blocks = parts[0].shape[0]
    heads = LANES // CHUNK
    group = heads // 2
    lane = lax.broadcasted_iota(jnp.int32, (heads, LANES), 1)
    low_head = lax.broadcasted_iota(jnp.int32, (heads, LANES), 0) < group
    def spread(new, r, which):
        low = jnp.broadcast_to(new[4 * r + which : 4 * r + which + 1], (heads, LANES))
        high = jnp.broadcast_to(new[4 * r + 2 + which : 4 * r + 3 + which], (heads, LANES))
        return jnp.where(low_head, low, high)

    for b in range(blocks):
        new = sum(part[b, (mine + 1) * heads :, :].astype(jnp.float32) for part in parts)
        new = new.astype(jnp.bfloat16).astype(jnp.float32)
        own = jnp.zeros((heads, LANES), jnp.float32)
        for r in range(mine):
            request = b * mine + r
            rows = query[request * heads : (request + 1) * heads, :].astype(jnp.float32)
            dot = jnp.sum(rows * spread(new, r, 0), axis=1, keepdims=True)
            own = jnp.where(lane == r, dot * (1.0 / math.sqrt(HD)), own)
        maxima, sums = [], []
        for part in parts:
            whole = join_stat(part[b, mine * heads : (mine + 1) * heads, :])
            maxima.append(jnp.where(lane < mine, whole, 0.0))
            sums.append(jnp.where(lane < mine, pltpu.roll(whole, LANES - STAT // 2, 1), 0.0))
        top = functools.reduce(jnp.maximum, maxima, own)
        fresh = jnp.exp(own - top)
        factors = [jnp.exp(m - top) for m in maxima]
        denom = sum((s * f for s, f in zip(sums, factors)), fresh)
        fresh = fresh / denom
        factors = [f / denom for f in factors]
        for r in range(mine):
            numer = fresh[:, r : r + 1] * spread(new, r, 1)
            for part, f in zip(parts, factors):
                rows = part[b, r * heads : (r + 1) * heads, :].astype(jnp.float32)
                numer = numer + f[:, r : r + 1] * rows
            request = b * mine + r
            numers[request * heads : (request + 1) * heads, :] = numer
    for h in range(heads):
        out[:, h * HD : (h + 1) * HD] = numers[
            pl.ds(h, blocks * mine, stride=heads), :
        ].astype(jnp.bfloat16)


def body(
    hidden_in,
    w_query,
    w_keyval,
    w_out,
    key_cache,
    value_cache,
    key_scale,
    value_scale,
    page_counts,
    slot_pages,
    trim,
    seq_size,
    head_size,
):
    requests = hidden_in.shape[0]
    slots = key_cache.shape[0]
    kv_local = w_keyval.shape[1] // (2 * HD)
    heads_local = w_query.shape[1] // HD
    wide = heads_local * HD
    group = heads_local // kv_local
    assert kv_local == 2 and heads_local * CHUNK == LANES
    assert slots % CHUNK == 0
    mine = requests // seq_size
    inverse_square_root = 1.0 / math.sqrt(HD)

    assert slots == LANES and mine & (mine - 1) == 0
    ways = lower_groups(seq_size)[0][1]
    chunks = slots // CHUNK
    smem = pl.BlockSpec(memory_space=pltpu.SMEM)
    vmem = pl.BlockSpec(memory_space=pltpu.VMEM)
    hbm = pl.BlockSpec(memory_space=pl.ANY)
    small = pltpu.CompilerParams(vmem_limit_bytes=6 * 2**20)
    me = lax.axis_index("seq").reshape(1)

    tables, place_of = pl.pallas_call(
        functools.partial(table_kernel, seq_size, ways),
        out_shape=[
            jax.ShapeDtypeStruct((4 * chunks, LANES), jnp.float32),
            jax.ShapeDtypeStruct((1, slots), jnp.int32),
        ],
        in_specs=[smem, smem, smem, vmem, vmem, vmem],
        out_specs=[vmem, vmem],
        compiler_params=small,
        name="page_table",
    )(me, page_counts, trim, slot_pages.reshape(1, slots), key_scale.T, value_scale.T)
    place_of = place_of.reshape(slots)

    held = last_group(seq_size)[1] * mine
    part_shape = jax.ShapeDtypeStruct((seq_size // ways, mine, wide), jnp.float32)
    keyval_shape = jax.ShapeDtypeStruct((requests, w_keyval.shape[1]), jnp.float32)
    *parts, keyval = pl.pallas_call(
        functools.partial(project_kernel, ways),
        out_shape=[part_shape] * ways + [keyval_shape],
        in_specs=[smem, vmem, hbm, hbm],
        out_specs=[vmem] * (ways + 1),
        scratch_shapes=[
            pltpu.VMEM(w_query.shape, jnp.bfloat16),
            pltpu.VMEM(w_keyval.shape, jnp.bfloat16),
            pltpu.VMEM((requests, wide), jnp.float32),
            pltpu.SemaphoreType.DMA((2, pl.cdiv(w_query.shape[0], 256))),
        ],
        compiler_params=pltpu.CompilerParams(vmem_limit_bytes=53 * 2**20),
        name="project",
    )(me, hidden_in, w_query, w_keyval)
    terms, (tables, place_of) = scatter_terms(parts, "seq", seq_size, (tables, place_of))
    my_query = pl.pallas_call(
        join_kernel,
        out_shape=jax.ShapeDtypeStruct((held * heads_local, HD), jnp.bfloat16),
        in_specs=[vmem] * len(terms),
        out_specs=vmem,
        scratch_shapes=[pltpu.VMEM((held * heads_local, HD), jnp.float32)],
        compiler_params=small,
        cost_estimate=pl.CostEstimate(flops=10**10, bytes_accessed=10**7, transcendentals=0),
        name="join",
    )(*terms)
    query = gather_relative(my_query, "seq", seq_size)

    every_row = requests * heads_local
    block_rows = (mine + 1) * heads_local + new_rows(mine)
    totals = pl.pallas_call(
        functools.partial(attention_kernel, ways, mine),
        out_shape=[jax.ShapeDtypeStruct((seq_size // ways, block_rows, HD), jnp.bfloat16)] * ways,
        in_specs=[smem] + [vmem] * (ways + 4),
        out_specs=[vmem] * ways,
        scratch_shapes=[
            pltpu.VMEM((every_row, HD), jnp.bfloat16),
            pltpu.VMEM((every_row, HD), jnp.bfloat16),
            pltpu.VMEM((chunks, LANES, PAGE), jnp.bfloat16),
            pltpu.VMEM((slots * heads_local, HD), jnp.float32),
            pltpu.VMEM((chunks, LANES), jnp.float32),
            pltpu.VMEM((chunks, LANES), jnp.float32),
            pltpu.VMEM((chunks, LANES), jnp.float32),
            pltpu.VMEM((2, every_row, HD), jnp.float32),
            pltpu.VMEM((2, every_row, HD), jnp.float32),
            pltpu.VMEM((requests * 2 * kv_local, HD), jnp.float32),
        ],
        compiler_params=pltpu.CompilerParams(vmem_limit_bytes=24 * 2**20),
        cost_estimate=pl.CostEstimate(
            flops=4 * slots * PAGE * wide,
            bytes_accessed=2 * (key_cache.size + value_cache.size),
            transcendentals=slots * PAGE * heads_local,
        ),
        name="paged_attention",
    )(place_of, *query, keyval, tables, key_cache, value_cache)

    for shift, size in lower_groups(seq_size):
        if shift:
            totals = [pick_digit(totals, "seq", shift, size, d) for d in range(size)]
        parts = swap_all(totals, "seq", seq_size, shift)
        totals = pl.pallas_call(
            functools.partial(combine_kernel, mine),
            out_shape=jax.ShapeDtypeStruct(parts[0].shape, jnp.bfloat16),
            in_specs=[vmem] * size,
            out_specs=vmem,
            compiler_params=pltpu.CompilerParams(vmem_limit_bytes=6 * 2**20),
            name="combine",
        )(*parts)
    shift, size = last_group(seq_size)
    parts = [totals] + [swap(totals, "seq", seq_size, d << shift) for d in range(1, size)]
    my_context = pl.pallas_call(
        functools.partial(finish_kernel, mine),
        out_shape=jax.ShapeDtypeStruct((held, wide), jnp.bfloat16),
        in_specs=[vmem] * (size + 1),
        out_specs=vmem,
        scratch_shapes=[pltpu.VMEM((held * heads_local, HD), jnp.float32)],
        compiler_params=pltpu.CompilerParams(vmem_limit_bytes=6 * 2**20),
        name="finish",
    )(*parts, my_query)

    total = pl.pallas_call(
        functools.partial(output_kernel, ways, seq_size),
        out_shape=jax.ShapeDtypeStruct((requests, w_out.shape[1]), jnp.bfloat16),
        in_specs=[smem] + [vmem] * (ways + 1),
        out_specs=vmem,
        scratch_shapes=[pltpu.VMEM((requests, w_out.shape[1]), jnp.float32)],
        compiler_params=pltpu.CompilerParams(vmem_limit_bytes=16 * 2**20),
        name="project_out",
    )(me, *gather_relative(my_context, "seq", seq_size), w_out)
    mask = head_size // 2
    while mask:
        if mask > 1:
            if total.dtype != jnp.bfloat16:
                total = lax.reduce_precision(total, 8, 7).astype(jnp.bfloat16)
            other = swap(total, "head", head_size, mask)
            total = total.astype(jnp.float32) + other.astype(jnp.float32)
        else:
            total = total + swap(total, "head", head_size, mask)
        mask //= 2
    return total.astype(jnp.bfloat16)


def solution(mesh):
    seq_size, head_size = mesh.shape["seq"], mesh.shape["head"]

    def local(*args):
        return body(*args, seq_size=seq_size, head_size=head_size)

    return jax.shard_map(
        local,
        mesh=mesh,
        in_specs=(
            P(None, "seq"),
            P("seq", "head"),
            P("seq", "head"),
            P("head", "seq"),
            P("seq", None, "head"),
            P("seq", None, "head"),
            P("seq", "head"),
            P("seq", "head"),
            P(),
            P("seq"),
            P(),
        ),
        out_specs=P(None, "seq"),
        check_vma=False,
    )
```

```python
import functools
import math

import jax
import jax.numpy as jnp
from jax import lax
from jax.experimental import pallas as pl
from jax.experimental.pallas import tpu as pltpu
from jax.sharding import PartitionSpec as P

HD = 128
PAGE = 128
LANES = 128
CHUNK = 8
STAT = 16


masked_low = -1e30


def swap(x, axis, n, mask):
    return lax.ppermute(x, axis, [(j, j ^ mask) for j in range(n)])


def way_order(size):
    return [0, size - 1, *range(1, size - 1)]


def swap_all(parts, axis, n, shift):
    return [
        swap(parts[d], axis, n, d << shift) if d else parts[0] for d in way_order(len(parts))
    ]


def in_order(parts):
    return [parts[i] for i in sorted(range(len(parts)), key=way_order(len(parts)).__getitem__)]


def bit_groups(n):
    groups, shift = [], 0
    while (1 << shift) < n:
        size = min(4, n >> shift)
        groups.append((shift, size))
        shift += size.bit_length() - 1
    return groups


def lower_groups(n):
    return bit_groups(n)[:-1]


def last_group(n):
    return bit_groups(n)[-1]


def pick_digit(x, axis, shift, size, offset):
    digit = (lax.axis_index(axis) >> shift) % size
    x = x.reshape(x.shape[0] // size, size, *x.shape[1:])
    return lax.dynamic_index_in_dim(x, digit ^ offset, axis=1, keepdims=False)


def scatter_terms(parts, axis, n, beside):
    for shift, size in lower_groups(n):
        if shift:
            parts = [pick_digit(x, axis, shift, size, d) for d in range(size)]
        got = swap_all(parts, axis, n, shift)
        if shift == 0:
            got, beside = lax.optimization_barrier((got, beside))
        x = sum(got[1:], got[0])
    shift, size = last_group(n)
    return [x] + [swap(x, axis, n, d << shift) for d in range(1, size)], beside


def gather_relative(x, axis, n):
    parts = [x]
    for shift, size in reversed(lower_groups(n)):
        x = jnp.concatenate(in_order(parts), axis=0) if len(parts) > 1 else parts[0]
        parts = swap_all([x] * size, axis, n, shift)
    return parts


def relative_place(block, me, n):
    last_shift, _ = last_group(n)
    offset = me ^ block
    place, weight = block >> last_shift, n
    for shift, size in lower_groups(n):
        weight //= size
        place = place + ((offset >> shift) & (size - 1)) * weight
    return place


def gathered_blocks(me, n):
    last_shift, last_size = last_group(n)
    offsets = [0]
    for shift, size in reversed(lower_groups(n)):
        offsets = [d << shift | e for d in range(size) for e in offsets]
    low = me & ((1 << last_shift) - 1)
    return [(c << last_shift) + (low ^ e) for e in offsets for c in range(last_size)]


def table_kernel(seq_size, ways, me, counts, trim, pages, key_scale, value_scale, tables, place_of):
    requests = counts.shape[0]
    chunks = tables.shape[0] // 4
    heads = LANES // CHUNK
    mine = requests // seq_size
    page = pages[...]
    owner, first, length = [jnp.zeros_like(page)] * 3
    start = 0
    for r in range(requests):
        end = start + counts[r]
        inside = (page >= start) & (page < end)
        owner = owner + jnp.where(page >= end, 1, 0)
        first = jnp.where(inside, start, first)
        length = jnp.where(inside, PAGE * counts[r] - trim[r], length)
        start = end
    valid = length - (page - first) * PAGE
    block = owner >> (mine.bit_length() - 1)
    row = relative_place(block, me[0], seq_size) * mine + (owner & (mine - 1))
    place_of[...] = ((me[0] & (ways - 1)) << 24) + (row << 16) + owner

    chunk_slot = lax.broadcasted_iota(jnp.int32, (chunks, LANES), 1) // CHUNK
    in_chunk = chunk_slot == lax.broadcasted_iota(jnp.int32, (chunks, LANES), 0)
    slot = lax.broadcasted_iota(jnp.int32, (LANES, LANES), 0) % CHUNK
    lane = lax.broadcasted_iota(jnp.int32, (LANES, LANES), 1)
    same_slot = slot == lane // heads
    low_head = lane % heads < heads // 2

    def spread(row, to):
        rest = jnp.where(in_chunk, jnp.broadcast_to(row, (chunks, LANES)), 0.0)
        total = jnp.zeros((chunks, LANES), jnp.float32)
        for _ in range(3):
            piece = rest.astype(jnp.bfloat16)
            rest = rest - piece.astype(jnp.float32)
            total = total + jnp.dot(
                piece,
                jnp.where(to, 1.0, 0.0).astype(jnp.bfloat16),
                preferred_element_type=jnp.float32,
            )
        return total

    def by_head(scale):
        return spread(scale[0:1, :], same_slot & low_head) + spread(
            scale[1:2, :], same_slot & jnp.logical_not(low_head)
        )

    tables[:chunks, :] = by_head(key_scale) * (1.0 / math.sqrt(HD))
    tables[chunks : 2 * chunks, :] = spread(valid.astype(jnp.float32), same_slot)
    tables[2 * chunks : 3 * chunks, :] = by_head(value_scale)
    tables[3 * chunks :, :] = spread(owner.astype(jnp.float32), same_slot)


def project_kernel(ways, me, hidden, w_query, w_keyval, *refs):
    outs, (keyval_out, rows_held, query, keyval, result, sem, rows_sem) = refs[:ways], refs[ways:]
    depth = w_query.shape[0]
    tile = min(256, depth)
    copies = [
        [
            pltpu.make_async_copy(
                ref.at[pl.ds(row, tile)], held.at[pl.ds(row, tile)], sem.at[which, row // tile]
            )
            for which, (ref, held) in enumerate(((w_query, query), (w_keyval, keyval)))
        ]
        for row in range(0, depth, tile)
    ]
    rows_copy = pltpu.make_async_copy(hidden, rows_held, rows_sem)
    rows_copy.start()
    for pair in copies:
        for copy in pair:
            copy.start()
    rows_copy.wait()
    for row, pair in zip(range(0, depth, tile), copies):
        here = slice(row, row + tile)
        rows = rows_held[:, here]
        for copy, held, to in zip(pair, (query, keyval), (result, keyval_out)):
            copy.wait()
            part = jnp.dot(rows, held[here, :], preferred_element_type=jnp.float32)
            to[...] = to[...] + part if row else part
    digit = me[0] & (ways - 1)
    for d, out in enumerate(outs):
        blocks, mine, _ = out.shape
        for b in range(blocks):
            if mine % 8 == 0:
                first = (b * ways + (digit ^ d)) * mine
                out[b] = result[pl.ds(pl.multiple_of(first, mine), mine), :]
                continue
            chosen = result[b * ways * mine : (b * ways + 1) * mine, :]
            for j in range(1, ways):
                first = (b * ways + j) * mine
                chosen = jnp.where((digit ^ d) == j, result[first : first + mine, :], chosen)
            out[b] = chosen


def output_kernel(ways, seq_size, me, *refs):
    parts, (w_out, rounded, out) = refs[:ways], refs[ways:]
    rows = jnp.concatenate([part[...] for part in in_order(parts)], axis=0)
    total = jnp.dot(rows, w_out[...], preferred_element_type=jnp.float32)
    blocks = gathered_blocks(me[0], seq_size)
    mine = rows.shape[0] // len(blocks)
    if mine % 8 == 0:
        for i, block in enumerate(blocks):
            here = pl.ds(pl.multiple_of(block * mine, mine), mine)
            out[here, :] = total[i * mine : (i + 1) * mine]
        rounded[...] = out[...].astype(jnp.bfloat16)
        return
    for place in range(len(blocks)):
        chosen = total[:mine]
        for i, block in enumerate(blocks):
            chosen = jnp.where(block == place, total[i * mine : (i + 1) * mine], chosen)
        out[place * mine : (place + 1) * mine, :] = chosen
    rounded[...] = out[...].astype(jnp.bfloat16)


def join_kernel(*refs):
    *parts, out, rows = refs
    blocks, mine, columns = parts[0].shape
    held = blocks * mine
    whole = functools.reduce(jnp.add, [part[...] for part in parts]).reshape(held, columns)
    heads = columns // HD
    for h in range(heads):
        rows[pl.ds(h, held, stride=heads), :] = whole[:, h * HD : (h + 1) * HD]
    out[...] = rows[...].astype(jnp.bfloat16)


def new_rows(mine):
    return -(-4 * mine // 16) * 16


def split_stat(stat, lane):
    hi = stat.astype(jnp.bfloat16).astype(jnp.float32)
    rest = stat - hi
    mid = rest.astype(jnp.bfloat16).astype(jnp.float32)
    piece = jnp.where(lane < STAT, hi, jnp.where(lane < 2 * STAT, mid, rest - mid))
    return piece.astype(jnp.bfloat16)


def join_stat(pieces):
    pieces = pieces.astype(jnp.float32)
    return (pieces + pltpu.roll(pieces, LANES - STAT, 1)) + pltpu.roll(
        pieces, LANES - 2 * STAT, 1
    )


def attention_kernel(ways, mine, place_of, *refs):
    queries, refs = refs[:ways], refs[ways:]
    (keyval, tables, keys, values), refs = refs[:4], refs[4:]
    outs, refs = refs[:ways], refs[ways:]
    (
        query_low,
        query_high,
        probs,
        page_out,
        page_sum,
        page_max,
        dev_max,
        total_out,
        total_stat,
        keyval_rows,
    ) = refs
    slots = keys.shape[0]
    heads = LANES // CHUNK
    group = heads // 2
    chunks = slots // CHUNK
    blocks = outs[0].shape[0]
    step_chunks = 4

    for d, part in enumerate(in_order(queries)):
        rows = part[...]
        low_head = lax.broadcasted_iota(jnp.int32, rows.shape, 0) % heads < group
        zero = jnp.zeros_like(rows)
        here = slice(rows.shape[0] * d, rows.shape[0] * (d + 1))
        query_low[here, :] = jnp.where(low_head, rows, zero)
        query_high[here, :] = jnp.where(low_head, zero, rows)
    total_out[...] = jnp.zeros_like(total_out)
    stat_lane = lax.broadcasted_iota(jnp.int32, total_stat.shape, 2) % STAT
    total_stat[...] = jnp.where(stat_lane < STAT // 2, masked_low, 0.0)

    def table(which, c):
        return tables[pl.ds(which * chunks + c, 1), :]

    lane_slot = lax.broadcasted_iota(jnp.int32, (PAGE, LANES), 1) // heads
    token = lax.broadcasted_iota(jnp.int32, (PAGE, LANES), 0).astype(jnp.float32)

    def score_chunk(c):
        places = [
            pl.multiple_of(((place_of[c * CHUNK + s] >> 16) & 0xFF) * heads, heads)
            for s in range(CHUNK)
        ]
        chosen = jnp.concatenate(
            [
                jnp.concatenate([ref[pl.ds(place, heads), :] for place in places], axis=0)
                for ref in (query_low, query_high)
            ],
            axis=1,
        )
        block = keys[pl.ds(c * CHUNK, CHUNK)].reshape(CHUNK * PAGE, 2 * HD)
        every = lax.dot_general(
            block, chosen, (((1,), (1,)), ((), ())), preferred_element_type=jnp.float32
        )
        score = every[:PAGE]
        for s in range(1, CHUNK):
            score = jnp.where(lane_slot == s, every[s * PAGE : (s + 1) * PAGE], score)
        score = jnp.where(token < table(1, c), score * table(0, c), masked_low)
        top = jnp.max(score, axis=0, keepdims=True)
        page_max[pl.ds(c, 1), :] = top
        prob = jnp.exp(score - top).astype(jnp.bfloat16).astype(jnp.float32)
        page_sum[pl.ds(c, 1), :] = jnp.sum(prob, axis=0, keepdims=True)
        probs[c] = prob.T.astype(jnp.bfloat16)

    empty = jnp.zeros((heads, PAGE), jnp.bfloat16)

    def value_chunk(c):
        prob = probs[c]
        for s in range(0, CHUNK, 2):
            pair = jnp.concatenate(
                [
                    jnp.concatenate([prob[s * heads : (s + 1) * heads], empty], axis=1),
                    jnp.concatenate([empty, prob[(s + 1) * heads : (s + 2) * heads]], axis=1),
                ],
                axis=0,
            )
            block = values[pl.ds(c * CHUNK + s, 2)].reshape(2 * PAGE, 2 * HD)
            both = jnp.dot(pair, block, preferred_element_type=jnp.float32)
            page_out[pl.ds(pl.multiple_of((c * CHUNK + s) * heads, heads), 2 * heads), :] = (
                jnp.concatenate(
                    [
                        both[:group, :HD],
                        both[group:heads, HD:],
                        both[heads : heads + group, :HD],
                        both[heads + group :, HD:],
                    ],
                    axis=0,
                )
            )

    for c in range(step_chunks):
        score_chunk(c)

    @pl.loop(1, chunks // step_chunks)
    def _(step):
        first = step * step_chunks
        for c in range(step_chunks):
            value_chunk(first + c - step_chunks)
            score_chunk(first + c)

    for c in range(chunks - step_chunks, chunks):
        value_chunk(c)

    biggest, who = page_max[...], tables[3 * chunks :, :]
    best = biggest
    for turn in range(CHUNK):
        other = pltpu.roll(biggest, turn * heads, 1) if turn else biggest
        other_who = pltpu.roll(who, turn * heads, 1) if turn else who
        for c in range(chunks):
            best = jnp.maximum(
                best, jnp.where(other_who[c : c + 1] == who, other[c : c + 1], masked_low)
            )
    dev_max[...] = best

    keep_max = lax.broadcasted_iota(jnp.int32, (heads, LANES), 1) % STAT < STAT // 2

    keep_max_row = lax.broadcasted_iota(jnp.int32, (PAGE, LANES), 0) % STAT < STAT // 2

    @pl.loop(0, chunks // step_chunks)
    def _(step):
        for c in [step * step_chunks + c for c in range(step_chunks)]:
            top = dev_max[pl.ds(c, 1), :]
            weight = jnp.exp(page_max[pl.ds(c, 1), :] - top)
            out_weight = jnp.broadcast_to(weight * table(2, c), (PAGE, LANES)).T
            stat = jnp.where(keep_max_row, top, weight * page_sum[pl.ds(c, 1), :]).T
            for s in range(CHUNK):
                here = pl.ds(
                    pl.multiple_of((place_of[c * CHUNK + s] & 0xFFFF) * heads, heads), heads
                )
                there = pl.ds(pl.multiple_of((c * CHUNK + s) * heads, heads), heads)
                part = slice(s * heads, (s + 1) * heads)
                turn = s % 2
                total_out[turn, here, :] += page_out[there, :] * out_weight[part]
                total_stat[turn, here, :] = jnp.where(
                    keep_max, stat[part], total_stat[turn, here, :] + stat[part]
                )

    lane = lax.broadcasted_iota(jnp.int32, (heads, LANES), 1)
    digit = place_of[0] >> 24
    for j in range(4):
        keyval_rows[pl.ds(j, keyval.shape[0], stride=4), :] = keyval[:, j * HD : (j + 1) * HD]
    for d, out in enumerate(outs):
        for b in range(blocks):
            block = b * ways + (digit ^ d)
            rows = pl.ds(pl.multiple_of(block * (mine * heads), mine * heads), mine * heads)
            out[b, : mine * heads, :] = (total_out[0, rows, :] + total_out[1, rows, :]).astype(
                jnp.bfloat16
            )
            even, odd = total_stat[0, rows, :], total_stat[1, rows, :]
            is_max = lax.broadcasted_iota(jnp.int32, even.shape, 1) % STAT < STAT // 2
            both = jnp.where(is_max, jnp.maximum(even, odd), even + odd)
            stat = jnp.zeros((heads, LANES), jnp.float32)
            for r in range(mine):
                stat = jnp.where(
                    lane % (STAT // 2) == r, both[r * heads : (r + 1) * heads], stat
                )
            out[b, mine * heads : (mine + 1) * heads, :] = split_stat(stat, lane)
            new = keyval_rows[pl.ds(pl.multiple_of(block * (4 * mine), 4 * mine), 4 * mine), :]
            if new.shape[0] < new_rows(mine):
                empty_rows = jnp.zeros((new_rows(mine) - new.shape[0], LANES), jnp.float32)
                new = jnp.concatenate([new, empty_rows], axis=0)
            out[b, (mine + 1) * heads :, :] = new.astype(jnp.bfloat16)


def combine_kernel(mine, *refs):
    *parts, out = refs
    blocks = out.shape[0]
    heads = LANES // CHUNK
    lane = lax.broadcasted_iota(jnp.int32, (heads, LANES), 1)
    for b in range(blocks):
        stats = [join_stat(part[b, mine * heads : (mine + 1) * heads, :]) for part in parts]
        maxima = [jnp.where(lane < mine, stat, 0.0) for stat in stats]
        top = functools.reduce(jnp.maximum, maxima)
        factors = [jnp.exp(m - top) for m in maxima]
        sums = sum(
            pltpu.roll(f, STAT // 2, 1) * jnp.where(lane < STAT, stat, 0.0)
            for f, stat in zip(factors, stats)
        )
        both = jnp.where(lane < STAT // 2, top, sums)
        both = jnp.where(lane < STAT, both, 0.0)
        both = (both + pltpu.roll(both, STAT, 1)) + pltpu.roll(both, 2 * STAT, 1)
        out[b, mine * heads : (mine + 1) * heads, :] = split_stat(both, lane)
        new = sum(part[b, (mine + 1) * heads :, :].astype(jnp.float32) for part in parts)
        out[b, (mine + 1) * heads :, :] = new.astype(jnp.bfloat16)
        for r in range(mine):
            rows = slice(r * heads, (r + 1) * heads)
            numer = sum(
                f[:, r : r + 1] * part[b, rows, :].astype(jnp.float32)
                for f, part in zip(factors, parts)
            )
            out[b, rows, :] = numer.astype(jnp.bfloat16)


def finish_kernel(mine, *refs):
    *parts, query, out, numers = refs
    blocks = parts[0].shape[0]
    heads = LANES // CHUNK
    group = heads // 2
    lane = lax.broadcasted_iota(jnp.int32, (heads, LANES), 1)
    low_head = lax.broadcasted_iota(jnp.int32, (heads, LANES), 0) < group
    def spread(new, r, which):
        low = jnp.broadcast_to(new[4 * r + which : 4 * r + which + 1], (heads, LANES))
        high = jnp.broadcast_to(new[4 * r + 2 + which : 4 * r + 3 + which], (heads, LANES))
        return jnp.where(low_head, low, high)

    for b in range(blocks):
        new = sum(part[b, (mine + 1) * heads :, :].astype(jnp.float32) for part in parts)
        new = new.astype(jnp.bfloat16).astype(jnp.float32)
        own = jnp.zeros((heads, LANES), jnp.float32)
        for r in range(mine):
            request = b * mine + r
            rows = query[request * heads : (request + 1) * heads, :].astype(jnp.float32)
            dot = jnp.sum(rows * spread(new, r, 0), axis=1, keepdims=True)
            own = jnp.where(lane == r, dot * (1.0 / math.sqrt(HD)), own)
        maxima, sums = [], []
        for part in parts:
            whole = join_stat(part[b, mine * heads : (mine + 1) * heads, :])
            maxima.append(jnp.where(lane < mine, whole, 0.0))
            sums.append(jnp.where(lane < mine, pltpu.roll(whole, LANES - STAT // 2, 1), 0.0))
        top = functools.reduce(jnp.maximum, maxima, own)
        fresh = jnp.exp(own - top)
        factors = [jnp.exp(m - top) for m in maxima]
        denom = sum((s * f for s, f in zip(sums, factors)), fresh)
        fresh = fresh / denom
        factors = [f / denom for f in factors]
        for r in range(mine):
            numer = fresh[:, r : r + 1] * spread(new, r, 1)
            for part, f in zip(parts, factors):
                rows = part[b, r * heads : (r + 1) * heads, :].astype(jnp.float32)
                numer = numer + f[:, r : r + 1] * rows
            request = b * mine + r
            numers[request * heads : (request + 1) * heads, :] = numer
    for h in range(heads):
        out[:, h * HD : (h + 1) * HD] = numers[
            pl.ds(h, blocks * mine, stride=heads), :
        ].astype(jnp.bfloat16)


def body(
    hidden_in,
    w_query,
    w_keyval,
    w_out,
    key_cache,
    value_cache,
    key_scale,
    value_scale,
    page_counts,
    slot_pages,
    trim,
    seq_size,
    head_size,
):
    requests = hidden_in.shape[0]
    slots = key_cache.shape[0]
    kv_local = w_keyval.shape[1] // (2 * HD)
    heads_local = w_query.shape[1] // HD
    wide = heads_local * HD
    group = heads_local // kv_local
    assert kv_local == 2 and heads_local * CHUNK == LANES
    assert slots % CHUNK == 0
    mine = requests // seq_size
    inverse_square_root = 1.0 / math.sqrt(HD)

    assert slots == LANES and mine & (mine - 1) == 0
    ways = lower_groups(seq_size)[0][1]
    chunks = slots // CHUNK
    smem = pl.BlockSpec(memory_space=pltpu.SMEM)
    vmem = pl.BlockSpec(memory_space=pltpu.VMEM)
    hbm = pl.BlockSpec(memory_space=pl.ANY)
    small = pltpu.CompilerParams(vmem_limit_bytes=6 * 2**20)
    me = lax.axis_index("seq").reshape(1)

    def in_hbm(x):
        return pltpu.with_memory_space_constraint(x, pltpu.HBM)

    tables, place_of = pl.pallas_call(
        functools.partial(table_kernel, seq_size, ways),
        out_shape=[
            jax.ShapeDtypeStruct((4 * chunks, LANES), jnp.float32),
            jax.ShapeDtypeStruct((1, slots), jnp.int32),
        ],
        in_specs=[smem, smem, smem, vmem, vmem, vmem],
        out_specs=[vmem, vmem],
        compiler_params=small,
        name="page_table",
    )(me, page_counts, trim, slot_pages.reshape(1, slots), key_scale.T, value_scale.T)
    place_of = place_of.reshape(slots)

    held = last_group(seq_size)[1] * mine
    part_shape = jax.ShapeDtypeStruct((seq_size // ways, mine, wide), jnp.float32)
    keyval_shape = jax.ShapeDtypeStruct((requests, w_keyval.shape[1]), jnp.float32)
    *parts, keyval = pl.pallas_call(
        functools.partial(project_kernel, ways),
        out_shape=[part_shape] * ways + [keyval_shape],
        in_specs=[smem, hbm, hbm, hbm],
        out_specs=[vmem] * (ways + 1),
        scratch_shapes=[
            pltpu.VMEM(hidden_in.shape, jnp.bfloat16),
            pltpu.VMEM(w_query.shape, jnp.bfloat16),
            pltpu.VMEM(w_keyval.shape, jnp.bfloat16),
            pltpu.VMEM((requests, wide), jnp.float32),
            pltpu.SemaphoreType.DMA((2, pl.cdiv(w_query.shape[0], 256))),
            pltpu.SemaphoreType.DMA,
        ],
        compiler_params=pltpu.CompilerParams(vmem_limit_bytes=53 * 2**20),
        name="project",
    )(me, in_hbm(hidden_in), in_hbm(w_query), in_hbm(w_keyval))
    terms, (tables, place_of) = scatter_terms(parts, "seq", seq_size, (tables, place_of))
    my_query = pl.pallas_call(
        join_kernel,
        out_shape=jax.ShapeDtypeStruct((held * heads_local, HD), jnp.bfloat16),
        in_specs=[vmem] * len(terms),
        out_specs=vmem,
        scratch_shapes=[pltpu.VMEM((held * heads_local, HD), jnp.float32)],
        compiler_params=small,
        cost_estimate=pl.CostEstimate(flops=10**10, bytes_accessed=10**7, transcendentals=0),
        name="join",
    )(*terms)
    query = gather_relative(my_query, "seq", seq_size)

    every_row = requests * heads_local
    block_rows = (mine + 1) * heads_local + new_rows(mine)
    totals = pl.pallas_call(
        functools.partial(attention_kernel, ways, mine),
        out_shape=[jax.ShapeDtypeStruct((seq_size // ways, block_rows, HD), jnp.bfloat16)] * ways,
        in_specs=[smem] + [vmem] * (ways + 4),
        out_specs=[vmem] * ways,
        scratch_shapes=[
            pltpu.VMEM((every_row, HD), jnp.bfloat16),
            pltpu.VMEM((every_row, HD), jnp.bfloat16),
            pltpu.VMEM((chunks, LANES, PAGE), jnp.bfloat16),
            pltpu.VMEM((slots * heads_local, HD), jnp.float32),
            pltpu.VMEM((chunks, LANES), jnp.float32),
            pltpu.VMEM((chunks, LANES), jnp.float32),
            pltpu.VMEM((chunks, LANES), jnp.float32),
            pltpu.VMEM((2, every_row, HD), jnp.float32),
            pltpu.VMEM((2, every_row, HD), jnp.float32),
            pltpu.VMEM((requests * 2 * kv_local, HD), jnp.float32),
        ],
        compiler_params=pltpu.CompilerParams(vmem_limit_bytes=24 * 2**20),
        cost_estimate=pl.CostEstimate(
            flops=4 * slots * PAGE * wide,
            bytes_accessed=2 * (key_cache.size + value_cache.size),
            transcendentals=slots * PAGE * heads_local,
        ),
        name="paged_attention",
    )(place_of, *query, keyval, tables, key_cache, value_cache)

    for shift, size in lower_groups(seq_size):
        if shift:
            totals = [pick_digit(totals, "seq", shift, size, d) for d in range(size)]
        parts = swap_all(totals, "seq", seq_size, shift)
        totals = pl.pallas_call(
            functools.partial(combine_kernel, mine),
            out_shape=jax.ShapeDtypeStruct(parts[0].shape, jnp.bfloat16),
            in_specs=[vmem] * size,
            out_specs=vmem,
            compiler_params=pltpu.CompilerParams(vmem_limit_bytes=6 * 2**20),
            name="combine",
        )(*parts)
    shift, size = last_group(seq_size)
    parts = [totals] + [swap(totals, "seq", seq_size, d << shift) for d in range(1, size)]
    my_context = pl.pallas_call(
        functools.partial(finish_kernel, mine),
        out_shape=jax.ShapeDtypeStruct((held, wide), jnp.bfloat16),
        in_specs=[vmem] * (size + 1),
        out_specs=vmem,
        scratch_shapes=[pltpu.VMEM((held * heads_local, HD), jnp.float32)],
        compiler_params=pltpu.CompilerParams(vmem_limit_bytes=6 * 2**20),
        name="finish",
    )(*parts, my_query)

    total = pl.pallas_call(
        functools.partial(output_kernel, ways, seq_size),
        out_shape=jax.ShapeDtypeStruct((requests, w_out.shape[1]), jnp.bfloat16),
        in_specs=[smem] + [vmem] * (ways + 1),
        out_specs=vmem,
        scratch_shapes=[pltpu.VMEM((requests, w_out.shape[1]), jnp.float32)],
        compiler_params=pltpu.CompilerParams(vmem_limit_bytes=16 * 2**20),
        name="project_out",
    )(me, *gather_relative(my_context, "seq", seq_size), w_out)
    mask = head_size // 2
    while mask:
        if mask > 1:
            if total.dtype != jnp.bfloat16:
                total = lax.reduce_precision(total, 8, 7).astype(jnp.bfloat16)
            other = swap(total, "head", head_size, mask)
            total = total.astype(jnp.float32) + other.astype(jnp.float32)
        else:
            total = total + swap(total, "head", head_size, mask)
        mask //= 2
    return total.astype(jnp.bfloat16)


def solution(mesh):
    seq_size, head_size = mesh.shape["seq"], mesh.shape["head"]

    def local(*args):
        return body(*args, seq_size=seq_size, head_size=head_size)

    return jax.shard_map(
        local,
        mesh=mesh,
        in_specs=(
            P(None, "seq"),
            P("seq", "head"),
            P("seq", "head"),
            P("head", "seq"),
            P("seq", None, "head"),
            P("seq", None, "head"),
            P("seq", "head"),
            P("seq", "head"),
            P(),
            P("seq"),
            P(),
        ),
        out_specs=P(None, "seq"),
        check_vma=False,
    )
```

```python
import functools
import math

import jax
import jax.numpy as jnp
from jax import lax
from jax.experimental import pallas as pl
from jax.experimental.pallas import tpu as pltpu
from jax.sharding import PartitionSpec as P

HD = 128
PAGE = 128
LANES = 128
CHUNK = 8
STAT = 16


masked_low = -1e30


def swap(x, axis, n, mask):
    return lax.ppermute(x, axis, [(j, j ^ mask) for j in range(n)])


def way_order(size):
    return [0, size - 1, *range(1, size - 1)]


def swap_all(parts, axis, n, shift):
    return [
        swap(parts[d], axis, n, d << shift) if d else parts[0] for d in way_order(len(parts))
    ]


def in_order(parts):
    return [parts[i] for i in sorted(range(len(parts)), key=way_order(len(parts)).__getitem__)]


def bit_groups(n):
    groups, shift = [], 0
    while (1 << shift) < n:
        size = min(4, n >> shift)
        groups.append((shift, size))
        shift += size.bit_length() - 1
    return groups


def lower_groups(n):
    return bit_groups(n)[:-1]


def last_group(n):
    return bit_groups(n)[-1]


def pick_digit(x, axis, shift, size, offset):
    digit = (lax.axis_index(axis) >> shift) % size
    x = x.reshape(x.shape[0] // size, size, *x.shape[1:])
    return lax.dynamic_index_in_dim(x, digit ^ offset, axis=1, keepdims=False)


def scatter_terms(parts, axis, n, beside):
    for shift, size in lower_groups(n):
        if shift:
            parts = [pick_digit(x, axis, shift, size, d) for d in range(size)]
        got = swap_all(parts, axis, n, shift)
        if shift == 0:
            got, beside = lax.optimization_barrier((got, beside))
        x = sum(got[1:], got[0])
    shift, size = last_group(n)
    return [x] + [swap(x, axis, n, d << shift) for d in range(1, size)], beside


def gather_relative(x, axis, n):
    parts = [x]
    for shift, size in reversed(lower_groups(n)):
        x = jnp.concatenate(in_order(parts), axis=0) if len(parts) > 1 else parts[0]
        parts = swap_all([x] * size, axis, n, shift)
    return parts


def relative_place(block, me, n):
    last_shift, _ = last_group(n)
    offset = me ^ block
    place, weight = block >> last_shift, n
    for shift, size in lower_groups(n):
        weight //= size
        place = place + ((offset >> shift) & (size - 1)) * weight
    return place


def gathered_blocks(me, n):
    last_shift, last_size = last_group(n)
    offsets = [0]
    for shift, size in reversed(lower_groups(n)):
        offsets = [d << shift | e for d in range(size) for e in offsets]
    low = me & ((1 << last_shift) - 1)
    return [(c << last_shift) + (low ^ e) for e in offsets for c in range(last_size)]


def table_kernel(seq_size, ways, me, counts, trim, pages, key_scale, value_scale, tables, place_of):
    requests = counts.shape[0]
    chunks = tables.shape[0] // 4
    heads = LANES // CHUNK
    mine = requests // seq_size
    page = pages[...]
    owner, first, length = [jnp.zeros_like(page)] * 3
    start = 0
    for r in range(requests):
        end = start + counts[r]
        inside = (page >= start) & (page < end)
        owner = owner + jnp.where(page >= end, 1, 0)
        first = jnp.where(inside, start, first)
        length = jnp.where(inside, PAGE * counts[r] - trim[r], length)
        start = end
    valid = length - (page - first) * PAGE
    block = owner >> (mine.bit_length() - 1)
    row = relative_place(block, me[0], seq_size) * mine + (owner & (mine - 1))
    place_of[...] = ((me[0] & (ways - 1)) << 24) + (row << 16) + owner

    chunk_slot = lax.broadcasted_iota(jnp.int32, (chunks, LANES), 1) // CHUNK
    in_chunk = chunk_slot == lax.broadcasted_iota(jnp.int32, (chunks, LANES), 0)
    slot = lax.broadcasted_iota(jnp.int32, (LANES, LANES), 0) % CHUNK
    lane = lax.broadcasted_iota(jnp.int32, (LANES, LANES), 1)
    same_slot = slot == lane // heads
    low_head = lane % heads < heads // 2

    def spread(row, to):
        rest = jnp.where(in_chunk, jnp.broadcast_to(row, (chunks, LANES)), 0.0)
        total = jnp.zeros((chunks, LANES), jnp.float32)
        for _ in range(3):
            piece = rest.astype(jnp.bfloat16)
            rest = rest - piece.astype(jnp.float32)
            total = total + jnp.dot(
                piece,
                jnp.where(to, 1.0, 0.0).astype(jnp.bfloat16),
                preferred_element_type=jnp.float32,
            )
        return total

    def by_head(scale):
        return spread(scale[0:1, :], same_slot & low_head) + spread(
            scale[1:2, :], same_slot & jnp.logical_not(low_head)
        )

    tables[:chunks, :] = by_head(key_scale) * (1.0 / math.sqrt(HD))
    tables[chunks : 2 * chunks, :] = spread(valid.astype(jnp.float32), same_slot)
    tables[2 * chunks : 3 * chunks, :] = by_head(value_scale)
    tables[3 * chunks :, :] = spread(owner.astype(jnp.float32), same_slot)


def project_kernel(ways, me, hidden, w_query, w_keyval, *refs):
    outs, (keyval_out, rows_held, query, keyval, result, sem, rows_sem) = refs[:ways], refs[ways:]
    depth = w_query.shape[0]
    tile = min(256, depth)
    copies = [
        [
            pltpu.make_async_copy(
                ref.at[pl.ds(row, tile)], held.at[pl.ds(row, tile)], sem.at[which, row // tile]
            )
            for which, (ref, held) in enumerate(((w_query, query), (w_keyval, keyval)))
        ]
        for row in range(0, depth, tile)
    ]
    rows_copy = pltpu.make_async_copy(hidden, rows_held, rows_sem)
    rows_copy.start()
    for pair in copies:
        for copy in pair:
            copy.start()
    rows_copy.wait()
    for row, pair in zip(range(0, depth, tile), copies):
        here = slice(row, row + tile)
        rows = rows_held[:, here]
        for copy, held, to in zip(pair, (query, keyval), (result, keyval_out)):
            copy.wait()
            part = jnp.dot(rows, held[here, :], preferred_element_type=jnp.float32)
            to[...] = to[...] + part if row else part
    digit = me[0] & (ways - 1)
    for d, out in enumerate(outs):
        blocks, mine, _ = out.shape
        for b in range(blocks):
            if mine % 8 == 0:
                first = (b * ways + (digit ^ d)) * mine
                out[b] = result[pl.ds(pl.multiple_of(first, mine), mine), :]
                continue
            chosen = result[b * ways * mine : (b * ways + 1) * mine, :]
            for j in range(1, ways):
                first = (b * ways + j) * mine
                chosen = jnp.where((digit ^ d) == j, result[first : first + mine, :], chosen)
            out[b] = chosen


def output_kernel(ways, seq_size, me, *refs):
    parts, (w_out, rounded, out) = refs[:ways], refs[ways:]
    rows = jnp.concatenate([part[...] for part in in_order(parts)], axis=0)
    total = jnp.dot(rows, w_out[...], preferred_element_type=jnp.float32)
    blocks = gathered_blocks(me[0], seq_size)
    mine = rows.shape[0] // len(blocks)
    if mine % 8 == 0:
        for i, block in enumerate(blocks):
            here = pl.ds(pl.multiple_of(block * mine, mine), mine)
            out[here, :] = total[i * mine : (i + 1) * mine]
        rounded[...] = out[...].astype(jnp.bfloat16)
        return
    for place in range(len(blocks)):
        chosen = total[:mine]
        for i, block in enumerate(blocks):
            chosen = jnp.where(block == place, total[i * mine : (i + 1) * mine], chosen)
        out[place * mine : (place + 1) * mine, :] = chosen
    rounded[...] = out[...].astype(jnp.bfloat16)


def join_kernel(*refs):
    *parts, out, rows = refs
    blocks, mine, columns = parts[0].shape
    held = blocks * mine
    whole = functools.reduce(jnp.add, [part[...] for part in parts]).reshape(held, columns)
    heads = columns // HD
    for h in range(heads):
        rows[pl.ds(h, held, stride=heads), :] = whole[:, h * HD : (h + 1) * HD]
    out[...] = rows[...].astype(jnp.bfloat16)


def new_rows(mine):
    return -(-4 * mine // 16) * 16


def split_stat(stat, lane):
    hi = stat.astype(jnp.bfloat16).astype(jnp.float32)
    rest = stat - hi
    mid = rest.astype(jnp.bfloat16).astype(jnp.float32)
    piece = jnp.where(lane < STAT, hi, jnp.where(lane < 2 * STAT, mid, rest - mid))
    return piece.astype(jnp.bfloat16)


def join_stat(pieces):
    pieces = pieces.astype(jnp.float32)
    return (pieces + pltpu.roll(pieces, LANES - STAT, 1)) + pltpu.roll(
        pieces, LANES - 2 * STAT, 1
    )


def attention_kernel(ways, mine, place_of, *refs):
    queries, refs = refs[:ways], refs[ways:]
    (keyval, tables, keys, values), refs = refs[:4], refs[4:]
    outs, refs = refs[:ways], refs[ways:]
    (
        query_low,
        query_high,
        probs,
        page_out,
        page_sum,
        page_max,
        dev_max,
        total_out,
        total_stat,
        keyval_rows,
    ) = refs
    slots = keys.shape[0]
    heads = LANES // CHUNK
    group = heads // 2
    chunks = slots // CHUNK
    blocks = outs[0].shape[0]
    step_chunks = 8

    for d, part in enumerate(in_order(queries)):
        rows = part[...]
        low_head = lax.broadcasted_iota(jnp.int32, rows.shape, 0) % heads < group
        zero = jnp.zeros_like(rows)
        here = slice(rows.shape[0] * d, rows.shape[0] * (d + 1))
        query_low[here, :] = jnp.where(low_head, rows, zero)
        query_high[here, :] = jnp.where(low_head, zero, rows)
    total_out[...] = jnp.zeros_like(total_out)
    stat_lane = lax.broadcasted_iota(jnp.int32, total_stat.shape, 2) % STAT
    total_stat[...] = jnp.where(stat_lane < STAT // 2, masked_low, 0.0)

    def table(which, c):
        return tables[pl.ds(which * chunks + c, 1), :]

    lane_slot = lax.broadcasted_iota(jnp.int32, (PAGE, LANES), 1) // heads
    token = lax.broadcasted_iota(jnp.int32, (PAGE, LANES), 0).astype(jnp.float32)

    def score_chunk(c):
        places = [
            pl.multiple_of(((place_of[c * CHUNK + s] >> 16) & 0xFF) * heads, heads)
            for s in range(CHUNK)
        ]
        chosen = jnp.concatenate(
            [
                jnp.concatenate([ref[pl.ds(place, heads), :] for place in places], axis=0)
                for ref in (query_low, query_high)
            ],
            axis=1,
        )
        block = keys[pl.ds(c * CHUNK, CHUNK)].reshape(CHUNK * PAGE, 2 * HD)
        every = lax.dot_general(
            block, chosen, (((1,), (1,)), ((), ())), preferred_element_type=jnp.float32
        )
        score = every[:PAGE]
        for s in range(1, CHUNK):
            score = jnp.where(lane_slot == s, every[s * PAGE : (s + 1) * PAGE], score)
        score = jnp.where(token < table(1, c), score * table(0, c), masked_low)
        top = jnp.max(score, axis=0, keepdims=True)
        page_max[pl.ds(c, 1), :] = top
        prob = jnp.exp(score - top).astype(jnp.bfloat16).astype(jnp.float32)
        page_sum[pl.ds(c, 1), :] = jnp.sum(prob, axis=0, keepdims=True)
        probs[c] = prob.T.astype(jnp.bfloat16)

    empty = jnp.zeros((heads, PAGE), jnp.bfloat16)

    def value_chunk(c):
        prob = probs[c]
        for s in range(0, CHUNK, 2):
            pair = jnp.concatenate(
                [
                    jnp.concatenate([prob[s * heads : (s + 1) * heads], empty], axis=1),
                    jnp.concatenate([empty, prob[(s + 1) * heads : (s + 2) * heads]], axis=1),
                ],
                axis=0,
            )
            block = values[pl.ds(c * CHUNK + s, 2)].reshape(2 * PAGE, 2 * HD)
            both = jnp.dot(pair, block, preferred_element_type=jnp.float32)
            page_out[pl.ds(pl.multiple_of((c * CHUNK + s) * heads, heads), 2 * heads), :] = (
                jnp.concatenate(
                    [
                        both[:group, :HD],
                        both[group:heads, HD:],
                        both[heads : heads + group, :HD],
                        both[heads + group :, HD:],
                    ],
                    axis=0,
                )
            )

    for c in range(step_chunks):
        score_chunk(c)

    @pl.loop(1, chunks // step_chunks)
    def _(step):
        first = step * step_chunks
        for c in range(step_chunks):
            value_chunk(first + c - step_chunks)
            score_chunk(first + c)

    for c in range(chunks - step_chunks, chunks):
        value_chunk(c)

    biggest, who = page_max[...], tables[3 * chunks :, :]
    best = biggest
    for turn in range(CHUNK):
        other = pltpu.roll(biggest, turn * heads, 1) if turn else biggest
        other_who = pltpu.roll(who, turn * heads, 1) if turn else who
        for c in range(chunks):
            best = jnp.maximum(
                best, jnp.where(other_who[c : c + 1] == who, other[c : c + 1], masked_low)
            )
    dev_max[...] = best

    keep_max = lax.broadcasted_iota(jnp.int32, (heads, LANES), 1) % STAT < STAT // 2

    keep_max_row = lax.broadcasted_iota(jnp.int32, (PAGE, LANES), 0) % STAT < STAT // 2

    @pl.loop(0, chunks // step_chunks)
    def _(step):
        for c in [step * step_chunks + c for c in range(step_chunks)]:
            top = dev_max[pl.ds(c, 1), :]
            weight = jnp.exp(page_max[pl.ds(c, 1), :] - top)
            out_weight = jnp.broadcast_to(weight * table(2, c), (PAGE, LANES)).T
            stat = jnp.where(keep_max_row, top, weight * page_sum[pl.ds(c, 1), :]).T
            for s in range(CHUNK):
                here = pl.ds(
                    pl.multiple_of((place_of[c * CHUNK + s] & 0xFFFF) * heads, heads), heads
                )
                there = pl.ds(pl.multiple_of((c * CHUNK + s) * heads, heads), heads)
                part = slice(s * heads, (s + 1) * heads)
                turn = s % 2
                total_out[turn, here, :] += page_out[there, :] * out_weight[part]
                total_stat[turn, here, :] = jnp.where(
                    keep_max, stat[part], total_stat[turn, here, :] + stat[part]
                )

    lane = lax.broadcasted_iota(jnp.int32, (heads, LANES), 1)
    digit = place_of[0] >> 24
    for j in range(4):
        keyval_rows[pl.ds(j, keyval.shape[0], stride=4), :] = keyval[:, j * HD : (j + 1) * HD]
    for d, out in enumerate(outs):
        for b in range(blocks):
            block = b * ways + (digit ^ d)
            rows = pl.ds(pl.multiple_of(block * (mine * heads), mine * heads), mine * heads)
            out[b, : mine * heads, :] = (total_out[0, rows, :] + total_out[1, rows, :]).astype(
                jnp.bfloat16
            )
            even, odd = total_stat[0, rows, :], total_stat[1, rows, :]
            is_max = lax.broadcasted_iota(jnp.int32, even.shape, 1) % STAT < STAT // 2
            both = jnp.where(is_max, jnp.maximum(even, odd), even + odd)
            stat = jnp.zeros((heads, LANES), jnp.float32)
            for r in range(mine):
                stat = jnp.where(
                    lane % (STAT // 2) == r, both[r * heads : (r + 1) * heads], stat
                )
            out[b, mine * heads : (mine + 1) * heads, :] = split_stat(stat, lane)
            new = keyval_rows[pl.ds(pl.multiple_of(block * (4 * mine), 4 * mine), 4 * mine), :]
            if new.shape[0] < new_rows(mine):
                empty_rows = jnp.zeros((new_rows(mine) - new.shape[0], LANES), jnp.float32)
                new = jnp.concatenate([new, empty_rows], axis=0)
            out[b, (mine + 1) * heads :, :] = new.astype(jnp.bfloat16)


def combine_kernel(mine, *refs):
    *parts, out = refs
    blocks = out.shape[0]
    heads = LANES // CHUNK
    lane = lax.broadcasted_iota(jnp.int32, (heads, LANES), 1)
    for b in range(blocks):
        stats = [join_stat(part[b, mine * heads : (mine + 1) * heads, :]) for part in parts]
        maxima = [jnp.where(lane < mine, stat, 0.0) for stat in stats]
        top = functools.reduce(jnp.maximum, maxima)
        factors = [jnp.exp(m - top) for m in maxima]
        sums = sum(
            pltpu.roll(f, STAT // 2, 1) * jnp.where(lane < STAT, stat, 0.0)
            for f, stat in zip(factors, stats)
        )
        both = jnp.where(lane < STAT // 2, top, sums)
        both = jnp.where(lane < STAT, both, 0.0)
        both = (both + pltpu.roll(both, STAT, 1)) + pltpu.roll(both, 2 * STAT, 1)
        out[b, mine * heads : (mine + 1) * heads, :] = split_stat(both, lane)
        new = sum(part[b, (mine + 1) * heads :, :].astype(jnp.float32) for part in parts)
        out[b, (mine + 1) * heads :, :] = new.astype(jnp.bfloat16)
        for r in range(mine):
            rows = slice(r * heads, (r + 1) * heads)
            numer = sum(
                f[:, r : r + 1] * part[b, rows, :].astype(jnp.float32)
                for f, part in zip(factors, parts)
            )
            out[b, rows, :] = numer.astype(jnp.bfloat16)


def finish_kernel(mine, *refs):
    *parts, query, out, numers = refs
    blocks = parts[0].shape[0]
    heads = LANES // CHUNK
    group = heads // 2
    lane = lax.broadcasted_iota(jnp.int32, (heads, LANES), 1)
    low_head = lax.broadcasted_iota(jnp.int32, (heads, LANES), 0) < group
    def spread(new, r, which):
        low = jnp.broadcast_to(new[4 * r + which : 4 * r + which + 1], (heads, LANES))
        high = jnp.broadcast_to(new[4 * r + 2 + which : 4 * r + 3 + which], (heads, LANES))
        return jnp.where(low_head, low, high)

    for b in range(blocks):
        new = sum(part[b, (mine + 1) * heads :, :].astype(jnp.float32) for part in parts)
        new = new.astype(jnp.bfloat16).astype(jnp.float32)
        own = jnp.zeros((heads, LANES), jnp.float32)
        for r in range(mine):
            request = b * mine + r
            rows = query[request * heads : (request + 1) * heads, :].astype(jnp.float32)
            dot = jnp.sum(rows * spread(new, r, 0), axis=1, keepdims=True)
            own = jnp.where(lane == r, dot * (1.0 / math.sqrt(HD)), own)
        maxima, sums = [], []
        for part in parts:
            whole = join_stat(part[b, mine * heads : (mine + 1) * heads, :])
            maxima.append(jnp.where(lane < mine, whole, 0.0))
            sums.append(jnp.where(lane < mine, pltpu.roll(whole, LANES - STAT // 2, 1), 0.0))
        top = functools.reduce(jnp.maximum, maxima, own)
        fresh = jnp.exp(own - top)
        factors = [jnp.exp(m - top) for m in maxima]
        denom = sum((s * f for s, f in zip(sums, factors)), fresh)
        fresh = fresh / denom
        factors = [f / denom for f in factors]
        for r in range(mine):
            numer = fresh[:, r : r + 1] * spread(new, r, 1)
            for part, f in zip(parts, factors):
                rows = part[b, r * heads : (r + 1) * heads, :].astype(jnp.float32)
                numer = numer + f[:, r : r + 1] * rows
            request = b * mine + r
            numers[request * heads : (request + 1) * heads, :] = numer
    for h in range(heads):
        out[:, h * HD : (h + 1) * HD] = numers[
            pl.ds(h, blocks * mine, stride=heads), :
        ].astype(jnp.bfloat16)


def body(
    hidden_in,
    w_query,
    w_keyval,
    w_out,
    key_cache,
    value_cache,
    key_scale,
    value_scale,
    page_counts,
    slot_pages,
    trim,
    seq_size,
    head_size,
):
    requests = hidden_in.shape[0]
    slots = key_cache.shape[0]
    kv_local = w_keyval.shape[1] // (2 * HD)
    heads_local = w_query.shape[1] // HD
    wide = heads_local * HD
    group = heads_local // kv_local
    assert kv_local == 2 and heads_local * CHUNK == LANES
    assert slots % CHUNK == 0
    mine = requests // seq_size
    inverse_square_root = 1.0 / math.sqrt(HD)

    assert slots == LANES and mine & (mine - 1) == 0
    ways = lower_groups(seq_size)[0][1]
    chunks = slots // CHUNK
    smem = pl.BlockSpec(memory_space=pltpu.SMEM)
    vmem = pl.BlockSpec(memory_space=pltpu.VMEM)
    hbm = pl.BlockSpec(memory_space=pl.ANY)
    small = pltpu.CompilerParams(vmem_limit_bytes=6 * 2**20)
    me = lax.axis_index("seq").reshape(1)

    def in_hbm(x):
        return pltpu.with_memory_space_constraint(x, pltpu.HBM)

    tables, place_of = pl.pallas_call(
        functools.partial(table_kernel, seq_size, ways),
        out_shape=[
            jax.ShapeDtypeStruct((4 * chunks, LANES), jnp.float32),
            jax.ShapeDtypeStruct((1, slots), jnp.int32),
        ],
        in_specs=[smem, smem, smem, vmem, vmem, vmem],
        out_specs=[vmem, vmem],
        compiler_params=small,
        name="page_table",
    )(me, page_counts, trim, slot_pages.reshape(1, slots), key_scale.T, value_scale.T)
    place_of = place_of.reshape(slots)

    held = last_group(seq_size)[1] * mine
    part_shape = jax.ShapeDtypeStruct((seq_size // ways, mine, wide), jnp.float32)
    keyval_shape = jax.ShapeDtypeStruct((requests, w_keyval.shape[1]), jnp.float32)
    *parts, keyval = pl.pallas_call(
        functools.partial(project_kernel, ways),
        out_shape=[part_shape] * ways + [keyval_shape],
        in_specs=[smem, hbm, hbm, hbm],
        out_specs=[vmem] * (ways + 1),
        scratch_shapes=[
            pltpu.VMEM(hidden_in.shape, jnp.bfloat16),
            pltpu.VMEM(w_query.shape, jnp.bfloat16),
            pltpu.VMEM(w_keyval.shape, jnp.bfloat16),
            pltpu.VMEM((requests, wide), jnp.float32),
            pltpu.SemaphoreType.DMA((2, pl.cdiv(w_query.shape[0], 256))),
            pltpu.SemaphoreType.DMA,
        ],
        compiler_params=pltpu.CompilerParams(vmem_limit_bytes=53 * 2**20),
        name="project",
    )(me, in_hbm(hidden_in), in_hbm(w_query), in_hbm(w_keyval))
    terms, (tables, place_of) = scatter_terms(parts, "seq", seq_size, (tables, place_of))
    my_query = pl.pallas_call(
        join_kernel,
        out_shape=jax.ShapeDtypeStruct((held * heads_local, HD), jnp.bfloat16),
        in_specs=[vmem] * len(terms),
        out_specs=vmem,
        scratch_shapes=[pltpu.VMEM((held * heads_local, HD), jnp.float32)],
        compiler_params=small,
        cost_estimate=pl.CostEstimate(flops=10**10, bytes_accessed=10**7, transcendentals=0),
        name="join",
    )(*terms)
    query = gather_relative(my_query, "seq", seq_size)

    every_row = requests * heads_local
    block_rows = (mine + 1) * heads_local + new_rows(mine)
    totals = pl.pallas_call(
        functools.partial(attention_kernel, ways, mine),
        out_shape=[jax.ShapeDtypeStruct((seq_size // ways, block_rows, HD), jnp.bfloat16)] * ways,
        in_specs=[smem] + [vmem] * (ways + 4),
        out_specs=[vmem] * ways,
        scratch_shapes=[
            pltpu.VMEM((every_row, HD), jnp.bfloat16),
            pltpu.VMEM((every_row, HD), jnp.bfloat16),
            pltpu.VMEM((chunks, LANES, PAGE), jnp.bfloat16),
            pltpu.VMEM((slots * heads_local, HD), jnp.float32),
            pltpu.VMEM((chunks, LANES), jnp.float32),
            pltpu.VMEM((chunks, LANES), jnp.float32),
            pltpu.VMEM((chunks, LANES), jnp.float32),
            pltpu.VMEM((2, every_row, HD), jnp.float32),
            pltpu.VMEM((2, every_row, HD), jnp.float32),
            pltpu.VMEM((requests * 2 * kv_local, HD), jnp.float32),
        ],
        compiler_params=pltpu.CompilerParams(vmem_limit_bytes=24 * 2**20),
        cost_estimate=pl.CostEstimate(
            flops=4 * slots * PAGE * wide,
            bytes_accessed=2 * (key_cache.size + value_cache.size),
            transcendentals=slots * PAGE * heads_local,
        ),
        name="paged_attention",
    )(place_of, *query, keyval, tables, key_cache, value_cache)

    for shift, size in lower_groups(seq_size):
        if shift:
            totals = [pick_digit(totals, "seq", shift, size, d) for d in range(size)]
        parts = swap_all(totals, "seq", seq_size, shift)
        totals = pl.pallas_call(
            functools.partial(combine_kernel, mine),
            out_shape=jax.ShapeDtypeStruct(parts[0].shape, jnp.bfloat16),
            in_specs=[vmem] * size,
            out_specs=vmem,
            compiler_params=pltpu.CompilerParams(vmem_limit_bytes=6 * 2**20),
            name="combine",
        )(*parts)
    shift, size = last_group(seq_size)
    parts = [totals] + [swap(totals, "seq", seq_size, d << shift) for d in range(1, size)]
    my_context = pl.pallas_call(
        functools.partial(finish_kernel, mine),
        out_shape=jax.ShapeDtypeStruct((held, wide), jnp.bfloat16),
        in_specs=[vmem] * (size + 1),
        out_specs=vmem,
        scratch_shapes=[pltpu.VMEM((held * heads_local, HD), jnp.float32)],
        compiler_params=pltpu.CompilerParams(vmem_limit_bytes=6 * 2**20),
        name="finish",
    )(*parts, my_query)

    total = pl.pallas_call(
        functools.partial(output_kernel, ways, seq_size),
        out_shape=jax.ShapeDtypeStruct((requests, w_out.shape[1]), jnp.bfloat16),
        in_specs=[smem] + [vmem] * (ways + 1),
        out_specs=vmem,
        scratch_shapes=[pltpu.VMEM((requests, w_out.shape[1]), jnp.float32)],
        compiler_params=pltpu.CompilerParams(vmem_limit_bytes=16 * 2**20),
        name="project_out",
    )(me, *gather_relative(my_context, "seq", seq_size), w_out)
    mask = head_size // 2
    while mask:
        if mask > 1:
            if total.dtype != jnp.bfloat16:
                total = lax.reduce_precision(total, 8, 7).astype(jnp.bfloat16)
            other = swap(total, "head", head_size, mask)
            total = total.astype(jnp.float32) + other.astype(jnp.float32)
        else:
            total = total + swap(total, "head", head_size, mask)
        mask //= 2
    return total.astype(jnp.bfloat16)


def solution(mesh):
    seq_size, head_size = mesh.shape["seq"], mesh.shape["head"]

    def local(*args):
        return body(*args, seq_size=seq_size, head_size=head_size)

    return jax.shard_map(
        local,
        mesh=mesh,
        in_specs=(
            P(None, "seq"),
            P("seq", "head"),
            P("seq", "head"),
            P("head", "seq"),
            P("seq", None, "head"),
            P("seq", None, "head"),
            P("seq", "head"),
            P("seq", "head"),
            P(),
            P("seq"),
            P(),
        ),
        out_specs=P(None, "seq"),
        check_vma=False,
    )
```

```python
import functools
import math

import jax
import jax.numpy as jnp
from jax import lax
from jax.experimental import pallas as pl
from jax.experimental.pallas import tpu as pltpu
from jax.sharding import PartitionSpec as P

HD = 128
PAGE = 128
LANES = 128
CHUNK = 8
STAT = 16


masked_low = -1e30


def swap(x, axis, n, mask):
    return lax.ppermute(x, axis, [(j, j ^ mask) for j in range(n)])


def way_order(size):
    return [0, size - 1, *range(1, size - 1)]


def swap_all(parts, axis, n, shift):
    return [
        swap(parts[d], axis, n, d << shift) if d else parts[0] for d in way_order(len(parts))
    ]


def in_order(parts):
    return [parts[i] for i in sorted(range(len(parts)), key=way_order(len(parts)).__getitem__)]


def bit_groups(n):
    groups, shift = [], 0
    while (1 << shift) < n:
        size = min(4, n >> shift)
        groups.append((shift, size))
        shift += size.bit_length() - 1
    return groups


def lower_groups(n):
    return bit_groups(n)[:-1]


def last_group(n):
    return bit_groups(n)[-1]


def pick_digit(x, axis, shift, size, offset):
    digit = (lax.axis_index(axis) >> shift) % size
    x = x.reshape(x.shape[0] // size, size, *x.shape[1:])
    return lax.dynamic_index_in_dim(x, digit ^ offset, axis=1, keepdims=False)


def scatter_terms(parts, axis, n, beside):
    for shift, size in lower_groups(n):
        if shift:
            parts = [pick_digit(x, axis, shift, size, d) for d in range(size)]
        got = swap_all(parts, axis, n, shift)
        if shift == 0:
            got, beside = lax.optimization_barrier((got, beside))
        x = sum(got[1:], got[0])
    shift, size = last_group(n)
    return [x] + [swap(x, axis, n, d << shift) for d in range(1, size)], beside


def gather_relative(x, axis, n):
    parts = [x]
    for shift, size in reversed(lower_groups(n)):
        x = jnp.concatenate(in_order(parts), axis=0) if len(parts) > 1 else parts[0]
        parts = swap_all([x] * size, axis, n, shift)
    return parts


def relative_place(block, me, n):
    last_shift, _ = last_group(n)
    offset = me ^ block
    place, weight = block >> last_shift, n
    for shift, size in lower_groups(n):
        weight //= size
        place = place + ((offset >> shift) & (size - 1)) * weight
    return place


def gathered_blocks(me, n):
    last_shift, last_size = last_group(n)
    offsets = [0]
    for shift, size in reversed(lower_groups(n)):
        offsets = [d << shift | e for d in range(size) for e in offsets]
    low = me & ((1 << last_shift) - 1)
    return [(c << last_shift) + (low ^ e) for e in offsets for c in range(last_size)]


def table_kernel(seq_size, ways, me, counts, trim, pages, key_scale, value_scale, tables, place_of):
    requests = counts.shape[0]
    chunks = tables.shape[0] // 4
    heads = LANES // CHUNK
    mine = requests // seq_size
    page = pages[...]
    owner, first, length = [jnp.zeros_like(page)] * 3
    start = 0
    for r in range(requests):
        end = start + counts[r]
        inside = (page >= start) & (page < end)
        owner = owner + jnp.where(page >= end, 1, 0)
        first = jnp.where(inside, start, first)
        length = jnp.where(inside, PAGE * counts[r] - trim[r], length)
        start = end
    valid = length - (page - first) * PAGE
    block = owner >> (mine.bit_length() - 1)
    row = relative_place(block, me[0], seq_size) * mine + (owner & (mine - 1))
    place_of[...] = ((me[0] & (ways - 1)) << 24) + (row << 16) + owner

    chunk_slot = lax.broadcasted_iota(jnp.int32, (chunks, LANES), 1) // CHUNK
    in_chunk = chunk_slot == lax.broadcasted_iota(jnp.int32, (chunks, LANES), 0)
    slot = lax.broadcasted_iota(jnp.int32, (LANES, LANES), 0) % CHUNK
    lane = lax.broadcasted_iota(jnp.int32, (LANES, LANES), 1)
    same_slot = slot == lane // heads
    low_head = lane % heads < heads // 2

    def spread(row, to):
        rest = jnp.where(in_chunk, jnp.broadcast_to(row, (chunks, LANES)), 0.0)
        total = jnp.zeros((chunks, LANES), jnp.float32)
        for _ in range(3):
            piece = rest.astype(jnp.bfloat16)
            rest = rest - piece.astype(jnp.float32)
            total = total + jnp.dot(
                piece,
                jnp.where(to, 1.0, 0.0).astype(jnp.bfloat16),
                preferred_element_type=jnp.float32,
            )
        return total

    def by_head(scale):
        return spread(scale[0:1, :], same_slot & low_head) + spread(
            scale[1:2, :], same_slot & jnp.logical_not(low_head)
        )

    tables[:chunks, :] = by_head(key_scale) * (1.0 / math.sqrt(HD))
    tables[chunks : 2 * chunks, :] = spread(valid.astype(jnp.float32), same_slot)
    tables[2 * chunks : 3 * chunks, :] = by_head(value_scale)
    tables[3 * chunks :, :] = spread(owner.astype(jnp.float32), same_slot)


def project_kernel(ways, me, hidden, w_query, w_keyval, *refs):
    outs, (keyval_out, rows_held, query, keyval, result, sem, rows_sem) = refs[:ways], refs[ways:]
    depth = w_query.shape[0]
    tile = min(256, depth)
    copies = [
        [
            pltpu.make_async_copy(
                ref.at[pl.ds(row, tile)], held.at[pl.ds(row, tile)], sem.at[which, row // tile]
            )
            for which, (ref, held) in enumerate(((w_query, query), (w_keyval, keyval)))
        ]
        for row in range(0, depth, tile)
    ]
    rows_copy = pltpu.make_async_copy(hidden, rows_held, rows_sem)
    rows_copy.start()
    for pair in copies:
        for copy in pair:
            copy.start()
    rows_copy.wait()
    for row, pair in zip(range(0, depth, tile), copies):
        here = slice(row, row + tile)
        rows = rows_held[:, here]
        for copy, held, to in zip(pair, (query, keyval), (result, keyval_out)):
            copy.wait()
            part = jnp.dot(rows, held[here, :], preferred_element_type=jnp.float32)
            to[...] = to[...] + part if row else part
    digit = me[0] & (ways - 1)
    for d, out in enumerate(outs):
        blocks, mine, _ = out.shape
        for b in range(blocks):
            if mine % 8 == 0:
                first = (b * ways + (digit ^ d)) * mine
                out[b] = result[pl.ds(pl.multiple_of(first, mine), mine), :]
                continue
            chosen = result[b * ways * mine : (b * ways + 1) * mine, :]
            for j in range(1, ways):
                first = (b * ways + j) * mine
                chosen = jnp.where((digit ^ d) == j, result[first : first + mine, :], chosen)
            out[b] = chosen


def output_kernel(ways, seq_size, me, *refs):
    parts, (w_out, rounded, out) = refs[:ways], refs[ways:]
    rows = jnp.concatenate([part[...] for part in in_order(parts)], axis=0)
    total = jnp.dot(rows, w_out[...], preferred_element_type=jnp.float32)
    blocks = gathered_blocks(me[0], seq_size)
    mine = rows.shape[0] // len(blocks)
    if mine % 8 == 0:
        for i, block in enumerate(blocks):
            here = pl.ds(pl.multiple_of(block * mine, mine), mine)
            out[here, :] = total[i * mine : (i + 1) * mine]
        rounded[...] = out[...].astype(jnp.bfloat16)
        return
    for place in range(len(blocks)):
        chosen = total[:mine]
        for i, block in enumerate(blocks):
            chosen = jnp.where(block == place, total[i * mine : (i + 1) * mine], chosen)
        out[place * mine : (place + 1) * mine, :] = chosen
    rounded[...] = out[...].astype(jnp.bfloat16)


def join_kernel(*refs):
    *parts, out, rows = refs
    blocks, mine, columns = parts[0].shape
    held = blocks * mine
    whole = functools.reduce(jnp.add, [part[...] for part in parts]).reshape(held, columns)
    heads = columns // HD
    for h in range(heads):
        rows[pl.ds(h, held, stride=heads), :] = whole[:, h * HD : (h + 1) * HD]
    out[...] = rows[...].astype(jnp.bfloat16)


def new_rows(mine):
    return -(-4 * mine // 16) * 16


def split_stat(stat, lane):
    hi = stat.astype(jnp.bfloat16).astype(jnp.float32)
    rest = stat - hi
    mid = rest.astype(jnp.bfloat16).astype(jnp.float32)
    piece = jnp.where(lane < STAT, hi, jnp.where(lane < 2 * STAT, mid, rest - mid))
    return piece.astype(jnp.bfloat16)


def join_stat(pieces):
    pieces = pieces.astype(jnp.float32)
    return (pieces + pltpu.roll(pieces, LANES - STAT, 1)) + pltpu.roll(
        pieces, LANES - 2 * STAT, 1
    )


def attention_kernel(ways, mine, place_of, *refs):
    queries, refs = refs[:ways], refs[ways:]
    (keyval, tables, keys, values), refs = refs[:4], refs[4:]
    outs, refs = refs[:ways], refs[ways:]
    (
        query_low,
        query_high,
        probs,
        page_out,
        page_sum,
        page_max,
        dev_max,
        total_out,
        total_stat,
        keyval_rows,
    ) = refs
    slots = keys.shape[0]
    heads = LANES // CHUNK
    group = heads // 2
    chunks = slots // CHUNK
    blocks = outs[0].shape[0]
    lag = 4

    for d, part in enumerate(in_order(queries)):
        rows = part[...]
        low_head = lax.broadcasted_iota(jnp.int32, rows.shape, 0) % heads < group
        zero = jnp.zeros_like(rows)
        here = slice(rows.shape[0] * d, rows.shape[0] * (d + 1))
        query_low[here, :] = jnp.where(low_head, rows, zero)
        query_high[here, :] = jnp.where(low_head, zero, rows)
    total_out[...] = jnp.zeros_like(total_out)
    stat_lane = lax.broadcasted_iota(jnp.int32, total_stat.shape, 2) % STAT
    total_stat[...] = jnp.where(stat_lane < STAT // 2, masked_low, 0.0)

    def table(which, c):
        return tables[pl.ds(which * chunks + c, 1), :]

    lane_slot = lax.broadcasted_iota(jnp.int32, (PAGE, LANES), 1) // heads
    token = lax.broadcasted_iota(jnp.int32, (PAGE, LANES), 0).astype(jnp.float32)

    def score_chunk(c):
        places = [
            pl.multiple_of(((place_of[c * CHUNK + s] >> 16) & 0xFF) * heads, heads)
            for s in range(CHUNK)
        ]
        chosen = jnp.concatenate(
            [
                jnp.concatenate([ref[pl.ds(place, heads), :] for place in places], axis=0)
                for ref in (query_low, query_high)
            ],
            axis=1,
        )
        block = keys[pl.ds(c * CHUNK, CHUNK)].reshape(CHUNK * PAGE, 2 * HD)
        every = lax.dot_general(
            block, chosen, (((1,), (1,)), ((), ())), preferred_element_type=jnp.float32
        )
        score = every[:PAGE]
        for s in range(1, CHUNK):
            score = jnp.where(lane_slot == s, every[s * PAGE : (s + 1) * PAGE], score)
        score = jnp.where(token < table(1, c), score * table(0, c), masked_low)
        top = jnp.max(score, axis=0, keepdims=True)
        page_max[pl.ds(c, 1), :] = top
        prob = jnp.exp(score - top).astype(jnp.bfloat16).astype(jnp.float32)
        page_sum[pl.ds(c, 1), :] = jnp.sum(prob, axis=0, keepdims=True)
        probs[c] = prob.T.astype(jnp.bfloat16)

    empty = jnp.zeros((heads, PAGE), jnp.bfloat16)

    def value_chunk(c):
        prob = probs[c]
        for s in range(0, CHUNK, 2):
            pair = jnp.concatenate(
                [
                    jnp.concatenate([prob[s * heads : (s + 1) * heads], empty], axis=1),
                    jnp.concatenate([empty, prob[(s + 1) * heads : (s + 2) * heads]], axis=1),
                ],
                axis=0,
            )
            block = values[pl.ds(c * CHUNK + s, 2)].reshape(2 * PAGE, 2 * HD)
            both = jnp.dot(pair, block, preferred_element_type=jnp.float32)
            page_out[pl.ds(pl.multiple_of((c * CHUNK + s) * heads, heads), 2 * heads), :] = (
                jnp.concatenate(
                    [
                        both[:group, :HD],
                        both[group:heads, HD:],
                        both[heads : heads + group, :HD],
                        both[heads + group :, HD:],
                    ],
                    axis=0,
                )
            )

    for c in range(chunks + lag):
        if c >= lag:
            value_chunk(c - lag)
        if c < chunks:
            score_chunk(c)

    biggest, who = page_max[...], tables[3 * chunks :, :]
    best = biggest
    for turn in range(CHUNK):
        other = pltpu.roll(biggest, turn * heads, 1) if turn else biggest
        other_who = pltpu.roll(who, turn * heads, 1) if turn else who
        for c in range(chunks):
            best = jnp.maximum(
                best, jnp.where(other_who[c : c + 1] == who, other[c : c + 1], masked_low)
            )
    dev_max[...] = best

    keep_max = lax.broadcasted_iota(jnp.int32, (heads, LANES), 1) % STAT < STAT // 2

    keep_max_row = lax.broadcasted_iota(jnp.int32, (PAGE, LANES), 0) % STAT < STAT // 2

    for c in range(chunks):
        top = dev_max[pl.ds(c, 1), :]
        weight = jnp.exp(page_max[pl.ds(c, 1), :] - top)
        out_weight = jnp.broadcast_to(weight * table(2, c), (PAGE, LANES)).T
        stat = jnp.where(keep_max_row, top, weight * page_sum[pl.ds(c, 1), :]).T
        for s in range(CHUNK):
            here = pl.ds(
                pl.multiple_of((place_of[c * CHUNK + s] & 0xFFFF) * heads, heads), heads
            )
            there = pl.ds(pl.multiple_of((c * CHUNK + s) * heads, heads), heads)
            part = slice(s * heads, (s + 1) * heads)
            turn = s % 2
            total_out[turn, here, :] += page_out[there, :] * out_weight[part]
            total_stat[turn, here, :] = jnp.where(
                keep_max, stat[part], total_stat[turn, here, :] + stat[part]
            )

    lane = lax.broadcasted_iota(jnp.int32, (heads, LANES), 1)
    digit = place_of[0] >> 24
    for j in range(4):
        keyval_rows[pl.ds(j, keyval.shape[0], stride=4), :] = keyval[:, j * HD : (j + 1) * HD]
    for d, out in enumerate(outs):
        for b in range(blocks):
            block = b * ways + (digit ^ d)
            rows = pl.ds(pl.multiple_of(block * (mine * heads), mine * heads), mine * heads)
            out[b, : mine * heads, :] = (total_out[0, rows, :] + total_out[1, rows, :]).astype(
                jnp.bfloat16
            )
            even, odd = total_stat[0, rows, :], total_stat[1, rows, :]
            is_max = lax.broadcasted_iota(jnp.int32, even.shape, 1) % STAT < STAT // 2
            both = jnp.where(is_max, jnp.maximum(even, odd), even + odd)
            stat = jnp.zeros((heads, LANES), jnp.float32)
            for r in range(mine):
                stat = jnp.where(
                    lane % (STAT // 2) == r, both[r * heads : (r + 1) * heads], stat
                )
            out[b, mine * heads : (mine + 1) * heads, :] = split_stat(stat, lane)
            new = keyval_rows[pl.ds(pl.multiple_of(block * (4 * mine), 4 * mine), 4 * mine), :]
            if new.shape[0] < new_rows(mine):
                empty_rows = jnp.zeros((new_rows(mine) - new.shape[0], LANES), jnp.float32)
                new = jnp.concatenate([new, empty_rows], axis=0)
            out[b, (mine + 1) * heads :, :] = new.astype(jnp.bfloat16)


def combine_kernel(mine, *refs):
    *parts, out = refs
    blocks = out.shape[0]
    heads = LANES // CHUNK
    lane = lax.broadcasted_iota(jnp.int32, (heads, LANES), 1)
    for b in range(blocks):
        stats = [join_stat(part[b, mine * heads : (mine + 1) * heads, :]) for part in parts]
        maxima = [jnp.where(lane < mine, stat, 0.0) for stat in stats]
        top = functools.reduce(jnp.maximum, maxima)
        factors = [jnp.exp(m - top) for m in maxima]
        sums = sum(
            pltpu.roll(f, STAT // 2, 1) * jnp.where(lane < STAT, stat, 0.0)
            for f, stat in zip(factors, stats)
        )
        both = jnp.where(lane < STAT // 2, top, sums)
        both = jnp.where(lane < STAT, both, 0.0)
        both = (both + pltpu.roll(both, STAT, 1)) + pltpu.roll(both, 2 * STAT, 1)
        out[b, mine * heads : (mine + 1) * heads, :] = split_stat(both, lane)
        new = sum(part[b, (mine + 1) * heads :, :].astype(jnp.float32) for part in parts)
        out[b, (mine + 1) * heads :, :] = new.astype(jnp.bfloat16)
        for r in range(mine):
            rows = slice(r * heads, (r + 1) * heads)
            numer = sum(
                f[:, r : r + 1] * part[b, rows, :].astype(jnp.float32)
                for f, part in zip(factors, parts)
            )
            out[b, rows, :] = numer.astype(jnp.bfloat16)


def finish_kernel(mine, *refs):
    *parts, query, out, numers = refs
    blocks = parts[0].shape[0]
    heads = LANES // CHUNK
    group = heads // 2
    lane = lax.broadcasted_iota(jnp.int32, (heads, LANES), 1)
    low_head = lax.broadcasted_iota(jnp.int32, (heads, LANES), 0) < group
    def spread(new, r, which):
        low = jnp.broadcast_to(new[4 * r + which : 4 * r + which + 1], (heads, LANES))
        high = jnp.broadcast_to(new[4 * r + 2 + which : 4 * r + 3 + which], (heads, LANES))
        return jnp.where(low_head, low, high)

    for b in range(blocks):
        new = sum(part[b, (mine + 1) * heads :, :].astype(jnp.float32) for part in parts)
        new = new.astype(jnp.bfloat16).astype(jnp.float32)
        own = jnp.zeros((heads, LANES), jnp.float32)
        for r in range(mine):
            request = b * mine + r
            rows = query[request * heads : (request + 1) * heads, :].astype(jnp.float32)
            dot = jnp.sum(rows * spread(new, r, 0), axis=1, keepdims=True)
            own = jnp.where(lane == r, dot * (1.0 / math.sqrt(HD)), own)
        maxima, sums = [], []
        for part in parts:
            whole = join_stat(part[b, mine * heads : (mine + 1) * heads, :])
            maxima.append(jnp.where(lane < mine, whole, 0.0))
            sums.append(jnp.where(lane < mine, pltpu.roll(whole, LANES - STAT // 2, 1), 0.0))
        top = functools.reduce(jnp.maximum, maxima, own)
        fresh = jnp.exp(own - top)
        factors = [jnp.exp(m - top) for m in maxima]
        denom = sum((s * f for s, f in zip(sums, factors)), fresh)
        fresh = fresh / denom
        factors = [f / denom for f in factors]
        for r in range(mine):
            numer = fresh[:, r : r + 1] * spread(new, r, 1)
            for part, f in zip(parts, factors):
                rows = part[b, r * heads : (r + 1) * heads, :].astype(jnp.float32)
                numer = numer + f[:, r : r + 1] * rows
            request = b * mine + r
            numers[request * heads : (request + 1) * heads, :] = numer
    for h in range(heads):
        out[:, h * HD : (h + 1) * HD] = numers[
            pl.ds(h, blocks * mine, stride=heads), :
        ].astype(jnp.bfloat16)


def body(
    hidden_in,
    w_query,
    w_keyval,
    w_out,
    key_cache,
    value_cache,
    key_scale,
    value_scale,
    page_counts,
    slot_pages,
    trim,
    seq_size,
    head_size,
):
    requests = hidden_in.shape[0]
    slots = key_cache.shape[0]
    kv_local = w_keyval.shape[1] // (2 * HD)
    heads_local = w_query.shape[1] // HD
    wide = heads_local * HD
    group = heads_local // kv_local
    assert kv_local == 2 and heads_local * CHUNK == LANES
    assert slots % CHUNK == 0
    mine = requests // seq_size
    inverse_square_root = 1.0 / math.sqrt(HD)

    assert slots == LANES and mine & (mine - 1) == 0
    ways = lower_groups(seq_size)[0][1]
    chunks = slots // CHUNK
    smem = pl.BlockSpec(memory_space=pltpu.SMEM)
    vmem = pl.BlockSpec(memory_space=pltpu.VMEM)
    hbm = pl.BlockSpec(memory_space=pl.ANY)
    small = pltpu.CompilerParams(vmem_limit_bytes=6 * 2**20)
    me = lax.axis_index("seq").reshape(1)

    def in_hbm(x):
        return pltpu.with_memory_space_constraint(x, pltpu.HBM)

    tables, place_of = pl.pallas_call(
        functools.partial(table_kernel, seq_size, ways),
        out_shape=[
            jax.ShapeDtypeStruct((4 * chunks, LANES), jnp.float32),
            jax.ShapeDtypeStruct((1, slots), jnp.int32),
        ],
        in_specs=[smem, smem, smem, vmem, vmem, vmem],
        out_specs=[vmem, vmem],
        compiler_params=small,
        name="page_table",
    )(me, page_counts, trim, slot_pages.reshape(1, slots), key_scale.T, value_scale.T)
    place_of = place_of.reshape(slots)

    held = last_group(seq_size)[1] * mine
    part_shape = jax.ShapeDtypeStruct((seq_size // ways, mine, wide), jnp.float32)
    keyval_shape = jax.ShapeDtypeStruct((requests, w_keyval.shape[1]), jnp.float32)
    *parts, keyval = pl.pallas_call(
        functools.partial(project_kernel, ways),
        out_shape=[part_shape] * ways + [keyval_shape],
        in_specs=[smem, hbm, hbm, hbm],
        out_specs=[vmem] * (ways + 1),
        scratch_shapes=[
            pltpu.VMEM(hidden_in.shape, jnp.bfloat16),
            pltpu.VMEM(w_query.shape, jnp.bfloat16),
            pltpu.VMEM(w_keyval.shape, jnp.bfloat16),
            pltpu.VMEM((requests, wide), jnp.float32),
            pltpu.SemaphoreType.DMA((2, pl.cdiv(w_query.shape[0], 256))),
            pltpu.SemaphoreType.DMA,
        ],
        compiler_params=pltpu.CompilerParams(vmem_limit_bytes=53 * 2**20),
        name="project",
    )(me, in_hbm(hidden_in), in_hbm(w_query), in_hbm(w_keyval))
    terms, (tables, place_of) = scatter_terms(parts, "seq", seq_size, (tables, place_of))
    my_query = pl.pallas_call(
        join_kernel,
        out_shape=jax.ShapeDtypeStruct((held * heads_local, HD), jnp.bfloat16),
        in_specs=[vmem] * len(terms),
        out_specs=vmem,
        scratch_shapes=[pltpu.VMEM((held * heads_local, HD), jnp.float32)],
        compiler_params=small,
        cost_estimate=pl.CostEstimate(flops=10**10, bytes_accessed=10**7, transcendentals=0),
        name="join",
    )(*terms)
    query = gather_relative(my_query, "seq", seq_size)

    every_row = requests * heads_local
    block_rows = (mine + 1) * heads_local + new_rows(mine)
    totals = pl.pallas_call(
        functools.partial(attention_kernel, ways, mine),
        out_shape=[jax.ShapeDtypeStruct((seq_size // ways, block_rows, HD), jnp.bfloat16)] * ways,
        in_specs=[smem] + [vmem] * (ways + 4),
        out_specs=[vmem] * ways,
        scratch_shapes=[
            pltpu.VMEM((every_row, HD), jnp.bfloat16),
            pltpu.VMEM((every_row, HD), jnp.bfloat16),
            pltpu.VMEM((chunks, LANES, PAGE), jnp.bfloat16),
            pltpu.VMEM((slots * heads_local, HD), jnp.float32),
            pltpu.VMEM((chunks, LANES), jnp.float32),
            pltpu.VMEM((chunks, LANES), jnp.float32),
            pltpu.VMEM((chunks, LANES), jnp.float32),
            pltpu.VMEM((2, every_row, HD), jnp.float32),
            pltpu.VMEM((2, every_row, HD), jnp.float32),
            pltpu.VMEM((requests * 2 * kv_local, HD), jnp.float32),
        ],
        compiler_params=pltpu.CompilerParams(vmem_limit_bytes=24 * 2**20),
        cost_estimate=pl.CostEstimate(
            flops=4 * slots * PAGE * wide,
            bytes_accessed=2 * (key_cache.size + value_cache.size),
            transcendentals=slots * PAGE * heads_local,
        ),
        name="paged_attention",
    )(place_of, *query, keyval, tables, key_cache, value_cache)

    for shift, size in lower_groups(seq_size):
        if shift:
            totals = [pick_digit(totals, "seq", shift, size, d) for d in range(size)]
        parts = swap_all(totals, "seq", seq_size, shift)
        totals = pl.pallas_call(
            functools.partial(combine_kernel, mine),
            out_shape=jax.ShapeDtypeStruct(parts[0].shape, jnp.bfloat16),
            in_specs=[vmem] * size,
            out_specs=vmem,
            compiler_params=pltpu.CompilerParams(vmem_limit_bytes=6 * 2**20),
            name="combine",
        )(*parts)
    shift, size = last_group(seq_size)
    parts = [totals] + [swap(totals, "seq", seq_size, d << shift) for d in range(1, size)]
    my_context = pl.pallas_call(
        functools.partial(finish_kernel, mine),
        out_shape=jax.ShapeDtypeStruct((held, wide), jnp.bfloat16),
        in_specs=[vmem] * (size + 1),
        out_specs=vmem,
        scratch_shapes=[pltpu.VMEM((held * heads_local, HD), jnp.float32)],
        compiler_params=pltpu.CompilerParams(vmem_limit_bytes=6 * 2**20),
        name="finish",
    )(*parts, my_query)

    total = pl.pallas_call(
        functools.partial(output_kernel, ways, seq_size),
        out_shape=jax.ShapeDtypeStruct((requests, w_out.shape[1]), jnp.bfloat16),
        in_specs=[smem] + [vmem] * (ways + 1),
        out_specs=vmem,
        scratch_shapes=[pltpu.VMEM((requests, w_out.shape[1]), jnp.float32)],
        compiler_params=pltpu.CompilerParams(vmem_limit_bytes=16 * 2**20),
        name="project_out",
    )(me, *gather_relative(my_context, "seq", seq_size), w_out)
    mask = head_size // 2
    while mask:
        if mask > 1:
            if total.dtype != jnp.bfloat16:
                total = lax.reduce_precision(total, 8, 7).astype(jnp.bfloat16)
            other = swap(total, "head", head_size, mask)
            total = total.astype(jnp.float32) + other.astype(jnp.float32)
        else:
            total = total + swap(total, "head", head_size, mask)
        mask //= 2
    return total.astype(jnp.bfloat16)


def solution(mesh):
    seq_size, head_size = mesh.shape["seq"], mesh.shape["head"]

    def local(*args):
        return body(*args, seq_size=seq_size, head_size=head_size)

    return jax.shard_map(
        local,
        mesh=mesh,
        in_specs=(
            P(None, "seq"),
            P("seq", "head"),
            P("seq", "head"),
            P("head", "seq"),
            P("seq", None, "head"),
            P("seq", None, "head"),
            P("seq", "head"),
            P("seq", "head"),
            P(),
            P("seq"),
            P(),
        ),
        out_specs=P(None, "seq"),
        check_vma=False,
    )
```

```python
import functools
import math

import jax
import jax.numpy as jnp
from jax import lax
from jax.experimental import pallas as pl
from jax.experimental.pallas import tpu as pltpu
from jax.sharding import PartitionSpec as P

HD = 128
PAGE = 128
LANES = 128
CHUNK = 8
STAT = 16


masked_low = -1e30


def swap(x, axis, n, mask):
    return lax.ppermute(x, axis, [(j, j ^ mask) for j in range(n)])


def way_order(size):
    return [0, size - 1, *range(1, size - 1)]


def swap_all(parts, axis, n, shift):
    return [
        swap(parts[d], axis, n, d << shift) if d else parts[0] for d in way_order(len(parts))
    ]


def in_order(parts):
    return [parts[i] for i in sorted(range(len(parts)), key=way_order(len(parts)).__getitem__)]


def bit_groups(n):
    groups, shift = [], 0
    while (1 << shift) < n:
        size = min(4, n >> shift)
        groups.append((shift, size))
        shift += size.bit_length() - 1
    return groups


def lower_groups(n):
    return bit_groups(n)[:-1]


def last_group(n):
    return bit_groups(n)[-1]


def pick_digit(x, axis, shift, size, offset):
    digit = (lax.axis_index(axis) >> shift) % size
    x = x.reshape(x.shape[0] // size, size, *x.shape[1:])
    return lax.dynamic_index_in_dim(x, digit ^ offset, axis=1, keepdims=False)


def scatter_terms(parts, axis, n, beside):
    for shift, size in lower_groups(n):
        if shift:
            parts = [pick_digit(x, axis, shift, size, d) for d in range(size)]
        got = swap_all(parts, axis, n, shift)
        if shift == 0:
            got, beside = lax.optimization_barrier((got, beside))
        x = sum(got[1:], got[0])
    shift, size = last_group(n)
    return [x] + [swap(x, axis, n, d << shift) for d in range(1, size)], beside


def gather_relative(x, axis, n):
    parts = [x]
    for shift, size in reversed(lower_groups(n)):
        x = jnp.concatenate(in_order(parts), axis=0) if len(parts) > 1 else parts[0]
        parts = swap_all([x] * size, axis, n, shift)
    return parts


def relative_place(block, me, n):
    last_shift, _ = last_group(n)
    offset = me ^ block
    place, weight = block >> last_shift, n
    for shift, size in lower_groups(n):
        weight //= size
        place = place + ((offset >> shift) & (size - 1)) * weight
    return place


def gathered_blocks(me, n):
    last_shift, last_size = last_group(n)
    offsets = [0]
    for shift, size in reversed(lower_groups(n)):
        offsets = [d << shift | e for d in range(size) for e in offsets]
    low = me & ((1 << last_shift) - 1)
    return [(c << last_shift) + (low ^ e) for e in offsets for c in range(last_size)]


def table_kernel(seq_size, ways, counts, trim, pages, key_scale, value_scale, tables, place_of):
    requests = counts.shape[0]
    chunks = tables.shape[0] // 4
    heads = LANES // CHUNK
    mine = requests // seq_size
    page = pages[...]
    owner, first, length = [jnp.zeros_like(page)] * 3
    start = 0
    for r in range(requests):
        end = start + counts[r]
        inside = (page >= start) & (page < end)
        owner = owner + jnp.where(page >= end, 1, 0)
        first = jnp.where(inside, start, first)
        length = jnp.where(inside, PAGE * counts[r] - trim[r], length)
        start = end
    valid = length - (page - first) * PAGE
    block = owner >> (mine.bit_length() - 1)
    me = lax.axis_index("seq")
    row = relative_place(block, me, seq_size) * mine + (owner & (mine - 1))
    place_of[...] = ((me & (ways - 1)) << 24) + (row << 16) + owner

    chunk_slot = lax.broadcasted_iota(jnp.int32, (chunks, LANES), 1) // CHUNK
    in_chunk = chunk_slot == lax.broadcasted_iota(jnp.int32, (chunks, LANES), 0)
    slot = lax.broadcasted_iota(jnp.int32, (LANES, LANES), 0) % CHUNK
    lane = lax.broadcasted_iota(jnp.int32, (LANES, LANES), 1)
    same_slot = slot == lane // heads
    low_head = lane % heads < heads // 2

    def spread(row, to):
        rest = jnp.where(in_chunk, jnp.broadcast_to(row, (chunks, LANES)), 0.0)
        total = jnp.zeros((chunks, LANES), jnp.float32)
        for _ in range(3):
            piece = rest.astype(jnp.bfloat16)
            rest = rest - piece.astype(jnp.float32)
            total = total + jnp.dot(
                piece,
                jnp.where(to, 1.0, 0.0).astype(jnp.bfloat16),
                preferred_element_type=jnp.float32,
            )
        return total

    def by_head(scale):
        return spread(scale[0:1, :], same_slot & low_head) + spread(
            scale[1:2, :], same_slot & jnp.logical_not(low_head)
        )

    tables[:chunks, :] = by_head(key_scale) * (1.0 / math.sqrt(HD))
    tables[chunks : 2 * chunks, :] = spread(valid.astype(jnp.float32), same_slot)
    tables[2 * chunks : 3 * chunks, :] = by_head(value_scale)
    tables[3 * chunks :, :] = spread(owner.astype(jnp.float32), same_slot)


def project_kernel(ways, hidden, w_query, w_keyval, *refs):
    outs, (keyval_out, rows_held, query, keyval, result, sem, rows_sem) = refs[:ways], refs[ways:]
    depth = w_query.shape[0]
    tile = min(256, depth)
    copies = [
        [
            pltpu.make_async_copy(
                ref.at[pl.ds(row, tile)], held.at[pl.ds(row, tile)], sem.at[which, row // tile]
            )
            for which, (ref, held) in enumerate(((w_query, query), (w_keyval, keyval)))
        ]
        for row in range(0, depth, tile)
    ]
    rows_copy = pltpu.make_async_copy(hidden, rows_held, rows_sem)
    rows_copy.start()
    for pair in copies:
        for copy in pair:
            copy.start()
    rows_copy.wait()
    for row, pair in zip(range(0, depth, tile), copies):
        here = slice(row, row + tile)
        rows = rows_held[:, here]
        for copy in pair:
            copy.wait()
        for held, to in ((query, result), (keyval, keyval_out)):
            part = jnp.dot(rows, held[here, :], preferred_element_type=jnp.float32)
            to[...] = to[...] + part if row else part
    digit = lax.axis_index("seq") & (ways - 1)
    for d, out in enumerate(outs):
        blocks, mine, _ = out.shape
        for b in range(blocks):
            if mine % 8 == 0:
                first = (b * ways + (digit ^ d)) * mine
                out[b] = result[pl.ds(pl.multiple_of(first, mine), mine), :]
                continue
            chosen = result[b * ways * mine : (b * ways + 1) * mine, :]
            for j in range(1, ways):
                first = (b * ways + j) * mine
                chosen = jnp.where((digit ^ d) == j, result[first : first + mine, :], chosen)
            out[b] = chosen


def output_kernel(ways, seq_size, *refs):
    parts, (w_out, rounded, out) = refs[:ways], refs[ways:]
    rows = jnp.concatenate([part[...] for part in in_order(parts)], axis=0)
    total = jnp.dot(rows, w_out[...], preferred_element_type=jnp.float32)
    blocks = gathered_blocks(lax.axis_index("seq"), seq_size)
    mine = rows.shape[0] // len(blocks)
    if mine % 8 == 0:
        for i, block in enumerate(blocks):
            here = pl.ds(pl.multiple_of(block * mine, mine), mine)
            out[here, :] = total[i * mine : (i + 1) * mine]
        rounded[...] = out[...].astype(jnp.bfloat16)
        return
    for place in range(len(blocks)):
        chosen = total[:mine]
        for i, block in enumerate(blocks):
            chosen = jnp.where(block == place, total[i * mine : (i + 1) * mine], chosen)
        out[place * mine : (place + 1) * mine, :] = chosen
    rounded[...] = out[...].astype(jnp.bfloat16)


def join_kernel(*refs):
    *parts, out, rows = refs
    blocks, mine, columns = parts[0].shape
    held = blocks * mine
    whole = functools.reduce(jnp.add, [part[...] for part in parts]).reshape(held, columns)
    heads = columns // HD
    for h in range(heads):
        rows[pl.ds(h, held, stride=heads), :] = whole[:, h * HD : (h + 1) * HD]
    out[...] = rows[...].astype(jnp.bfloat16)


def new_rows(mine):
    return -(-4 * mine // 16) * 16


def split_stat(stat, lane):
    hi = stat.astype(jnp.bfloat16).astype(jnp.float32)
    rest = stat - hi
    mid = rest.astype(jnp.bfloat16).astype(jnp.float32)
    piece = jnp.where(lane < STAT, hi, jnp.where(lane < 2 * STAT, mid, rest - mid))
    return piece.astype(jnp.bfloat16)


def join_stat(pieces):
    pieces = pieces.astype(jnp.float32)
    return (pieces + pltpu.roll(pieces, LANES - STAT, 1)) + pltpu.roll(
        pieces, LANES - 2 * STAT, 1
    )


def attention_kernel(ways, mine, place_of, *refs):
    queries, refs = refs[:ways], refs[ways:]
    (keyval, tables, keys, values), refs = refs[:4], refs[4:]
    outs, refs = refs[:ways], refs[ways:]
    (
        query_low,
        query_high,
        probs,
        page_out,
        page_sum,
        page_max,
        dev_max,
        total_out,
        total_stat,
        keyval_rows,
    ) = refs
    slots = keys.shape[0]
    heads = LANES // CHUNK
    group = heads // 2
    chunks = slots // CHUNK
    blocks = outs[0].shape[0]
    lag = 4

    for d, part in enumerate(in_order(queries)):
        rows = part[...]
        low_head = lax.broadcasted_iota(jnp.int32, rows.shape, 0) % heads < group
        zero = jnp.zeros_like(rows)
        here = slice(rows.shape[0] * d, rows.shape[0] * (d + 1))
        query_low[here, :] = jnp.where(low_head, rows, zero)
        query_high[here, :] = jnp.where(low_head, zero, rows)
    total_out[...] = jnp.zeros_like(total_out)
    stat_lane = lax.broadcasted_iota(jnp.int32, total_stat.shape, 2) % STAT
    total_stat[...] = jnp.where(stat_lane < STAT // 2, masked_low, 0.0)

    def table(which, c):
        return tables[pl.ds(which * chunks + c, 1), :]

    lane_slot = lax.broadcasted_iota(jnp.int32, (PAGE, LANES), 1) // heads
    token = lax.broadcasted_iota(jnp.int32, (PAGE, LANES), 0).astype(jnp.float32)

    def score_chunk(c):
        places = [
            pl.multiple_of(((place_of[c * CHUNK + s] >> 16) & 0xFF) * heads, heads)
            for s in range(CHUNK)
        ]
        chosen = jnp.concatenate(
            [
                jnp.concatenate([ref[pl.ds(place, heads), :] for place in places], axis=0)
                for ref in (query_low, query_high)
            ],
            axis=1,
        )
        block = keys[pl.ds(c * CHUNK, CHUNK)].reshape(CHUNK * PAGE, 2 * HD)
        every = lax.dot_general(
            block, chosen, (((1,), (1,)), ((), ())), preferred_element_type=jnp.float32
        )
        score = every[:PAGE]
        for s in range(1, CHUNK):
            score = jnp.where(lane_slot == s, every[s * PAGE : (s + 1) * PAGE], score)
        score = jnp.where(token < table(1, c), score * table(0, c), masked_low)
        top = jnp.max(score, axis=0, keepdims=True)
        page_max[pl.ds(c, 1), :] = top
        prob = jnp.exp(score - top).astype(jnp.bfloat16).astype(jnp.float32)
        page_sum[pl.ds(c, 1), :] = jnp.sum(prob, axis=0, keepdims=True)
        probs[c] = prob.T.astype(jnp.bfloat16)

    empty = jnp.zeros((heads, PAGE), jnp.bfloat16)

    def value_chunk(c):
        prob = probs[c]
        for s in range(0, CHUNK, 2):
            pair = jnp.concatenate(
                [
                    jnp.concatenate([prob[s * heads : (s + 1) * heads], empty], axis=1),
                    jnp.concatenate([empty, prob[(s + 1) * heads : (s + 2) * heads]], axis=1),
                ],
                axis=0,
            )
            block = values[pl.ds(c * CHUNK + s, 2)].reshape(2 * PAGE, 2 * HD)
            both = jnp.dot(pair, block, preferred_element_type=jnp.float32)
            page_out[pl.ds(pl.multiple_of((c * CHUNK + s) * heads, heads), 2 * heads), :] = (
                jnp.concatenate(
                    [
                        both[:group, :HD],
                        both[group:heads, HD:],
                        both[heads : heads + group, :HD],
                        both[heads + group :, HD:],
                    ],
                    axis=0,
                )
            )

    for c in range(chunks + lag):
        if c >= lag:
            value_chunk(c - lag)
        if c < chunks:
            score_chunk(c)

    biggest, who = page_max[...], tables[3 * chunks :, :]
    best = biggest
    for turn in range(CHUNK):
        other = pltpu.roll(biggest, turn * heads, 1) if turn else biggest
        other_who = pltpu.roll(who, turn * heads, 1) if turn else who
        for c in range(chunks):
            best = jnp.maximum(
                best, jnp.where(other_who[c : c + 1] == who, other[c : c + 1], masked_low)
            )
    dev_max[...] = best

    keep_max = lax.broadcasted_iota(jnp.int32, (heads, LANES), 1) % STAT < STAT // 2

    keep_max_row = lax.broadcasted_iota(jnp.int32, (PAGE, LANES), 0) % STAT < STAT // 2

    for c in range(chunks):
        top = dev_max[pl.ds(c, 1), :]
        weight = jnp.exp(page_max[pl.ds(c, 1), :] - top)
        out_weight = jnp.broadcast_to(weight * table(2, c), (PAGE, LANES)).T
        stat = jnp.where(keep_max_row, top, weight * page_sum[pl.ds(c, 1), :]).T
        for s in range(CHUNK):
            here = pl.ds(
                pl.multiple_of((place_of[c * CHUNK + s] & 0xFFFF) * heads, heads), heads
            )
            there = pl.ds(pl.multiple_of((c * CHUNK + s) * heads, heads), heads)
            part = slice(s * heads, (s + 1) * heads)
            turn = s % 2
            total_out[turn, here, :] += page_out[there, :] * out_weight[part]
            total_stat[turn, here, :] = jnp.where(
                keep_max, stat[part], total_stat[turn, here, :] + stat[part]
            )

    lane = lax.broadcasted_iota(jnp.int32, (heads, LANES), 1)
    digit = place_of[0] >> 24
    for j in range(4):
        keyval_rows[pl.ds(j, keyval.shape[0], stride=4), :] = keyval[:, j * HD : (j + 1) * HD]
    for d, out in enumerate(outs):
        for b in range(blocks):
            block = b * ways + (digit ^ d)
            rows = pl.ds(pl.multiple_of(block * (mine * heads), mine * heads), mine * heads)
            out[b, : mine * heads, :] = (total_out[0, rows, :] + total_out[1, rows, :]).astype(
                jnp.bfloat16
            )
            even, odd = total_stat[0, rows, :], total_stat[1, rows, :]
            is_max = lax.broadcasted_iota(jnp.int32, even.shape, 1) % STAT < STAT // 2
            both = jnp.where(is_max, jnp.maximum(even, odd), even + odd)
            stat = jnp.zeros((heads, LANES), jnp.float32)
            for r in range(mine):
                stat = jnp.where(
                    lane % (STAT // 2) == r, both[r * heads : (r + 1) * heads], stat
                )
            out[b, mine * heads : (mine + 1) * heads, :] = split_stat(stat, lane)
            new = keyval_rows[pl.ds(pl.multiple_of(block * (4 * mine), 4 * mine), 4 * mine), :]
            if new.shape[0] < new_rows(mine):
                empty_rows = jnp.zeros((new_rows(mine) - new.shape[0], LANES), jnp.float32)
                new = jnp.concatenate([new, empty_rows], axis=0)
            out[b, (mine + 1) * heads :, :] = new.astype(jnp.bfloat16)


def combine_kernel(mine, *refs):
    *parts, out = refs
    blocks = out.shape[0]
    heads = LANES // CHUNK
    lane = lax.broadcasted_iota(jnp.int32, (heads, LANES), 1)
    for b in range(blocks):
        stats = [join_stat(part[b, mine * heads : (mine + 1) * heads, :]) for part in parts]
        maxima = [jnp.where(lane < mine, stat, 0.0) for stat in stats]
        top = functools.reduce(jnp.maximum, maxima)
        factors = [jnp.exp(m - top) for m in maxima]
        sums = sum(
            pltpu.roll(f, STAT // 2, 1) * jnp.where(lane < STAT, stat, 0.0)
            for f, stat in zip(factors, stats)
        )
        both = jnp.where(lane < STAT // 2, top, sums)
        both = jnp.where(lane < STAT, both, 0.0)
        both = (both + pltpu.roll(both, STAT, 1)) + pltpu.roll(both, 2 * STAT, 1)
        out[b, mine * heads : (mine + 1) * heads, :] = split_stat(both, lane)
        new = sum(part[b, (mine + 1) * heads :, :].astype(jnp.float32) for part in parts)
        out[b, (mine + 1) * heads :, :] = new.astype(jnp.bfloat16)
        for r in range(mine):
            rows = slice(r * heads, (r + 1) * heads)
            numer = sum(
                f[:, r : r + 1] * part[b, rows, :].astype(jnp.float32)
                for f, part in zip(factors, parts)
            )
            out[b, rows, :] = numer.astype(jnp.bfloat16)


def finish_kernel(mine, *refs):
    *parts, query, out, numers = refs
    blocks = parts[0].shape[0]
    heads = LANES // CHUNK
    group = heads // 2
    lane = lax.broadcasted_iota(jnp.int32, (heads, LANES), 1)
    low_head = lax.broadcasted_iota(jnp.int32, (heads, LANES), 0) < group
    def spread(new, r, which):
        low = jnp.broadcast_to(new[4 * r + which : 4 * r + which + 1], (heads, LANES))
        high = jnp.broadcast_to(new[4 * r + 2 + which : 4 * r + 3 + which], (heads, LANES))
        return jnp.where(low_head, low, high)

    for b in range(blocks):
        new = sum(part[b, (mine + 1) * heads :, :].astype(jnp.float32) for part in parts)
        new = new.astype(jnp.bfloat16).astype(jnp.float32)
        own = jnp.zeros((heads, LANES), jnp.float32)
        for r in range(mine):
            request = b * mine + r
            rows = query[request * heads : (request + 1) * heads, :].astype(jnp.float32)
            dot = jnp.sum(rows * spread(new, r, 0), axis=1, keepdims=True)
            own = jnp.where(lane == r, dot * (1.0 / math.sqrt(HD)), own)
        maxima, sums = [], []
        for part in parts:
            whole = join_stat(part[b, mine * heads : (mine + 1) * heads, :])
            maxima.append(jnp.where(lane < mine, whole, 0.0))
            sums.append(jnp.where(lane < mine, pltpu.roll(whole, LANES - STAT // 2, 1), 0.0))
        top = functools.reduce(jnp.maximum, maxima, own)
        fresh = jnp.exp(own - top)
        factors = [jnp.exp(m - top) for m in maxima]
        denom = sum((s * f for s, f in zip(sums, factors)), fresh)
        fresh = fresh / denom
        factors = [f / denom for f in factors]
        for r in range(mine):
            numer = fresh[:, r : r + 1] * spread(new, r, 1)
            for part, f in zip(parts, factors):
                rows = part[b, r * heads : (r + 1) * heads, :].astype(jnp.float32)
                numer = numer + f[:, r : r + 1] * rows
            request = b * mine + r
            numers[request * heads : (request + 1) * heads, :] = numer
    for h in range(heads):
        out[:, h * HD : (h + 1) * HD] = numers[
            pl.ds(h, blocks * mine, stride=heads), :
        ].astype(jnp.bfloat16)


def body(
    hidden_in,
    w_query,
    w_keyval,
    w_out,
    key_cache,
    value_cache,
    key_scale,
    value_scale,
    page_counts,
    slot_pages,
    trim,
    seq_size,
    head_size,
):
    requests = hidden_in.shape[0]
    slots = key_cache.shape[0]
    kv_local = w_keyval.shape[1] // (2 * HD)
    heads_local = w_query.shape[1] // HD
    wide = heads_local * HD
    group = heads_local // kv_local
    assert kv_local == 2 and heads_local * CHUNK == LANES
    assert slots % CHUNK == 0
    mine = requests // seq_size
    inverse_square_root = 1.0 / math.sqrt(HD)

    assert slots == LANES and mine & (mine - 1) == 0
    ways = lower_groups(seq_size)[0][1]
    chunks = slots // CHUNK
    smem = pl.BlockSpec(memory_space=pltpu.SMEM)
    vmem = pl.BlockSpec(memory_space=pltpu.VMEM)
    hbm = pl.BlockSpec(memory_space=pl.ANY)
    small = pltpu.CompilerParams(vmem_limit_bytes=6 * 2**20)

    def in_hbm(x):
        return pltpu.with_memory_space_constraint(x, pltpu.HBM)

    tables, place_of = pl.pallas_call(
        functools.partial(table_kernel, seq_size, ways),
        out_shape=[
            jax.ShapeDtypeStruct((4 * chunks, LANES), jnp.float32),
            jax.ShapeDtypeStruct((1, slots), jnp.int32),
        ],
        in_specs=[smem, smem, vmem, vmem, vmem],
        out_specs=[vmem, vmem],
        compiler_params=small,
        name="page_table",
    )(page_counts, trim, slot_pages.reshape(1, slots), key_scale.T, value_scale.T)
    place_of = place_of.reshape(slots)

    held = last_group(seq_size)[1] * mine
    part_shape = jax.ShapeDtypeStruct((seq_size // ways, mine, wide), jnp.float32)
    keyval_shape = jax.ShapeDtypeStruct((requests, w_keyval.shape[1]), jnp.float32)
    *parts, keyval = pl.pallas_call(
        functools.partial(project_kernel, ways),
        out_shape=[part_shape] * ways + [keyval_shape],
        in_specs=[hbm, hbm, hbm],
        out_specs=[vmem] * (ways + 1),
        scratch_shapes=[
            pltpu.VMEM(hidden_in.shape, jnp.bfloat16),
            pltpu.VMEM(w_query.shape, jnp.bfloat16),
            pltpu.VMEM(w_keyval.shape, jnp.bfloat16),
            pltpu.VMEM((requests, wide), jnp.float32),
            pltpu.SemaphoreType.DMA((2, pl.cdiv(w_query.shape[0], 256))),
            pltpu.SemaphoreType.DMA,
        ],
        compiler_params=pltpu.CompilerParams(vmem_limit_bytes=53 * 2**20),
        name="project",
    )(in_hbm(hidden_in), in_hbm(w_query), in_hbm(w_keyval))
    terms, (tables, place_of) = scatter_terms(parts, "seq", seq_size, (tables, place_of))
    my_query = pl.pallas_call(
        join_kernel,
        out_shape=jax.ShapeDtypeStruct((held * heads_local, HD), jnp.bfloat16),
        in_specs=[vmem] * len(terms),
        out_specs=vmem,
        scratch_shapes=[pltpu.VMEM((held * heads_local, HD), jnp.float32)],
        compiler_params=small,
        cost_estimate=pl.CostEstimate(flops=10**10, bytes_accessed=10**7, transcendentals=0),
        name="join",
    )(*terms)
    query = gather_relative(my_query, "seq", seq_size)

    every_row = requests * heads_local
    block_rows = (mine + 1) * heads_local + new_rows(mine)
    totals = pl.pallas_call(
        functools.partial(attention_kernel, ways, mine),
        out_shape=[jax.ShapeDtypeStruct((seq_size // ways, block_rows, HD), jnp.bfloat16)] * ways,
        in_specs=[smem] + [vmem] * (ways + 4),
        out_specs=[vmem] * ways,
        scratch_shapes=[
            pltpu.VMEM((every_row, HD), jnp.bfloat16),
            pltpu.VMEM((every_row, HD), jnp.bfloat16),
            pltpu.VMEM((chunks, LANES, PAGE), jnp.bfloat16),
            pltpu.VMEM((slots * heads_local, HD), jnp.float32),
            pltpu.VMEM((chunks, LANES), jnp.float32),
            pltpu.VMEM((chunks, LANES), jnp.float32),
            pltpu.VMEM((chunks, LANES), jnp.float32),
            pltpu.VMEM((2, every_row, HD), jnp.float32),
            pltpu.VMEM((2, every_row, HD), jnp.float32),
            pltpu.VMEM((requests * 2 * kv_local, HD), jnp.float32),
        ],
        compiler_params=pltpu.CompilerParams(vmem_limit_bytes=24 * 2**20),
        cost_estimate=pl.CostEstimate(
            flops=4 * slots * PAGE * wide,
            bytes_accessed=2 * (key_cache.size + value_cache.size),
            transcendentals=slots * PAGE * heads_local,
        ),
        name="paged_attention",
    )(place_of, *query, keyval, tables, key_cache, value_cache)

    for shift, size in lower_groups(seq_size):
        if shift:
            totals = [pick_digit(totals, "seq", shift, size, d) for d in range(size)]
        parts = swap_all(totals, "seq", seq_size, shift)
        totals = pl.pallas_call(
            functools.partial(combine_kernel, mine),
            out_shape=jax.ShapeDtypeStruct(parts[0].shape, jnp.bfloat16),
            in_specs=[vmem] * size,
            out_specs=vmem,
            compiler_params=pltpu.CompilerParams(vmem_limit_bytes=6 * 2**20),
            name="combine",
        )(*parts)
    shift, size = last_group(seq_size)
    parts = [totals] + [swap(totals, "seq", seq_size, d << shift) for d in range(1, size)]
    my_context = pl.pallas_call(
        functools.partial(finish_kernel, mine),
        out_shape=jax.ShapeDtypeStruct((held, wide), jnp.bfloat16),
        in_specs=[vmem] * (size + 1),
        out_specs=vmem,
        scratch_shapes=[pltpu.VMEM((held * heads_local, HD), jnp.float32)],
        compiler_params=pltpu.CompilerParams(vmem_limit_bytes=6 * 2**20),
        name="finish",
    )(*parts, my_query)

    total = pl.pallas_call(
        functools.partial(output_kernel, ways, seq_size),
        out_shape=jax.ShapeDtypeStruct((requests, w_out.shape[1]), jnp.bfloat16),
        in_specs=[vmem] * (ways + 1),
        out_specs=vmem,
        scratch_shapes=[pltpu.VMEM((requests, w_out.shape[1]), jnp.float32)],
        compiler_params=pltpu.CompilerParams(vmem_limit_bytes=16 * 2**20),
        name="project_out",
    )(*gather_relative(my_context, "seq", seq_size), w_out)
    mask = head_size // 2
    while mask:
        if mask > 1:
            if total.dtype != jnp.bfloat16:
                total = lax.reduce_precision(total, 8, 7).astype(jnp.bfloat16)
            other = swap(total, "head", head_size, mask)
            total = total.astype(jnp.float32) + other.astype(jnp.float32)
        else:
            total = total + swap(total, "head", head_size, mask)
        mask //= 2
    return total.astype(jnp.bfloat16)


def solution(mesh):
    seq_size, head_size = mesh.shape["seq"], mesh.shape["head"]

    def local(*args):
        return body(*args, seq_size=seq_size, head_size=head_size)

    return jax.shard_map(
        local,
        mesh=mesh,
        in_specs=(
            P(None, "seq"),
            P("seq", "head"),
            P("seq", "head"),
            P("head", "seq"),
            P("seq", None, "head"),
            P("seq", None, "head"),
            P("seq", "head"),
            P("seq", "head"),
            P(),
            P("seq"),
            P(),
        ),
        out_specs=P(None, "seq"),
        check_vma=False,
    )
```

```python
import functools
import math

import jax
import jax.numpy as jnp
from jax import lax
from jax.experimental import pallas as pl
from jax.experimental.pallas import tpu as pltpu
from jax.sharding import PartitionSpec as P

HD = 128
PAGE = 128
LANES = 128
CHUNK = 8
STAT = 16


masked_low = -1e30


def swap(x, axis, n, mask):
    return lax.ppermute(x, axis, [(j, j ^ mask) for j in range(n)])


def way_order(size):
    return [0, size - 1, *range(1, size - 1)]


def swap_all(parts, axis, n, shift):
    return [
        swap(parts[d], axis, n, d << shift) if d else parts[0] for d in way_order(len(parts))
    ]


def in_order(parts):
    return [parts[i] for i in sorted(range(len(parts)), key=way_order(len(parts)).__getitem__)]


def bit_groups(n):
    groups, shift = [], 0
    while (1 << shift) < n:
        size = min(4, n >> shift)
        groups.append((shift, size))
        shift += size.bit_length() - 1
    return groups


def lower_groups(n):
    return bit_groups(n)[:-1]


def last_group(n):
    return bit_groups(n)[-1]


def pick_digit(x, axis, shift, size, offset):
    digit = (lax.axis_index(axis) >> shift) % size
    x = x.reshape(x.shape[0] // size, size, *x.shape[1:])
    return lax.dynamic_index_in_dim(x, digit ^ offset, axis=1, keepdims=False)


def scatter_terms(parts, axis, n, beside):
    for shift, size in lower_groups(n):
        if shift:
            parts = [pick_digit(x, axis, shift, size, d) for d in range(size)]
        got = swap_all(parts, axis, n, shift)
        if shift == 0:
            got, beside = lax.optimization_barrier((got, beside))
        x = sum(got[1:], got[0])
    shift, size = last_group(n)
    return [x] + [swap(x, axis, n, d << shift) for d in range(1, size)], beside


def gather_relative(x, axis, n):
    parts = [x]
    for shift, size in reversed(lower_groups(n)):
        x = jnp.concatenate(in_order(parts), axis=0) if len(parts) > 1 else parts[0]
        parts = swap_all([x] * size, axis, n, shift)
    return parts


def relative_place(block, me, n):
    last_shift, _ = last_group(n)
    offset = me ^ block
    place, weight = block >> last_shift, n
    for shift, size in lower_groups(n):
        weight //= size
        place = place + ((offset >> shift) & (size - 1)) * weight
    return place


def gathered_blocks(me, n):
    last_shift, last_size = last_group(n)
    offsets = [0]
    for shift, size in reversed(lower_groups(n)):
        offsets = [d << shift | e for d in range(size) for e in offsets]
    low = me & ((1 << last_shift) - 1)
    return [(c << last_shift) + (low ^ e) for e in offsets for c in range(last_size)]


def table_kernel(seq_size, ways, counts, trim, pages, key_scale, value_scale, tables, place_of):
    requests = counts.shape[0]
    chunks = tables.shape[0] // 4
    heads = LANES // CHUNK
    mine = requests // seq_size
    page = pages[...]
    owner, first, length = [jnp.zeros_like(page)] * 3
    start = 0
    for r in range(requests):
        end = start + counts[r]
        inside = (page >= start) & (page < end)
        owner = owner + jnp.where(page >= end, 1, 0)
        first = jnp.where(inside, start, first)
        length = jnp.where(inside, PAGE * counts[r] - trim[r], length)
        start = end
    valid = length - (page - first) * PAGE
    block = owner >> (mine.bit_length() - 1)
    me = lax.axis_index("seq")
    row = relative_place(block, me, seq_size) * mine + (owner & (mine - 1))
    place_of[...] = ((me & (ways - 1)) << 24) + (row << 16) + owner

    chunk_slot = lax.broadcasted_iota(jnp.int32, (chunks, LANES), 1) // CHUNK
    in_chunk = chunk_slot == lax.broadcasted_iota(jnp.int32, (chunks, LANES), 0)
    slot = lax.broadcasted_iota(jnp.int32, (LANES, LANES), 0) % CHUNK
    lane = lax.broadcasted_iota(jnp.int32, (LANES, LANES), 1)
    same_slot = slot == lane // heads
    low_head = lane % heads < heads // 2

    def spread(row, to):
        rest = jnp.where(in_chunk, jnp.broadcast_to(row, (chunks, LANES)), 0.0)
        total = jnp.zeros((chunks, LANES), jnp.float32)
        for _ in range(3):
            piece = rest.astype(jnp.bfloat16)
            rest = rest - piece.astype(jnp.float32)
            total = total + jnp.dot(
                piece,
                jnp.where(to, 1.0, 0.0).astype(jnp.bfloat16),
                preferred_element_type=jnp.float32,
            )
        return total

    def by_head(scale):
        return spread(scale[0:1, :], same_slot & low_head) + spread(
            scale[1:2, :], same_slot & jnp.logical_not(low_head)
        )

    tables[:chunks, :] = by_head(key_scale) * (1.0 / math.sqrt(HD))
    tables[chunks : 2 * chunks, :] = spread(valid.astype(jnp.float32), same_slot)
    tables[2 * chunks : 3 * chunks, :] = by_head(value_scale)
    tables[3 * chunks :, :] = spread(owner.astype(jnp.float32), same_slot)


def project_kernel(ways, hidden, w_query, w_keyval, *refs):
    outs, (keyval_out, rows_held, query, keyval, result, sem, rows_sem) = refs[:ways], refs[ways:]
    depth = w_query.shape[0]
    tile = min(256, depth)
    copies = [
        [
            pltpu.make_async_copy(
                ref.at[pl.ds(row, tile)], held.at[pl.ds(row, tile)], sem.at[which, row // tile]
            )
            for which, (ref, held) in enumerate(((w_query, query), (w_keyval, keyval)))
        ]
        for row in range(0, depth, tile)
    ]
    rows_copy = pltpu.make_async_copy(hidden, rows_held, rows_sem)
    rows_copy.start()
    for pair in copies:
        for copy in pair:
            copy.start()
    rows_copy.wait()
    for row, pair in zip(range(0, depth, tile), copies):
        here = slice(row, row + tile)
        rows = rows_held[:, here]
        for copy in pair:
            copy.wait()
        for held, to in ((query, result), (keyval, keyval_out)):
            part = jnp.dot(rows, held[here, :], preferred_element_type=jnp.float32)
            to[...] = to[...] + part if row else part
    digit = lax.axis_index("seq") & (ways - 1)
    for d, out in enumerate(outs):
        blocks, mine, _ = out.shape
        for b in range(blocks):
            if mine % 8 == 0:
                first = (b * ways + (digit ^ d)) * mine
                out[b] = result[pl.ds(pl.multiple_of(first, mine), mine), :]
                continue
            chosen = result[b * ways * mine : (b * ways + 1) * mine, :]
            for j in range(1, ways):
                first = (b * ways + j) * mine
                chosen = jnp.where((digit ^ d) == j, result[first : first + mine, :], chosen)
            out[b] = chosen


def output_kernel(ways, seq_size, *refs):
    parts, (w_out, rounded, out) = refs[:ways], refs[ways:]
    rows = jnp.concatenate([part[...] for part in in_order(parts)], axis=0)
    total = jnp.dot(rows, w_out[...], preferred_element_type=jnp.float32)
    blocks = gathered_blocks(lax.axis_index("seq"), seq_size)
    mine = rows.shape[0] // len(blocks)
    if mine % 8 == 0:
        for i, block in enumerate(blocks):
            here = pl.ds(pl.multiple_of(block * mine, mine), mine)
            out[here, :] = total[i * mine : (i + 1) * mine]
        rounded[...] = out[...].astype(jnp.bfloat16)
        return
    for place in range(len(blocks)):
        chosen = total[:mine]
        for i, block in enumerate(blocks):
            chosen = jnp.where(block == place, total[i * mine : (i + 1) * mine], chosen)
        out[place * mine : (place + 1) * mine, :] = chosen
    rounded[...] = out[...].astype(jnp.bfloat16)


def join_kernel(*refs):
    *parts, out, rows = refs
    blocks, mine, columns = parts[0].shape
    held = blocks * mine
    whole = functools.reduce(jnp.add, [part[...] for part in parts]).reshape(held, columns)
    heads = columns // HD
    for h in range(heads):
        rows[pl.ds(h, held, stride=heads), :] = whole[:, h * HD : (h + 1) * HD]
    out[...] = rows[...].astype(jnp.bfloat16)


def new_rows(mine):
    return -(-4 * mine // 16) * 16


def split_stat(stat, lane):
    hi = stat.astype(jnp.bfloat16).astype(jnp.float32)
    rest = stat - hi
    mid = rest.astype(jnp.bfloat16).astype(jnp.float32)
    piece = jnp.where(lane < STAT, hi, jnp.where(lane < 2 * STAT, mid, rest - mid))
    return piece.astype(jnp.bfloat16)


def join_stat(pieces):
    pieces = pieces.astype(jnp.float32)
    return (pieces + pltpu.roll(pieces, LANES - STAT, 1)) + pltpu.roll(
        pieces, LANES - 2 * STAT, 1
    )


def attention_kernel(ways, mine, place_of, *refs):
    queries, refs = refs[:ways], refs[ways:]
    (keyval, tables, keys, values), refs = refs[:4], refs[4:]
    outs, refs = refs[:ways], refs[ways:]
    (
        query_low,
        query_high,
        probs,
        page_out,
        page_sum,
        page_max,
        dev_max,
        total_out,
        total_stat,
        keyval_rows,
    ) = refs
    slots = keys.shape[0]
    heads = LANES // CHUNK
    group = heads // 2
    chunks = slots // CHUNK
    blocks = outs[0].shape[0]
    lag = 2

    for d, part in enumerate(in_order(queries)):
        rows = part[...]
        low_head = lax.broadcasted_iota(jnp.int32, rows.shape, 0) % heads < group
        zero = jnp.zeros_like(rows)
        here = slice(rows.shape[0] * d, rows.shape[0] * (d + 1))
        query_low[here, :] = jnp.where(low_head, rows, zero)
        query_high[here, :] = jnp.where(low_head, zero, rows)
    total_out[...] = jnp.zeros_like(total_out)
    stat_lane = lax.broadcasted_iota(jnp.int32, total_stat.shape, 2) % STAT
    total_stat[...] = jnp.where(stat_lane < STAT // 2, masked_low, 0.0)

    def table(which, c):
        return tables[pl.ds(which * chunks + c, 1), :]

    lane_slot = lax.broadcasted_iota(jnp.int32, (PAGE, LANES), 1) // heads
    token = lax.broadcasted_iota(jnp.int32, (PAGE, LANES), 0).astype(jnp.float32)

    def score_chunk(c):
        places = [
            pl.multiple_of(((place_of[c * CHUNK + s] >> 16) & 0xFF) * heads, heads)
            for s in range(CHUNK)
        ]
        chosen = jnp.concatenate(
            [
                jnp.concatenate([ref[pl.ds(place, heads), :] for place in places], axis=0)
                for ref in (query_low, query_high)
            ],
            axis=1,
        )
        block = keys[pl.ds(c * CHUNK, CHUNK)].reshape(CHUNK * PAGE, 2 * HD)
        every = lax.dot_general(
            block, chosen, (((1,), (1,)), ((), ())), preferred_element_type=jnp.float32
        )
        score = every[:PAGE]
        for s in range(1, CHUNK):
            score = jnp.where(lane_slot == s, every[s * PAGE : (s + 1) * PAGE], score)
        score = jnp.where(token < table(1, c), score * table(0, c), masked_low)
        top = jnp.max(score, axis=0, keepdims=True)
        page_max[pl.ds(c, 1), :] = top
        prob = jnp.exp(score - top).astype(jnp.bfloat16).astype(jnp.float32)
        page_sum[pl.ds(c, 1), :] = jnp.sum(prob, axis=0, keepdims=True)
        probs[c] = prob.T.astype(jnp.bfloat16)

    empty = jnp.zeros((heads, PAGE), jnp.bfloat16)

    def value_chunk(c):
        prob = probs[c]
        for s in range(0, CHUNK, 2):
            pair = jnp.concatenate(
                [
                    jnp.concatenate([prob[s * heads : (s + 1) * heads], empty], axis=1),
                    jnp.concatenate([empty, prob[(s + 1) * heads : (s + 2) * heads]], axis=1),
                ],
                axis=0,
            )
            block = values[pl.ds(c * CHUNK + s, 2)].reshape(2 * PAGE, 2 * HD)
            both = jnp.dot(pair, block, preferred_element_type=jnp.float32)
            page_out[pl.ds(pl.multiple_of((c * CHUNK + s) * heads, heads), 2 * heads), :] = (
                jnp.concatenate(
                    [
                        both[:group, :HD],
                        both[group:heads, HD:],
                        both[heads : heads + group, :HD],
                        both[heads + group :, HD:],
                    ],
                    axis=0,
                )
            )

    for c in range(chunks + lag):
        if c >= lag:
            value_chunk(c - lag)
        if c < chunks:
            score_chunk(c)

    biggest, who = page_max[...], tables[3 * chunks :, :]
    best = biggest
    for turn in range(CHUNK):
        other = pltpu.roll(biggest, turn * heads, 1) if turn else biggest
        other_who = pltpu.roll(who, turn * heads, 1) if turn else who
        for c in range(chunks):
            best = jnp.maximum(
                best, jnp.where(other_who[c : c + 1] == who, other[c : c + 1], masked_low)
            )
    dev_max[...] = best

    keep_max = lax.broadcasted_iota(jnp.int32, (heads, LANES), 1) % STAT < STAT // 2

    keep_max_row = lax.broadcasted_iota(jnp.int32, (PAGE, LANES), 0) % STAT < STAT // 2

    for c in range(chunks):
        top = dev_max[pl.ds(c, 1), :]
        weight = jnp.exp(page_max[pl.ds(c, 1), :] - top)
        out_weight = jnp.broadcast_to(weight * table(2, c), (PAGE, LANES)).T
        stat = jnp.where(keep_max_row, top, weight * page_sum[pl.ds(c, 1), :]).T
        for s in range(CHUNK):
            here = pl.ds(
                pl.multiple_of((place_of[c * CHUNK + s] & 0xFFFF) * heads, heads), heads
            )
            there = pl.ds(pl.multiple_of((c * CHUNK + s) * heads, heads), heads)
            part = slice(s * heads, (s + 1) * heads)
            turn = s % 2
            total_out[turn, here, :] += page_out[there, :] * out_weight[part]
            total_stat[turn, here, :] = jnp.where(
                keep_max, stat[part], total_stat[turn, here, :] + stat[part]
            )

    lane = lax.broadcasted_iota(jnp.int32, (heads, LANES), 1)
    digit = place_of[0] >> 24
    for j in range(4):
        keyval_rows[pl.ds(j, keyval.shape[0], stride=4), :] = keyval[:, j * HD : (j + 1) * HD]
    for d, out in enumerate(outs):
        for b in range(blocks):
            block = b * ways + (digit ^ d)
            rows = pl.ds(pl.multiple_of(block * (mine * heads), mine * heads), mine * heads)
            out[b, : mine * heads, :] = (total_out[0, rows, :] + total_out[1, rows, :]).astype(
                jnp.bfloat16
            )
            even, odd = total_stat[0, rows, :], total_stat[1, rows, :]
            is_max = lax.broadcasted_iota(jnp.int32, even.shape, 1) % STAT < STAT // 2
            both = jnp.where(is_max, jnp.maximum(even, odd), even + odd)
            stat = jnp.zeros((heads, LANES), jnp.float32)
            for r in range(mine):
                stat = jnp.where(
                    lane % (STAT // 2) == r, both[r * heads : (r + 1) * heads], stat
                )
            out[b, mine * heads : (mine + 1) * heads, :] = split_stat(stat, lane)
            new = keyval_rows[pl.ds(pl.multiple_of(block * (4 * mine), 4 * mine), 4 * mine), :]
            if new.shape[0] < new_rows(mine):
                empty_rows = jnp.zeros((new_rows(mine) - new.shape[0], LANES), jnp.float32)
                new = jnp.concatenate([new, empty_rows], axis=0)
            out[b, (mine + 1) * heads :, :] = new.astype(jnp.bfloat16)


def combine_kernel(mine, *refs):
    *parts, out = refs
    blocks = out.shape[0]
    heads = LANES // CHUNK
    lane = lax.broadcasted_iota(jnp.int32, (heads, LANES), 1)
    for b in range(blocks):
        stats = [join_stat(part[b, mine * heads : (mine + 1) * heads, :]) for part in parts]
        maxima = [jnp.where(lane < mine, stat, 0.0) for stat in stats]
        top = functools.reduce(jnp.maximum, maxima)
        factors = [jnp.exp(m - top) for m in maxima]
        sums = sum(
            pltpu.roll(f, STAT // 2, 1) * jnp.where(lane < STAT, stat, 0.0)
            for f, stat in zip(factors, stats)
        )
        both = jnp.where(lane < STAT // 2, top, sums)
        both = jnp.where(lane < STAT, both, 0.0)
        both = (both + pltpu.roll(both, STAT, 1)) + pltpu.roll(both, 2 * STAT, 1)
        out[b, mine * heads : (mine + 1) * heads, :] = split_stat(both, lane)
        new = sum(part[b, (mine + 1) * heads :, :].astype(jnp.float32) for part in parts)
        out[b, (mine + 1) * heads :, :] = new.astype(jnp.bfloat16)
        for r in range(mine):
            rows = slice(r * heads, (r + 1) * heads)
            numer = sum(
                f[:, r : r + 1] * part[b, rows, :].astype(jnp.float32)
                for f, part in zip(factors, parts)
            )
            out[b, rows, :] = numer.astype(jnp.bfloat16)


def finish_kernel(mine, *refs):
    *parts, query, out, numers = refs
    blocks = parts[0].shape[0]
    heads = LANES // CHUNK
    group = heads // 2
    lane = lax.broadcasted_iota(jnp.int32, (heads, LANES), 1)
    low_head = lax.broadcasted_iota(jnp.int32, (heads, LANES), 0) < group
    def spread(new, r, which):
        low = jnp.broadcast_to(new[4 * r + which : 4 * r + which + 1], (heads, LANES))
        high = jnp.broadcast_to(new[4 * r + 2 + which : 4 * r + 3 + which], (heads, LANES))
        return jnp.where(low_head, low, high)

    for b in range(blocks):
        new = sum(part[b, (mine + 1) * heads :, :].astype(jnp.float32) for part in parts)
        new = new.astype(jnp.bfloat16).astype(jnp.float32)
        own = jnp.zeros((heads, LANES), jnp.float32)
        for r in range(mine):
            request = b * mine + r
            rows = query[request * heads : (request + 1) * heads, :].astype(jnp.float32)
            dot = jnp.sum(rows * spread(new, r, 0), axis=1, keepdims=True)
            own = jnp.where(lane == r, dot * (1.0 / math.sqrt(HD)), own)
        maxima, sums = [], []
        for part in parts:
            whole = join_stat(part[b, mine * heads : (mine + 1) * heads, :])
            maxima.append(jnp.where(lane < mine, whole, 0.0))
            sums.append(jnp.where(lane < mine, pltpu.roll(whole, LANES - STAT // 2, 1), 0.0))
        top = functools.reduce(jnp.maximum, maxima, own)
        fresh = jnp.exp(own - top)
        factors = [jnp.exp(m - top) for m in maxima]
        denom = sum((s * f for s, f in zip(sums, factors)), fresh)
        fresh = fresh / denom
        factors = [f / denom for f in factors]
        for r in range(mine):
            numer = fresh[:, r : r + 1] * spread(new, r, 1)
            for part, f in zip(parts, factors):
                rows = part[b, r * heads : (r + 1) * heads, :].astype(jnp.float32)
                numer = numer + f[:, r : r + 1] * rows
            request = b * mine + r
            numers[request * heads : (request + 1) * heads, :] = numer
    for h in range(heads):
        out[:, h * HD : (h + 1) * HD] = numers[
            pl.ds(h, blocks * mine, stride=heads), :
        ].astype(jnp.bfloat16)


def body(
    hidden_in,
    w_query,
    w_keyval,
    w_out,
    key_cache,
    value_cache,
    key_scale,
    value_scale,
    page_counts,
    slot_pages,
    trim,
    seq_size,
    head_size,
):
    requests = hidden_in.shape[0]
    slots = key_cache.shape[0]
    kv_local = w_keyval.shape[1] // (2 * HD)
    heads_local = w_query.shape[1] // HD
    wide = heads_local * HD
    group = heads_local // kv_local
    assert kv_local == 2 and heads_local * CHUNK == LANES
    assert slots % CHUNK == 0
    mine = requests // seq_size
    inverse_square_root = 1.0 / math.sqrt(HD)

    assert slots == LANES and mine & (mine - 1) == 0
    ways = lower_groups(seq_size)[0][1]
    chunks = slots // CHUNK
    smem = pl.BlockSpec(memory_space=pltpu.SMEM)
    vmem = pl.BlockSpec(memory_space=pltpu.VMEM)
    hbm = pl.BlockSpec(memory_space=pl.ANY)
    small = pltpu.CompilerParams(vmem_limit_bytes=6 * 2**20)

    def in_hbm(x):
        return pltpu.with_memory_space_constraint(x, pltpu.HBM)

    tables, place_of = pl.pallas_call(
        functools.partial(table_kernel, seq_size, ways),
        out_shape=[
            jax.ShapeDtypeStruct((4 * chunks, LANES), jnp.float32),
            jax.ShapeDtypeStruct((1, slots), jnp.int32),
        ],
        in_specs=[smem, smem, vmem, vmem, vmem],
        out_specs=[vmem, vmem],
        compiler_params=small,
        name="page_table",
    )(page_counts, trim, slot_pages.reshape(1, slots), key_scale.T, value_scale.T)
    place_of = place_of.reshape(slots)

    held = last_group(seq_size)[1] * mine
    part_shape = jax.ShapeDtypeStruct((seq_size // ways, mine, wide), jnp.float32)
    keyval_shape = jax.ShapeDtypeStruct((requests, w_keyval.shape[1]), jnp.float32)
    *parts, keyval = pl.pallas_call(
        functools.partial(project_kernel, ways),
        out_shape=[part_shape] * ways + [keyval_shape],
        in_specs=[hbm, hbm, hbm],
        out_specs=[vmem] * (ways + 1),
        scratch_shapes=[
            pltpu.VMEM(hidden_in.shape, jnp.bfloat16),
            pltpu.VMEM(w_query.shape, jnp.bfloat16),
            pltpu.VMEM(w_keyval.shape, jnp.bfloat16),
            pltpu.VMEM((requests, wide), jnp.float32),
            pltpu.SemaphoreType.DMA((2, pl.cdiv(w_query.shape[0], 256))),
            pltpu.SemaphoreType.DMA,
        ],
        compiler_params=pltpu.CompilerParams(vmem_limit_bytes=53 * 2**20),
        name="project",
    )(in_hbm(hidden_in), in_hbm(w_query), in_hbm(w_keyval))
    terms, (tables, place_of) = scatter_terms(parts, "seq", seq_size, (tables, place_of))
    my_query = pl.pallas_call(
        join_kernel,
        out_shape=jax.ShapeDtypeStruct((held * heads_local, HD), jnp.bfloat16),
        in_specs=[vmem] * len(terms),
        out_specs=vmem,
        scratch_shapes=[pltpu.VMEM((held * heads_local, HD), jnp.float32)],
        compiler_params=small,
        cost_estimate=pl.CostEstimate(flops=10**10, bytes_accessed=10**7, transcendentals=0),
        name="join",
    )(*terms)
    query = gather_relative(my_query, "seq", seq_size)

    every_row = requests * heads_local
    block_rows = (mine + 1) * heads_local + new_rows(mine)
    totals = pl.pallas_call(
        functools.partial(attention_kernel, ways, mine),
        out_shape=[jax.ShapeDtypeStruct((seq_size // ways, block_rows, HD), jnp.bfloat16)] * ways,
        in_specs=[smem] + [vmem] * (ways + 4),
        out_specs=[vmem] * ways,
        scratch_shapes=[
            pltpu.VMEM((every_row, HD), jnp.bfloat16),
            pltpu.VMEM((every_row, HD), jnp.bfloat16),
            pltpu.VMEM((chunks, LANES, PAGE), jnp.bfloat16),
            pltpu.VMEM((slots * heads_local, HD), jnp.float32),
            pltpu.VMEM((chunks, LANES), jnp.float32),
            pltpu.VMEM((chunks, LANES), jnp.float32),
            pltpu.VMEM((chunks, LANES), jnp.float32),
            pltpu.VMEM((2, every_row, HD), jnp.float32),
            pltpu.VMEM((2, every_row, HD), jnp.float32),
            pltpu.VMEM((requests * 2 * kv_local, HD), jnp.float32),
        ],
        compiler_params=pltpu.CompilerParams(vmem_limit_bytes=24 * 2**20),
        cost_estimate=pl.CostEstimate(
            flops=4 * slots * PAGE * wide,
            bytes_accessed=2 * (key_cache.size + value_cache.size),
            transcendentals=slots * PAGE * heads_local,
        ),
        name="paged_attention",
    )(place_of, *query, keyval, tables, key_cache, value_cache)

    for shift, size in lower_groups(seq_size):
        if shift:
            totals = [pick_digit(totals, "seq", shift, size, d) for d in range(size)]
        parts = swap_all(totals, "seq", seq_size, shift)
        totals = pl.pallas_call(
            functools.partial(combine_kernel, mine),
            out_shape=jax.ShapeDtypeStruct(parts[0].shape, jnp.bfloat16),
            in_specs=[vmem] * size,
            out_specs=vmem,
            compiler_params=pltpu.CompilerParams(vmem_limit_bytes=6 * 2**20),
            name="combine",
        )(*parts)
    shift, size = last_group(seq_size)
    parts = [totals] + [swap(totals, "seq", seq_size, d << shift) for d in range(1, size)]
    my_context = pl.pallas_call(
        functools.partial(finish_kernel, mine),
        out_shape=jax.ShapeDtypeStruct((held, wide), jnp.bfloat16),
        in_specs=[vmem] * (size + 1),
        out_specs=vmem,
        scratch_shapes=[pltpu.VMEM((held * heads_local, HD), jnp.float32)],
        compiler_params=pltpu.CompilerParams(vmem_limit_bytes=6 * 2**20),
        name="finish",
    )(*parts, my_query)

    total = pl.pallas_call(
        functools.partial(output_kernel, ways, seq_size),
        out_shape=jax.ShapeDtypeStruct((requests, w_out.shape[1]), jnp.bfloat16),
        in_specs=[vmem] * (ways + 1),
        out_specs=vmem,
        scratch_shapes=[pltpu.VMEM((requests, w_out.shape[1]), jnp.float32)],
        compiler_params=pltpu.CompilerParams(vmem_limit_bytes=16 * 2**20),
        name="project_out",
    )(*gather_relative(my_context, "seq", seq_size), w_out)
    mask = head_size // 2
    while mask:
        if total.dtype != jnp.bfloat16:
            total = lax.reduce_precision(total, 8, 7).astype(jnp.bfloat16)
        other = swap(total, "head", head_size, mask)
        total = total.astype(jnp.float32) + other.astype(jnp.float32)
        mask //= 2
    return total.astype(jnp.bfloat16)


def solution(mesh):
    seq_size, head_size = mesh.shape["seq"], mesh.shape["head"]

    def local(*args):
        return body(*args, seq_size=seq_size, head_size=head_size)

    return jax.shard_map(
        local,
        mesh=mesh,
        in_specs=(
            P(None, "seq"),
            P("seq", "head"),
            P("seq", "head"),
            P("head", "seq"),
            P("seq", None, "head"),
            P("seq", None, "head"),
            P("seq", "head"),
            P("seq", "head"),
            P(),
            P("seq"),
            P(),
        ),
        out_specs=P(None, "seq"),
        check_vma=False,
    )
```

```python
import functools
import math

import jax
import jax.numpy as jnp
from jax import lax
from jax.experimental import pallas as pl
from jax.experimental.pallas import tpu as pltpu
from jax.sharding import PartitionSpec as P

HD = 128
PAGE = 128
LANES = 128
CHUNK = 8
STAT = 16


masked_low = -1e30


def swap(x, axis, n, mask):
    return lax.ppermute(x, axis, [(j, j ^ mask) for j in range(n)])


def way_order(size):
    return [0, size - 1, *range(1, size - 1)]


def swap_all(parts, axis, n, shift):
    return [
        swap(parts[d], axis, n, d << shift) if d else parts[0] for d in way_order(len(parts))
    ]


def in_order(parts):
    return [parts[i] for i in sorted(range(len(parts)), key=way_order(len(parts)).__getitem__)]


def bit_groups(n):
    groups, shift = [], 0
    while (1 << shift) < n:
        size = min(4, n >> shift)
        groups.append((shift, size))
        shift += size.bit_length() - 1
    return groups


def lower_groups(n):
    return bit_groups(n)[:-1]


def last_group(n):
    return bit_groups(n)[-1]


def pick_digit(x, axis, shift, size, offset):
    digit = (lax.axis_index(axis) >> shift) % size
    x = x.reshape(x.shape[0] // size, size, *x.shape[1:])
    return lax.dynamic_index_in_dim(x, digit ^ offset, axis=1, keepdims=False)


def scatter_terms(parts, axis, n, beside):
    for shift, size in lower_groups(n):
        if shift:
            parts = [pick_digit(x, axis, shift, size, d) for d in range(size)]
        got = swap_all(parts, axis, n, shift)
        if shift == 0:
            got, beside = lax.optimization_barrier((got, beside))
        x = sum(got[1:], got[0])
    shift, size = last_group(n)
    return [x] + [swap(x, axis, n, d << shift) for d in range(1, size)], beside


def gather_relative(x, axis, n):
    parts = [x]
    for shift, size in reversed(lower_groups(n)):
        x = jnp.concatenate(in_order(parts), axis=0) if len(parts) > 1 else parts[0]
        parts = swap_all([x] * size, axis, n, shift)
    return parts


def relative_place(block, me, n):
    last_shift, _ = last_group(n)
    offset = me ^ block
    place, weight = block >> last_shift, n
    for shift, size in lower_groups(n):
        weight //= size
        place = place + ((offset >> shift) & (size - 1)) * weight
    return place


def gathered_blocks(me, n):
    last_shift, last_size = last_group(n)
    offsets = [0]
    for shift, size in reversed(lower_groups(n)):
        offsets = [d << shift | e for d in range(size) for e in offsets]
    low = me & ((1 << last_shift) - 1)
    return [(c << last_shift) + (low ^ e) for e in offsets for c in range(last_size)]


def table_kernel(seq_size, ways, counts, trim, pages, key_scale, value_scale, tables, place_of):
    requests = counts.shape[0]
    chunks = tables.shape[0] // 4
    heads = LANES // CHUNK
    mine = requests // seq_size
    page = pages[...]
    owner, first, length = [jnp.zeros_like(page)] * 3
    start = 0
    for r in range(requests):
        end = start + counts[r]
        inside = (page >= start) & (page < end)
        owner = owner + jnp.where(page >= end, 1, 0)
        first = jnp.where(inside, start, first)
        length = jnp.where(inside, PAGE * counts[r] - trim[r], length)
        start = end
    valid = length - (page - first) * PAGE
    block = owner >> (mine.bit_length() - 1)
    me = lax.axis_index("seq")
    row = relative_place(block, me, seq_size) * mine + (owner & (mine - 1))
    place_of[...] = ((me & (ways - 1)) << 24) + (row << 16) + owner

    chunk_slot = lax.broadcasted_iota(jnp.int32, (chunks, LANES), 1) // CHUNK
    in_chunk = chunk_slot == lax.broadcasted_iota(jnp.int32, (chunks, LANES), 0)
    slot = lax.broadcasted_iota(jnp.int32, (LANES, LANES), 0) % CHUNK
    lane = lax.broadcasted_iota(jnp.int32, (LANES, LANES), 1)
    same_slot = slot == lane // heads
    low_head = lane % heads < heads // 2

    def spread(row, to):
        rest = jnp.where(in_chunk, jnp.broadcast_to(row, (chunks, LANES)), 0.0)
        total = jnp.zeros((chunks, LANES), jnp.float32)
        for _ in range(3):
            piece = rest.astype(jnp.bfloat16)
            rest = rest - piece.astype(jnp.float32)
            total = total + jnp.dot(
                piece,
                jnp.where(to, 1.0, 0.0).astype(jnp.bfloat16),
                preferred_element_type=jnp.float32,
            )
        return total

    def by_head(scale):
        return spread(scale[0:1, :], same_slot & low_head) + spread(
            scale[1:2, :], same_slot & jnp.logical_not(low_head)
        )

    tables[:chunks, :] = by_head(key_scale) * (1.0 / math.sqrt(HD))
    tables[chunks : 2 * chunks, :] = spread(valid.astype(jnp.float32), same_slot)
    tables[2 * chunks : 3 * chunks, :] = by_head(value_scale)
    tables[3 * chunks :, :] = spread(owner.astype(jnp.float32), same_slot)


def project_kernel(ways, hidden, w_query, w_keyval, *refs):
    outs, (keyval_out, rows_held, query, keyval, result, sem, rows_sem) = refs[:ways], refs[ways:]
    depth = w_query.shape[0]
    tile = min(256, depth)
    copies = [
        [
            pltpu.make_async_copy(
                ref.at[pl.ds(row, tile)], held.at[pl.ds(row, tile)], sem.at[which, row // tile]
            )
            for which, (ref, held) in enumerate(((w_query, query), (w_keyval, keyval)))
        ]
        for row in range(0, depth, tile)
    ]
    rows_copy = pltpu.make_async_copy(hidden, rows_held, rows_sem)
    rows_copy.start()
    for pair in copies:
        for copy in pair:
            copy.start()
    rows_copy.wait()
    for row, pair in zip(range(0, depth, tile), copies):
        here = slice(row, row + tile)
        rows = rows_held[:, here]
        for copy in pair:
            copy.wait()
        for held, to in ((query, result), (keyval, keyval_out)):
            part = jnp.dot(rows, held[here, :], preferred_element_type=jnp.float32)
            to[...] = to[...] + part if row else part
    digit = lax.axis_index("seq") & (ways - 1)
    for d, out in enumerate(outs):
        blocks, mine, _ = out.shape
        for b in range(blocks):
            if mine % 8 == 0:
                first = (b * ways + (digit ^ d)) * mine
                out[b] = result[pl.ds(pl.multiple_of(first, mine), mine), :]
                continue
            chosen = result[b * ways * mine : (b * ways + 1) * mine, :]
            for j in range(1, ways):
                first = (b * ways + j) * mine
                chosen = jnp.where((digit ^ d) == j, result[first : first + mine, :], chosen)
            out[b] = chosen


def output_kernel(ways, seq_size, *refs):
    parts, (w_out, rounded, out) = refs[:ways], refs[ways:]
    rows = jnp.concatenate([part[...] for part in in_order(parts)], axis=0)
    total = jnp.dot(rows, w_out[...], preferred_element_type=jnp.float32)
    blocks = gathered_blocks(lax.axis_index("seq"), seq_size)
    mine = rows.shape[0] // len(blocks)
    if mine % 8 == 0:
        for i, block in enumerate(blocks):
            here = pl.ds(pl.multiple_of(block * mine, mine), mine)
            out[here, :] = total[i * mine : (i + 1) * mine]
        rounded[...] = out[...].astype(jnp.bfloat16)
        return
    for place in range(len(blocks)):
        chosen = total[:mine]
        for i, block in enumerate(blocks):
            chosen = jnp.where(block == place, total[i * mine : (i + 1) * mine], chosen)
        out[place * mine : (place + 1) * mine, :] = chosen
    rounded[...] = out[...].astype(jnp.bfloat16)


def join_kernel(*refs):
    *parts, out, rows = refs
    blocks, mine, columns = parts[0].shape
    held = blocks * mine
    whole = functools.reduce(jnp.add, [part[...] for part in parts]).reshape(held, columns)
    heads = columns // HD
    for h in range(heads):
        rows[pl.ds(h, held, stride=heads), :] = whole[:, h * HD : (h + 1) * HD]
    out[...] = rows[...].astype(jnp.bfloat16)


def new_rows(mine):
    return -(-4 * mine // 16) * 16


def split_stat(stat, lane):
    hi = stat.astype(jnp.bfloat16).astype(jnp.float32)
    rest = stat - hi
    mid = rest.astype(jnp.bfloat16).astype(jnp.float32)
    piece = jnp.where(lane < STAT, hi, jnp.where(lane < 2 * STAT, mid, rest - mid))
    return piece.astype(jnp.bfloat16)


def join_stat(pieces):
    pieces = pieces.astype(jnp.float32)
    return (pieces + pltpu.roll(pieces, LANES - STAT, 1)) + pltpu.roll(
        pieces, LANES - 2 * STAT, 1
    )


def attention_kernel(ways, mine, place_of, *refs):
    queries, refs = refs[:ways], refs[ways:]
    (keyval, tables, keys, values), refs = refs[:4], refs[4:]
    outs, refs = refs[:ways], refs[ways:]
    (
        query_low,
        query_high,
        probs,
        page_out,
        page_sum,
        page_max,
        dev_max,
        total_out,
        total_stat,
        keyval_rows,
    ) = refs
    slots = keys.shape[0]
    heads = LANES // CHUNK
    group = heads // 2
    chunks = slots // CHUNK
    blocks = outs[0].shape[0]
    lag = 8

    for d, part in enumerate(in_order(queries)):
        rows = part[...]
        low_head = lax.broadcasted_iota(jnp.int32, rows.shape, 0) % heads < group
        zero = jnp.zeros_like(rows)
        here = slice(rows.shape[0] * d, rows.shape[0] * (d + 1))
        query_low[here, :] = jnp.where(low_head, rows, zero)
        query_high[here, :] = jnp.where(low_head, zero, rows)
    total_out[...] = jnp.zeros_like(total_out)
    stat_lane = lax.broadcasted_iota(jnp.int32, total_stat.shape, 2) % STAT
    total_stat[...] = jnp.where(stat_lane < STAT // 2, masked_low, 0.0)

    def table(which, c):
        return tables[pl.ds(which * chunks + c, 1), :]

    lane_slot = lax.broadcasted_iota(jnp.int32, (PAGE, LANES), 1) // heads
    token = lax.broadcasted_iota(jnp.int32, (PAGE, LANES), 0).astype(jnp.float32)

    def score_chunk(c):
        places = [
            pl.multiple_of(((place_of[c * CHUNK + s] >> 16) & 0xFF) * heads, heads)
            for s in range(CHUNK)
        ]
        chosen = jnp.concatenate(
            [
                jnp.concatenate([ref[pl.ds(place, heads), :] for place in places], axis=0)
                for ref in (query_low, query_high)
            ],
            axis=1,
        )
        block = keys[pl.ds(c * CHUNK, CHUNK)].reshape(CHUNK * PAGE, 2 * HD)
        every = lax.dot_general(
            block, chosen, (((1,), (1,)), ((), ())), preferred_element_type=jnp.float32
        )
        score = every[:PAGE]
        for s in range(1, CHUNK):
            score = jnp.where(lane_slot == s, every[s * PAGE : (s + 1) * PAGE], score)
        score = jnp.where(token < table(1, c), score * table(0, c), masked_low)
        top = jnp.max(score, axis=0, keepdims=True)
        page_max[pl.ds(c, 1), :] = top
        prob = jnp.exp(score - top).astype(jnp.bfloat16).astype(jnp.float32)
        page_sum[pl.ds(c, 1), :] = jnp.sum(prob, axis=0, keepdims=True)
        probs[c] = prob.T.astype(jnp.bfloat16)

    empty = jnp.zeros((heads, PAGE), jnp.bfloat16)

    def value_chunk(c):
        prob = probs[c]
        for s in range(0, CHUNK, 2):
            pair = jnp.concatenate(
                [
                    jnp.concatenate([prob[s * heads : (s + 1) * heads], empty], axis=1),
                    jnp.concatenate([empty, prob[(s + 1) * heads : (s + 2) * heads]], axis=1),
                ],
                axis=0,
            )
            block = values[pl.ds(c * CHUNK + s, 2)].reshape(2 * PAGE, 2 * HD)
            both = jnp.dot(pair, block, preferred_element_type=jnp.float32)
            page_out[pl.ds(pl.multiple_of((c * CHUNK + s) * heads, heads), 2 * heads), :] = (
                jnp.concatenate(
                    [
                        both[:group, :HD],
                        both[group:heads, HD:],
                        both[heads : heads + group, :HD],
                        both[heads + group :, HD:],
                    ],
                    axis=0,
                )
            )

    for c in range(chunks + lag):
        if c >= lag:
            value_chunk(c - lag)
        if c < chunks:
            score_chunk(c)

    biggest, who = page_max[...], tables[3 * chunks :, :]
    best = biggest
    for turn in range(CHUNK):
        other = pltpu.roll(biggest, turn * heads, 1) if turn else biggest
        other_who = pltpu.roll(who, turn * heads, 1) if turn else who
        for c in range(chunks):
            best = jnp.maximum(
                best, jnp.where(other_who[c : c + 1] == who, other[c : c + 1], masked_low)
            )
    dev_max[...] = best

    keep_max = lax.broadcasted_iota(jnp.int32, (heads, LANES), 1) % STAT < STAT // 2

    keep_max_row = lax.broadcasted_iota(jnp.int32, (PAGE, LANES), 0) % STAT < STAT // 2

    for c in range(chunks):
        top = dev_max[pl.ds(c, 1), :]
        weight = jnp.exp(page_max[pl.ds(c, 1), :] - top)
        out_weight = jnp.broadcast_to(weight * table(2, c), (PAGE, LANES)).T
        stat = jnp.where(keep_max_row, top, weight * page_sum[pl.ds(c, 1), :]).T
        for s in range(CHUNK):
            here = pl.ds(
                pl.multiple_of((place_of[c * CHUNK + s] & 0xFFFF) * heads, heads), heads
            )
            there = pl.ds(pl.multiple_of((c * CHUNK + s) * heads, heads), heads)
            part = slice(s * heads, (s + 1) * heads)
            turn = s % 2
            total_out[turn, here, :] += page_out[there, :] * out_weight[part]
            total_stat[turn, here, :] = jnp.where(
                keep_max, stat[part], total_stat[turn, here, :] + stat[part]
            )

    lane = lax.broadcasted_iota(jnp.int32, (heads, LANES), 1)
    digit = place_of[0] >> 24
    for j in range(4):
        keyval_rows[pl.ds(j, keyval.shape[0], stride=4), :] = keyval[:, j * HD : (j + 1) * HD]
    for d, out in enumerate(outs):
        for b in range(blocks):
            block = b * ways + (digit ^ d)
            rows = pl.ds(pl.multiple_of(block * (mine * heads), mine * heads), mine * heads)
            out[b, : mine * heads, :] = (total_out[0, rows, :] + total_out[1, rows, :]).astype(
                jnp.bfloat16
            )
            even, odd = total_stat[0, rows, :], total_stat[1, rows, :]
            is_max = lax.broadcasted_iota(jnp.int32, even.shape, 1) % STAT < STAT // 2
            both = jnp.where(is_max, jnp.maximum(even, odd), even + odd)
            stat = jnp.zeros((heads, LANES), jnp.float32)
            for r in range(mine):
                stat = jnp.where(
                    lane % (STAT // 2) == r, both[r * heads : (r + 1) * heads], stat
                )
            out[b, mine * heads : (mine + 1) * heads, :] = split_stat(stat, lane)
            new = keyval_rows[pl.ds(pl.multiple_of(block * (4 * mine), 4 * mine), 4 * mine), :]
            if new.shape[0] < new_rows(mine):
                empty_rows = jnp.zeros((new_rows(mine) - new.shape[0], LANES), jnp.float32)
                new = jnp.concatenate([new, empty_rows], axis=0)
            out[b, (mine + 1) * heads :, :] = new.astype(jnp.bfloat16)


def combine_kernel(mine, *refs):
    *parts, out = refs
    blocks = out.shape[0]
    heads = LANES // CHUNK
    lane = lax.broadcasted_iota(jnp.int32, (heads, LANES), 1)
    for b in range(blocks):
        stats = [join_stat(part[b, mine * heads : (mine + 1) * heads, :]) for part in parts]
        maxima = [jnp.where(lane < mine, stat, 0.0) for stat in stats]
        top = functools.reduce(jnp.maximum, maxima)
        factors = [jnp.exp(m - top) for m in maxima]
        sums = sum(
            pltpu.roll(f, STAT // 2, 1) * jnp.where(lane < STAT, stat, 0.0)
            for f, stat in zip(factors, stats)
        )
        both = jnp.where(lane < STAT // 2, top, sums)
        both = jnp.where(lane < STAT, both, 0.0)
        both = (both + pltpu.roll(both, STAT, 1)) + pltpu.roll(both, 2 * STAT, 1)
        out[b, mine * heads : (mine + 1) * heads, :] = split_stat(both, lane)
        new = sum(part[b, (mine + 1) * heads :, :].astype(jnp.float32) for part in parts)
        out[b, (mine + 1) * heads :, :] = new.astype(jnp.bfloat16)
        for r in range(mine):
            rows = slice(r * heads, (r + 1) * heads)
            numer = sum(
                f[:, r : r + 1] * part[b, rows, :].astype(jnp.float32)
                for f, part in zip(factors, parts)
            )
            out[b, rows, :] = numer.astype(jnp.bfloat16)


def finish_kernel(mine, *refs):
    *parts, query, out, numers = refs
    blocks = parts[0].shape[0]
    heads = LANES // CHUNK
    group = heads // 2
    lane = lax.broadcasted_iota(jnp.int32, (heads, LANES), 1)
    low_head = lax.broadcasted_iota(jnp.int32, (heads, LANES), 0) < group
    def spread(new, r, which):
        low = jnp.broadcast_to(new[4 * r + which : 4 * r + which + 1], (heads, LANES))
        high = jnp.broadcast_to(new[4 * r + 2 + which : 4 * r + 3 + which], (heads, LANES))
        return jnp.where(low_head, low, high)

    for b in range(blocks):
        new = sum(part[b, (mine + 1) * heads :, :].astype(jnp.float32) for part in parts)
        new = new.astype(jnp.bfloat16).astype(jnp.float32)
        own = jnp.zeros((heads, LANES), jnp.float32)
        for r in range(mine):
            request = b * mine + r
            rows = query[request * heads : (request + 1) * heads, :].astype(jnp.float32)
            dot = jnp.sum(rows * spread(new, r, 0), axis=1, keepdims=True)
            own = jnp.where(lane == r, dot * (1.0 / math.sqrt(HD)), own)
        maxima, sums = [], []
        for part in parts:
            whole = join_stat(part[b, mine * heads : (mine + 1) * heads, :])
            maxima.append(jnp.where(lane < mine, whole, 0.0))
            sums.append(jnp.where(lane < mine, pltpu.roll(whole, LANES - STAT // 2, 1), 0.0))
        top = functools.reduce(jnp.maximum, maxima, own)
        fresh = jnp.exp(own - top)
        factors = [jnp.exp(m - top) for m in maxima]
        denom = sum((s * f for s, f in zip(sums, factors)), fresh)
        fresh = fresh / denom
        factors = [f / denom for f in factors]
        for r in range(mine):
            numer = fresh[:, r : r + 1] * spread(new, r, 1)
            for part, f in zip(parts, factors):
                rows = part[b, r * heads : (r + 1) * heads, :].astype(jnp.float32)
                numer = numer + f[:, r : r + 1] * rows
            request = b * mine + r
            numers[request * heads : (request + 1) * heads, :] = numer
    for h in range(heads):
        out[:, h * HD : (h + 1) * HD] = numers[
            pl.ds(h, blocks * mine, stride=heads), :
        ].astype(jnp.bfloat16)


def body(
    hidden_in,
    w_query,
    w_keyval,
    w_out,
    key_cache,
    value_cache,
    key_scale,
    value_scale,
    page_counts,
    slot_pages,
    trim,
    seq_size,
    head_size,
):
    requests = hidden_in.shape[0]
    slots = key_cache.shape[0]
    kv_local = w_keyval.shape[1] // (2 * HD)
    heads_local = w_query.shape[1] // HD
    wide = heads_local * HD
    group = heads_local // kv_local
    assert kv_local == 2 and heads_local * CHUNK == LANES
    assert slots % CHUNK == 0
    mine = requests // seq_size
    inverse_square_root = 1.0 / math.sqrt(HD)

    assert slots == LANES and mine & (mine - 1) == 0
    ways = lower_groups(seq_size)[0][1]
    chunks = slots // CHUNK
    smem = pl.BlockSpec(memory_space=pltpu.SMEM)
    vmem = pl.BlockSpec(memory_space=pltpu.VMEM)
    hbm = pl.BlockSpec(memory_space=pl.ANY)
    small = pltpu.CompilerParams(vmem_limit_bytes=6 * 2**20)

    def in_hbm(x):
        return pltpu.with_memory_space_constraint(x, pltpu.HBM)

    tables, place_of = pl.pallas_call(
        functools.partial(table_kernel, seq_size, ways),
        out_shape=[
            jax.ShapeDtypeStruct((4 * chunks, LANES), jnp.float32),
            jax.ShapeDtypeStruct((1, slots), jnp.int32),
        ],
        in_specs=[smem, smem, vmem, vmem, vmem],
        out_specs=[vmem, vmem],
        compiler_params=small,
        name="page_table",
    )(page_counts, trim, slot_pages.reshape(1, slots), key_scale.T, value_scale.T)
    place_of = place_of.reshape(slots)

    held = last_group(seq_size)[1] * mine
    part_shape = jax.ShapeDtypeStruct((seq_size // ways, mine, wide), jnp.float32)
    keyval_shape = jax.ShapeDtypeStruct((requests, w_keyval.shape[1]), jnp.float32)
    *parts, keyval = pl.pallas_call(
        functools.partial(project_kernel, ways),
        out_shape=[part_shape] * ways + [keyval_shape],
        in_specs=[hbm, hbm, hbm],
        out_specs=[vmem] * (ways + 1),
        scratch_shapes=[
            pltpu.VMEM(hidden_in.shape, jnp.bfloat16),
            pltpu.VMEM(w_query.shape, jnp.bfloat16),
            pltpu.VMEM(w_keyval.shape, jnp.bfloat16),
            pltpu.VMEM((requests, wide), jnp.float32),
            pltpu.SemaphoreType.DMA((2, pl.cdiv(w_query.shape[0], 256))),
            pltpu.SemaphoreType.DMA,
        ],
        compiler_params=pltpu.CompilerParams(vmem_limit_bytes=53 * 2**20),
        name="project",
    )(in_hbm(hidden_in), in_hbm(w_query), in_hbm(w_keyval))
    terms, (tables, place_of) = scatter_terms(parts, "seq", seq_size, (tables, place_of))
    my_query = pl.pallas_call(
        join_kernel,
        out_shape=jax.ShapeDtypeStruct((held * heads_local, HD), jnp.bfloat16),
        in_specs=[vmem] * len(terms),
        out_specs=vmem,
        scratch_shapes=[pltpu.VMEM((held * heads_local, HD), jnp.float32)],
        compiler_params=small,
        cost_estimate=pl.CostEstimate(flops=10**10, bytes_accessed=10**7, transcendentals=0),
        name="join",
    )(*terms)
    query = gather_relative(my_query, "seq", seq_size)

    every_row = requests * heads_local
    block_rows = (mine + 1) * heads_local + new_rows(mine)
    totals = pl.pallas_call(
        functools.partial(attention_kernel, ways, mine),
        out_shape=[jax.ShapeDtypeStruct((seq_size // ways, block_rows, HD), jnp.bfloat16)] * ways,
        in_specs=[smem] + [vmem] * (ways + 4),
        out_specs=[vmem] * ways,
        scratch_shapes=[
            pltpu.VMEM((every_row, HD), jnp.bfloat16),
            pltpu.VMEM((every_row, HD), jnp.bfloat16),
            pltpu.VMEM((chunks, LANES, PAGE), jnp.bfloat16),
            pltpu.VMEM((slots * heads_local, HD), jnp.float32),
            pltpu.VMEM((chunks, LANES), jnp.float32),
            pltpu.VMEM((chunks, LANES), jnp.float32),
            pltpu.VMEM((chunks, LANES), jnp.float32),
            pltpu.VMEM((2, every_row, HD), jnp.float32),
            pltpu.VMEM((2, every_row, HD), jnp.float32),
            pltpu.VMEM((requests * 2 * kv_local, HD), jnp.float32),
        ],
        compiler_params=pltpu.CompilerParams(vmem_limit_bytes=24 * 2**20),
        cost_estimate=pl.CostEstimate(
            flops=4 * slots * PAGE * wide,
            bytes_accessed=2 * (key_cache.size + value_cache.size),
            transcendentals=slots * PAGE * heads_local,
        ),
        name="paged_attention",
    )(place_of, *query, keyval, tables, key_cache, value_cache)

    for shift, size in lower_groups(seq_size):
        if shift:
            totals = [pick_digit(totals, "seq", shift, size, d) for d in range(size)]
        parts = swap_all(totals, "seq", seq_size, shift)
        totals = pl.pallas_call(
            functools.partial(combine_kernel, mine),
            out_shape=jax.ShapeDtypeStruct(parts[0].shape, jnp.bfloat16),
            in_specs=[vmem] * size,
            out_specs=vmem,
            compiler_params=pltpu.CompilerParams(vmem_limit_bytes=6 * 2**20),
            name="combine",
        )(*parts)
    shift, size = last_group(seq_size)
    parts = [totals] + [swap(totals, "seq", seq_size, d << shift) for d in range(1, size)]
    my_context = pl.pallas_call(
        functools.partial(finish_kernel, mine),
        out_shape=jax.ShapeDtypeStruct((held, wide), jnp.bfloat16),
        in_specs=[vmem] * (size + 1),
        out_specs=vmem,
        scratch_shapes=[pltpu.VMEM((held * heads_local, HD), jnp.float32)],
        compiler_params=pltpu.CompilerParams(vmem_limit_bytes=6 * 2**20),
        name="finish",
    )(*parts, my_query)

    total = pl.pallas_call(
        functools.partial(output_kernel, ways, seq_size),
        out_shape=jax.ShapeDtypeStruct((requests, w_out.shape[1]), jnp.bfloat16),
        in_specs=[vmem] * (ways + 1),
        out_specs=vmem,
        scratch_shapes=[pltpu.VMEM((requests, w_out.shape[1]), jnp.float32)],
        compiler_params=pltpu.CompilerParams(vmem_limit_bytes=16 * 2**20),
        name="project_out",
    )(*gather_relative(my_context, "seq", seq_size), w_out)
    mask = head_size // 2
    while mask:
        if mask > 1:
            if total.dtype != jnp.bfloat16:
                total = lax.reduce_precision(total, 8, 7).astype(jnp.bfloat16)
            other = swap(total, "head", head_size, mask)
            total = total.astype(jnp.float32) + other.astype(jnp.float32)
        else:
            total = total + swap(total, "head", head_size, mask)
        mask //= 2
    return total.astype(jnp.bfloat16)


def solution(mesh):
    seq_size, head_size = mesh.shape["seq"], mesh.shape["head"]

    def local(*args):
        return body(*args, seq_size=seq_size, head_size=head_size)

    return jax.shard_map(
        local,
        mesh=mesh,
        in_specs=(
            P(None, "seq"),
            P("seq", "head"),
            P("seq", "head"),
            P("head", "seq"),
            P("seq", None, "head"),
            P("seq", None, "head"),
            P("seq", "head"),
            P("seq", "head"),
            P(),
            P("seq"),
            P(),
        ),
        out_specs=P(None, "seq"),
        check_vma=False,
    )
```

```python
import functools
import math

import jax
import jax.numpy as jnp
from jax import lax
from jax.experimental import pallas as pl
from jax.experimental.pallas import tpu as pltpu
from jax.sharding import PartitionSpec as P

HD = 128
PAGE = 128
LANES = 128
CHUNK = 8
STAT = 16


masked_low = -1e30


def swap(x, axis, n, mask):
    return lax.ppermute(x, axis, [(j, j ^ mask) for j in range(n)])


def way_order(size):
    return [0, size - 1, *range(1, size - 1)]


def swap_all(parts, axis, n, shift):
    return [
        swap(parts[d], axis, n, d << shift) if d else parts[0] for d in way_order(len(parts))
    ]


def in_order(parts):
    return [parts[i] for i in sorted(range(len(parts)), key=way_order(len(parts)).__getitem__)]


def bit_groups(n):
    groups, shift = [], 0
    while (1 << shift) < n:
        size = min(4, n >> shift)
        groups.append((shift, size))
        shift += size.bit_length() - 1
    return groups


def lower_groups(n):
    return bit_groups(n)[:-1]


def last_group(n):
    return bit_groups(n)[-1]


def pick_digit(x, axis, shift, size, offset):
    digit = (lax.axis_index(axis) >> shift) % size
    x = x.reshape(x.shape[0] // size, size, *x.shape[1:])
    return lax.dynamic_index_in_dim(x, digit ^ offset, axis=1, keepdims=False)


def scatter_terms(parts, axis, n, beside):
    for shift, size in lower_groups(n):
        if shift:
            parts = [pick_digit(x, axis, shift, size, d) for d in range(size)]
        got = swap_all(parts, axis, n, shift)
        if shift == 0:
            got, beside = lax.optimization_barrier((got, beside))
        x = sum(got[1:], got[0])
    shift, size = last_group(n)
    return [x] + [swap(x, axis, n, d << shift) for d in range(1, size)], beside


def gather_relative(x, axis, n):
    parts = [x]
    for shift, size in reversed(lower_groups(n)):
        x = jnp.concatenate(in_order(parts), axis=0) if len(parts) > 1 else parts[0]
        parts = swap_all([x] * size, axis, n, shift)
    return parts


def relative_place(block, me, n):
    last_shift, _ = last_group(n)
    offset = me ^ block
    place, weight = block >> last_shift, n
    for shift, size in lower_groups(n):
        weight //= size
        place = place + ((offset >> shift) & (size - 1)) * weight
    return place


def gathered_blocks(me, n):
    last_shift, last_size = last_group(n)
    offsets = [0]
    for shift, size in reversed(lower_groups(n)):
        offsets = [d << shift | e for d in range(size) for e in offsets]
    low = me & ((1 << last_shift) - 1)
    return [(c << last_shift) + (low ^ e) for e in offsets for c in range(last_size)]


def table_kernel(seq_size, ways, counts, trim, pages, key_scale, value_scale, tables, place_of):
    requests = counts.shape[0]
    chunks = tables.shape[0] // 4
    heads = LANES // CHUNK
    mine = requests // seq_size
    page = pages[...]
    owner, first, length = [jnp.zeros_like(page)] * 3
    start = 0
    for r in range(requests):
        end = start + counts[r]
        inside = (page >= start) & (page < end)
        owner = owner + jnp.where(page >= end, 1, 0)
        first = jnp.where(inside, start, first)
        length = jnp.where(inside, PAGE * counts[r] - trim[r], length)
        start = end
    valid = length - (page - first) * PAGE
    block = owner >> (mine.bit_length() - 1)
    me = lax.axis_index("seq")
    row = relative_place(block, me, seq_size) * mine + (owner & (mine - 1))
    place_of[...] = ((me & (ways - 1)) << 24) + (row << 16) + owner

    chunk_slot = lax.broadcasted_iota(jnp.int32, (chunks, LANES), 1) // CHUNK
    in_chunk = chunk_slot == lax.broadcasted_iota(jnp.int32, (chunks, LANES), 0)
    slot = lax.broadcasted_iota(jnp.int32, (LANES, LANES), 0) % CHUNK
    lane = lax.broadcasted_iota(jnp.int32, (LANES, LANES), 1)
    same_slot = slot == lane // heads
    low_head = lane % heads < heads // 2

    def spread(row, to):
        rest = jnp.where(in_chunk, jnp.broadcast_to(row, (chunks, LANES)), 0.0)
        total = jnp.zeros((chunks, LANES), jnp.float32)
        for _ in range(3):
            piece = rest.astype(jnp.bfloat16)
            rest = rest - piece.astype(jnp.float32)
            total = total + jnp.dot(
                piece,
                jnp.where(to, 1.0, 0.0).astype(jnp.bfloat16),
                preferred_element_type=jnp.float32,
            )
        return total

    def by_head(scale):
        return spread(scale[0:1, :], same_slot & low_head) + spread(
            scale[1:2, :], same_slot & jnp.logical_not(low_head)
        )

    tables[:chunks, :] = by_head(key_scale) * (1.0 / math.sqrt(HD))
    tables[chunks : 2 * chunks, :] = spread(valid.astype(jnp.float32), same_slot)
    tables[2 * chunks : 3 * chunks, :] = by_head(value_scale)
    tables[3 * chunks :, :] = spread(owner.astype(jnp.float32), same_slot)


def project_kernel(ways, hidden, w_query, w_keyval, *refs):
    outs, (keyval_out, rows_held, query, keyval, result, sem, rows_sem) = refs[:ways], refs[ways:]
    depth = w_query.shape[0]
    tile = min(256, depth)
    copies = [
        [
            pltpu.make_async_copy(
                ref.at[pl.ds(row, tile)], held.at[pl.ds(row, tile)], sem.at[which, row // tile]
            )
            for which, (ref, held) in enumerate(((w_query, query), (w_keyval, keyval)))
        ]
        for row in range(0, depth, tile)
    ]
    rows_copy = pltpu.make_async_copy(hidden, rows_held, rows_sem)
    rows_copy.start()
    for pair in copies:
        for copy in pair:
            copy.start()
    rows_copy.wait()
    for row, pair in zip(range(0, depth, tile), copies):
        here = slice(row, row + tile)
        rows = rows_held[:, here]
        for copy in pair:
            copy.wait()
        for held, to in ((query, result), (keyval, keyval_out)):
            part = jnp.dot(rows, held[here, :], preferred_element_type=jnp.float32)
            to[...] = to[...] + part if row else part
    digit = lax.axis_index("seq") & (ways - 1)
    for d, out in enumerate(outs):
        blocks, mine, _ = out.shape
        for b in range(blocks):
            if mine % 8 == 0:
                first = (b * ways + (digit ^ d)) * mine
                out[b] = result[pl.ds(pl.multiple_of(first, mine), mine), :]
                continue
            chosen = result[b * ways * mine : (b * ways + 1) * mine, :]
            for j in range(1, ways):
                first = (b * ways + j) * mine
                chosen = jnp.where((digit ^ d) == j, result[first : first + mine, :], chosen)
            out[b] = chosen


def output_kernel(ways, seq_size, *refs):
    parts, (w_out, rounded, out) = refs[:ways], refs[ways:]
    rows = jnp.concatenate([part[...] for part in in_order(parts)], axis=0)
    total = jnp.dot(rows, w_out[...], preferred_element_type=jnp.float32)
    blocks = gathered_blocks(lax.axis_index("seq"), seq_size)
    mine = rows.shape[0] // len(blocks)
    if mine % 8 == 0:
        for i, block in enumerate(blocks):
            here = pl.ds(pl.multiple_of(block * mine, mine), mine)
            out[here, :] = total[i * mine : (i + 1) * mine]
        rounded[...] = out[...].astype(jnp.bfloat16)
        return
    for place in range(len(blocks)):
        chosen = total[:mine]
        for i, block in enumerate(blocks):
            chosen = jnp.where(block == place, total[i * mine : (i + 1) * mine], chosen)
        out[place * mine : (place + 1) * mine, :] = chosen
    rounded[...] = out[...].astype(jnp.bfloat16)


def join_kernel(*refs):
    *parts, out, rows = refs
    blocks, mine, columns = parts[0].shape
    held = blocks * mine
    whole = functools.reduce(jnp.add, [part[...] for part in parts]).reshape(held, columns)
    heads = columns // HD
    for h in range(heads):
        rows[pl.ds(h, held, stride=heads), :] = whole[:, h * HD : (h + 1) * HD]
    out[...] = rows[...].astype(jnp.bfloat16)


def new_rows(mine):
    return -(-4 * mine // 16) * 16


def split_stat(stat, lane):
    hi = stat.astype(jnp.bfloat16).astype(jnp.float32)
    rest = stat - hi
    mid = rest.astype(jnp.bfloat16).astype(jnp.float32)
    piece = jnp.where(lane < STAT, hi, jnp.where(lane < 2 * STAT, mid, rest - mid))
    return piece.astype(jnp.bfloat16)


def join_stat(pieces):
    pieces = pieces.astype(jnp.float32)
    return (pieces + pltpu.roll(pieces, LANES - STAT, 1)) + pltpu.roll(
        pieces, LANES - 2 * STAT, 1
    )


def attention_kernel(ways, mine, place_of, *refs):
    queries, refs = refs[:ways], refs[ways:]
    (keyval, tables, keys, values), refs = refs[:4], refs[4:]
    outs, refs = refs[:ways], refs[ways:]
    (
        query_low,
        query_high,
        probs,
        page_out,
        page_sum,
        page_max,
        dev_max,
        total_out,
        total_stat,
        keyval_rows,
    ) = refs
    slots = keys.shape[0]
    heads = LANES // CHUNK
    group = heads // 2
    chunks = slots // CHUNK
    blocks = outs[0].shape[0]
    lag = 8

    for d, part in enumerate(in_order(queries)):
        rows = part[...]
        low_head = lax.broadcasted_iota(jnp.int32, rows.shape, 0) % heads < group
        zero = jnp.zeros_like(rows)
        here = slice(rows.shape[0] * d, rows.shape[0] * (d + 1))
        query_low[here, :] = jnp.where(low_head, rows, zero)
        query_high[here, :] = jnp.where(low_head, zero, rows)
    total_out[...] = jnp.zeros_like(total_out)
    stat_lane = lax.broadcasted_iota(jnp.int32, total_stat.shape, 2) % STAT
    total_stat[...] = jnp.where(stat_lane < STAT // 2, masked_low, 0.0)

    def table(which, c):
        return tables[pl.ds(which * chunks + c, 1), :]

    lane_slot = lax.broadcasted_iota(jnp.int32, (PAGE, LANES), 1) // heads
    token = lax.broadcasted_iota(jnp.int32, (PAGE, LANES), 0).astype(jnp.float32)

    def score_chunk(c):
        places = [
            pl.multiple_of(((place_of[c * CHUNK + s] >> 16) & 0xFF) * heads, heads)
            for s in range(CHUNK)
        ]
        chosen = jnp.concatenate(
            [
                jnp.concatenate([ref[pl.ds(place, heads), :] for place in places], axis=0)
                for ref in (query_low, query_high)
            ],
            axis=1,
        )
        block = keys[pl.ds(c * CHUNK, CHUNK)].reshape(CHUNK * PAGE, 2 * HD)
        every = lax.dot_general(
            block, chosen, (((1,), (1,)), ((), ())), preferred_element_type=jnp.float32
        )
        score = every[:PAGE]
        for s in range(1, CHUNK):
            score = jnp.where(lane_slot == s, every[s * PAGE : (s + 1) * PAGE], score)
        return jnp.where(token < table(1, c), score * table(0, c), masked_low)

    def prob_chunk(c, score):
        top = jnp.max(score, axis=0, keepdims=True)
        page_max[pl.ds(c, 1), :] = top
        prob = jnp.exp(score - top).astype(jnp.bfloat16).astype(jnp.float32)
        page_sum[pl.ds(c, 1), :] = jnp.sum(prob, axis=0, keepdims=True)
        probs[c] = prob.T.astype(jnp.bfloat16)

    empty = jnp.zeros((heads, PAGE), jnp.bfloat16)

    def value_chunk(c):
        prob = probs[c]
        for s in range(0, CHUNK, 2):
            pair = jnp.concatenate(
                [
                    jnp.concatenate([prob[s * heads : (s + 1) * heads], empty], axis=1),
                    jnp.concatenate([empty, prob[(s + 1) * heads : (s + 2) * heads]], axis=1),
                ],
                axis=0,
            )
            block = values[pl.ds(c * CHUNK + s, 2)].reshape(2 * PAGE, 2 * HD)
            both = jnp.dot(pair, block, preferred_element_type=jnp.float32)
            page_out[pl.ds(pl.multiple_of((c * CHUNK + s) * heads, heads), 2 * heads), :] = (
                jnp.concatenate(
                    [
                        both[:group, :HD],
                        both[group:heads, HD:],
                        both[heads : heads + group, :HD],
                        both[heads + group :, HD:],
                    ],
                    axis=0,
                )
            )

    held = {}
    for c in range(chunks + lag):
        if c >= lag:
            value_chunk(c - lag)
        if c < chunks:
            held[c] = score_chunk(c)
        if 2 <= c < chunks + 2:
            prob_chunk(c - 2, held.pop(c - 2))

    biggest, who = page_max[...], tables[3 * chunks :, :]
    best = biggest
    for turn in range(CHUNK):
        other = pltpu.roll(biggest, turn * heads, 1) if turn else biggest
        other_who = pltpu.roll(who, turn * heads, 1) if turn else who
        for c in range(chunks):
            best = jnp.maximum(
                best, jnp.where(other_who[c : c + 1] == who, other[c : c + 1], masked_low)
            )
    dev_max[...] = best

    keep_max = lax.broadcasted_iota(jnp.int32, (heads, LANES), 1) % STAT < STAT // 2

    keep_max_row = lax.broadcasted_iota(jnp.int32, (PAGE, LANES), 0) % STAT < STAT // 2

    def weigh_chunk(c):
        top = dev_max[pl.ds(c, 1), :]
        weight = jnp.exp(page_max[pl.ds(c, 1), :] - top)
        out_weight = jnp.broadcast_to(weight * table(2, c), (PAGE, LANES)).T
        stat = jnp.where(keep_max_row, top, weight * page_sum[pl.ds(c, 1), :]).T
        return out_weight, stat

    def total_chunk(c, out_weight, stat):
        for s in range(CHUNK):
            here = pl.ds(
                pl.multiple_of((place_of[c * CHUNK + s] & 0xFFFF) * heads, heads), heads
            )
            there = pl.ds(pl.multiple_of((c * CHUNK + s) * heads, heads), heads)
            part = slice(s * heads, (s + 1) * heads)
            turn = s % 2
            total_out[turn, here, :] += page_out[there, :] * out_weight[part]
            total_stat[turn, here, :] = jnp.where(
                keep_max, stat[part], total_stat[turn, here, :] + stat[part]
            )

    for c in range(chunks + 1):
        if c < chunks:
            held[c] = weigh_chunk(c)
        if c >= 1:
            total_chunk(c - 1, *held.pop(c - 1))

    lane = lax.broadcasted_iota(jnp.int32, (heads, LANES), 1)
    digit = place_of[0] >> 24
    for j in range(4):
        keyval_rows[pl.ds(j, keyval.shape[0], stride=4), :] = keyval[:, j * HD : (j + 1) * HD]
    for d, out in enumerate(outs):
        for b in range(blocks):
            block = b * ways + (digit ^ d)
            rows = pl.ds(pl.multiple_of(block * (mine * heads), mine * heads), mine * heads)
            out[b, : mine * heads, :] = (total_out[0, rows, :] + total_out[1, rows, :]).astype(
                jnp.bfloat16
            )
            even, odd = total_stat[0, rows, :], total_stat[1, rows, :]
            is_max = lax.broadcasted_iota(jnp.int32, even.shape, 1) % STAT < STAT // 2
            both = jnp.where(is_max, jnp.maximum(even, odd), even + odd)
            stat = jnp.zeros((heads, LANES), jnp.float32)
            for r in range(mine):
                stat = jnp.where(
                    lane % (STAT // 2) == r, both[r * heads : (r + 1) * heads], stat
                )
            out[b, mine * heads : (mine + 1) * heads, :] = split_stat(stat, lane)
            new = keyval_rows[pl.ds(pl.multiple_of(block * (4 * mine), 4 * mine), 4 * mine), :]
            if new.shape[0] < new_rows(mine):
                empty_rows = jnp.zeros((new_rows(mine) - new.shape[0], LANES), jnp.float32)
                new = jnp.concatenate([new, empty_rows], axis=0)
            out[b, (mine + 1) * heads :, :] = new.astype(jnp.bfloat16)


def combine_kernel(mine, *refs):
    *parts, out = refs
    blocks = out.shape[0]
    heads = LANES // CHUNK
    lane = lax.broadcasted_iota(jnp.int32, (heads, LANES), 1)
    for b in range(blocks):
        stats = [join_stat(part[b, mine * heads : (mine + 1) * heads, :]) for part in parts]
        maxima = [jnp.where(lane < mine, stat, 0.0) for stat in stats]
        top = functools.reduce(jnp.maximum, maxima)
        factors = [jnp.exp(m - top) for m in maxima]
        sums = sum(
            pltpu.roll(f, STAT // 2, 1) * jnp.where(lane < STAT, stat, 0.0)
            for f, stat in zip(factors, stats)
        )
        both = jnp.where(lane < STAT // 2, top, sums)
        both = jnp.where(lane < STAT, both, 0.0)
        both = (both + pltpu.roll(both, STAT, 1)) + pltpu.roll(both, 2 * STAT, 1)
        out[b, mine * heads : (mine + 1) * heads, :] = split_stat(both, lane)
        new = sum(part[b, (mine + 1) * heads :, :].astype(jnp.float32) for part in parts)
        out[b, (mine + 1) * heads :, :] = new.astype(jnp.bfloat16)
        for r in range(mine):
            rows = slice(r * heads, (r + 1) * heads)
            numer = sum(
                f[:, r : r + 1] * part[b, rows, :].astype(jnp.float32)
                for f, part in zip(factors, parts)
            )
            out[b, rows, :] = numer.astype(jnp.bfloat16)


def finish_kernel(mine, *refs):
    *parts, query, out, numers = refs
    blocks = parts[0].shape[0]
    heads = LANES // CHUNK
    group = heads // 2
    lane = lax.broadcasted_iota(jnp.int32, (heads, LANES), 1)
    low_head = lax.broadcasted_iota(jnp.int32, (heads, LANES), 0) < group
    def spread(new, r, which):
        low = jnp.broadcast_to(new[4 * r + which : 4 * r + which + 1], (heads, LANES))
        high = jnp.broadcast_to(new[4 * r + 2 + which : 4 * r + 3 + which], (heads, LANES))
        return jnp.where(low_head, low, high)

    for b in range(blocks):
        new = sum(part[b, (mine + 1) * heads :, :].astype(jnp.float32) for part in parts)
        new = new.astype(jnp.bfloat16).astype(jnp.float32)
        own = jnp.zeros((heads, LANES), jnp.float32)
        for r in range(mine):
            request = b * mine + r
            rows = query[request * heads : (request + 1) * heads, :].astype(jnp.float32)
            dot = jnp.sum(rows * spread(new, r, 0), axis=1, keepdims=True)
            own = jnp.where(lane == r, dot * (1.0 / math.sqrt(HD)), own)
        maxima, sums = [], []
        for part in parts:
            whole = join_stat(part[b, mine * heads : (mine + 1) * heads, :])
            maxima.append(jnp.where(lane < mine, whole, 0.0))
            sums.append(jnp.where(lane < mine, pltpu.roll(whole, LANES - STAT // 2, 1), 0.0))
        top = functools.reduce(jnp.maximum, maxima, own)
        fresh = jnp.exp(own - top)
        factors = [jnp.exp(m - top) for m in maxima]
        denom = sum((s * f for s, f in zip(sums, factors)), fresh)
        fresh = fresh / denom
        factors = [f / denom for f in factors]
        for r in range(mine):
            numer = fresh[:, r : r + 1] * spread(new, r, 1)
            for part, f in zip(parts, factors):
                rows = part[b, r * heads : (r + 1) * heads, :].astype(jnp.float32)
                numer = numer + f[:, r : r + 1] * rows
            request = b * mine + r
            numers[request * heads : (request + 1) * heads, :] = numer
    for h in range(heads):
        out[:, h * HD : (h + 1) * HD] = numers[
            pl.ds(h, blocks * mine, stride=heads), :
        ].astype(jnp.bfloat16)


def body(
    hidden_in,
    w_query,
    w_keyval,
    w_out,
    key_cache,
    value_cache,
    key_scale,
    value_scale,
    page_counts,
    slot_pages,
    trim,
    seq_size,
    head_size,
):
    requests = hidden_in.shape[0]
    slots = key_cache.shape[0]
    kv_local = w_keyval.shape[1] // (2 * HD)
    heads_local = w_query.shape[1] // HD
    wide = heads_local * HD
    group = heads_local // kv_local
    assert kv_local == 2 and heads_local * CHUNK == LANES
    assert slots % CHUNK == 0
    mine = requests // seq_size
    inverse_square_root = 1.0 / math.sqrt(HD)

    assert slots == LANES and mine & (mine - 1) == 0
    ways = lower_groups(seq_size)[0][1]
    chunks = slots // CHUNK
    smem = pl.BlockSpec(memory_space=pltpu.SMEM)
    vmem = pl.BlockSpec(memory_space=pltpu.VMEM)
    hbm = pl.BlockSpec(memory_space=pl.ANY)
    small = pltpu.CompilerParams(vmem_limit_bytes=6 * 2**20)

    def in_hbm(x):
        return pltpu.with_memory_space_constraint(x, pltpu.HBM)

    tables, place_of = pl.pallas_call(
        functools.partial(table_kernel, seq_size, ways),
        out_shape=[
            jax.ShapeDtypeStruct((4 * chunks, LANES), jnp.float32),
            jax.ShapeDtypeStruct((1, slots), jnp.int32),
        ],
        in_specs=[smem, smem, vmem, vmem, vmem],
        out_specs=[vmem, vmem],
        compiler_params=small,
        name="page_table",
    )(page_counts, trim, slot_pages.reshape(1, slots), key_scale.T, value_scale.T)
    place_of = place_of.reshape(slots)

    held = last_group(seq_size)[1] * mine
    part_shape = jax.ShapeDtypeStruct((seq_size // ways, mine, wide), jnp.float32)
    keyval_shape = jax.ShapeDtypeStruct((requests, w_keyval.shape[1]), jnp.float32)
    *parts, keyval = pl.pallas_call(
        functools.partial(project_kernel, ways),
        out_shape=[part_shape] * ways + [keyval_shape],
        in_specs=[hbm, hbm, hbm],
        out_specs=[vmem] * (ways + 1),
        scratch_shapes=[
            pltpu.VMEM(hidden_in.shape, jnp.bfloat16),
            pltpu.VMEM(w_query.shape, jnp.bfloat16),
            pltpu.VMEM(w_keyval.shape, jnp.bfloat16),
            pltpu.VMEM((requests, wide), jnp.float32),
            pltpu.SemaphoreType.DMA((2, pl.cdiv(w_query.shape[0], 256))),
            pltpu.SemaphoreType.DMA,
        ],
        compiler_params=pltpu.CompilerParams(vmem_limit_bytes=53 * 2**20),
        name="project",
    )(in_hbm(hidden_in), in_hbm(w_query), in_hbm(w_keyval))
    terms, (tables, place_of) = scatter_terms(parts, "seq", seq_size, (tables, place_of))
    my_query = pl.pallas_call(
        join_kernel,
        out_shape=jax.ShapeDtypeStruct((held * heads_local, HD), jnp.bfloat16),
        in_specs=[vmem] * len(terms),
        out_specs=vmem,
        scratch_shapes=[pltpu.VMEM((held * heads_local, HD), jnp.float32)],
        compiler_params=small,
        cost_estimate=pl.CostEstimate(flops=10**10, bytes_accessed=10**7, transcendentals=0),
        name="join",
    )(*terms)
    query = gather_relative(my_query, "seq", seq_size)

    every_row = requests * heads_local
    block_rows = (mine + 1) * heads_local + new_rows(mine)
    totals = pl.pallas_call(
        functools.partial(attention_kernel, ways, mine),
        out_shape=[jax.ShapeDtypeStruct((seq_size // ways, block_rows, HD), jnp.bfloat16)] * ways,
        in_specs=[smem] + [vmem] * (ways + 4),
        out_specs=[vmem] * ways,
        scratch_shapes=[
            pltpu.VMEM((every_row, HD), jnp.bfloat16),
            pltpu.VMEM((every_row, HD), jnp.bfloat16),
            pltpu.VMEM((chunks, LANES, PAGE), jnp.bfloat16),
            pltpu.VMEM((slots * heads_local, HD), jnp.float32),
            pltpu.VMEM((chunks, LANES), jnp.float32),
            pltpu.VMEM((chunks, LANES), jnp.float32),
            pltpu.VMEM((chunks, LANES), jnp.float32),
            pltpu.VMEM((2, every_row, HD), jnp.float32),
            pltpu.VMEM((2, every_row, HD), jnp.float32),
            pltpu.VMEM((requests * 2 * kv_local, HD), jnp.float32),
        ],
        compiler_params=pltpu.CompilerParams(vmem_limit_bytes=24 * 2**20),
        cost_estimate=pl.CostEstimate(
            flops=4 * slots * PAGE * wide,
            bytes_accessed=2 * (key_cache.size + value_cache.size),
            transcendentals=slots * PAGE * heads_local,
        ),
        name="paged_attention",
    )(place_of, *query, keyval, tables, key_cache, value_cache)

    for shift, size in lower_groups(seq_size):
        if shift:
            totals = [pick_digit(totals, "seq", shift, size, d) for d in range(size)]
        parts = swap_all(totals, "seq", seq_size, shift)
        totals = pl.pallas_call(
            functools.partial(combine_kernel, mine),
            out_shape=jax.ShapeDtypeStruct(parts[0].shape, jnp.bfloat16),
            in_specs=[vmem] * size,
            out_specs=vmem,
            compiler_params=pltpu.CompilerParams(vmem_limit_bytes=6 * 2**20),
            name="combine",
        )(*parts)
    shift, size = last_group(seq_size)
    parts = [totals] + [swap(totals, "seq", seq_size, d << shift) for d in range(1, size)]
    my_context = pl.pallas_call(
        functools.partial(finish_kernel, mine),
        out_shape=jax.ShapeDtypeStruct((held, wide), jnp.bfloat16),
        in_specs=[vmem] * (size + 1),
        out_specs=vmem,
        scratch_shapes=[pltpu.VMEM((held * heads_local, HD), jnp.float32)],
        compiler_params=pltpu.CompilerParams(vmem_limit_bytes=6 * 2**20),
        name="finish",
    )(*parts, my_query)

    total = pl.pallas_call(
        functools.partial(output_kernel, ways, seq_size),
        out_shape=jax.ShapeDtypeStruct((requests, w_out.shape[1]), jnp.bfloat16),
        in_specs=[vmem] * (ways + 1),
        out_specs=vmem,
        scratch_shapes=[pltpu.VMEM((requests, w_out.shape[1]), jnp.float32)],
        compiler_params=pltpu.CompilerParams(vmem_limit_bytes=16 * 2**20),
        name="project_out",
    )(*gather_relative(my_context, "seq", seq_size), w_out)
    mask = head_size // 2
    while mask:
        if mask > 1:
            if total.dtype != jnp.bfloat16:
                total = lax.reduce_precision(total, 8, 7).astype(jnp.bfloat16)
            other = swap(total, "head", head_size, mask)
            total = total.astype(jnp.float32) + other.astype(jnp.float32)
        else:
            total = total + swap(total, "head", head_size, mask)
        mask //= 2
    return total.astype(jnp.bfloat16)


def solution(mesh):
    seq_size, head_size = mesh.shape["seq"], mesh.shape["head"]

    def local(*args):
        return body(*args, seq_size=seq_size, head_size=head_size)

    return jax.shard_map(
        local,
        mesh=mesh,
        in_specs=(
            P(None, "seq"),
            P("seq", "head"),
            P("seq", "head"),
            P("head", "seq"),
            P("seq", None, "head"),
            P("seq", None, "head"),
            P("seq", "head"),
            P("seq", "head"),
            P(),
            P("seq"),
            P(),
        ),
        out_specs=P(None, "seq"),
        check_vma=False,
    )
```
